32 devices in a mesh: dp: 8 (over y, x, core), cache: 4 (over z).
Axes of the slice: x: 2, y: 2, z: 4, core: 2. Of those that a mesh axis runs over, the one named last changes fastest.
Arguments:
- queries: bfloat16 [2048, 64, 128], P('dp'), may hold values from -20 to 20
- out_grad: bfloat16 [2048, 64, 128], P('dp'), may hold values from -288 to 288
- self_lse: float32 [2048, 64], P('dp'), may hold values from 5 to 11
- self_dot: float32 [2048, 64], P('dp'), may hold values from -600 to 600
- cache: float32 [512, 2, 8, 128], P(('dp', 'cache')), may hold values from -20 to 20
- first_moment: float32 [512, 2, 8, 128], P(('dp', 'cache')), may hold values from -3 to 3
- second_moment: float32 [512, 2, 8, 128], P(('dp', 'cache')), may hold values from 0.3 to 6
Outputs:
- new_cache: float32 [512, 2, 8, 128], P(('dp', 'cache'))
- new_first: float32 [512, 2, 8, 128], P(('dp', 'cache'))
- new_second: float32 [512, 2, 8, 128], P(('dp', 'cache'))
The draws below stay inside these ranges and needn't reach their ends.
All inputs are finite; a program needn't handle non-finite values.
Results may differ from the reference program's by a relative error of at most 0.0086.
Values may be sent and summed in bfloat16 or wider, within the bound.
No kernel may reach another device: no remote copies, remote signals or barrier semaphores. Data moves between devices by JAX's collectives and lax.ppermute only.
A program may use at most 128 MiB of HBM per device.

```python
import math
import jax
import jax.numpy as jnp
from jax import lax

H = 64
G = 8
HD = 128
QBLOCK = 128
CS = 128
STEP = 200
TOKENS = 2048
CDEV = 16
CTOT = 512


def draw_queries(key, part):
    key = jax.random.fold_in(key, 11)
    first_key, second_key = jax.random.split(key, 2)
    noise_draw = jax.random.truncated_normal(first_key, -3.5, 3.5, (TOKENS, H, HD), jnp.float32)
    row_scale = jnp.exp(jax.random.uniform(second_key, (TOKENS, 1, 1), jnp.float32, math.log(0.3), math.log(1.2)))
    result = noise_draw * row_scale
    return result.astype(jnp.bfloat16)


def draw_cache(key, part):
    key = jax.random.fold_in(key, 23)
    first_key, second_key, third_key, fourth_key = jax.random.split(key, 4)
    noise_draw = jax.random.truncated_normal(first_key, -3.5, 3.5, (CTOT, 2, G, HD), jnp.float32)
    row_scale = jnp.exp(jax.random.uniform(second_key, (CTOT, 1, 1, 1), jnp.float32, math.log(0.3), math.log(3.0)))
    owner_index = jnp.arange(CTOT) // CDEV % (CTOT // CS)
    owner_share = owner_index.astype(jnp.float32) / max(CTOT // CS - 1, 1)
    ramp_scale = 0.8 + 0.5 * owner_share
    side_index = jnp.arange(2).reshape(1, 2, 1, 1)
    key_scale = row_scale * ramp_scale[:, None, None, None]
    result = noise_draw * jnp.where(side_index == 0, key_scale, 1.0)
    mean_sign = jnp.where(jax.random.bernoulli(third_key, 0.5, (G, HD)), 1.0, -1.0)
    mean_size = jax.random.uniform(fourth_key, (G, HD), jnp.float32, 0.5, 1.0)
    mean_ramp = 0.4 + 0.8 * owner_share
    value_mean = mean_ramp[:, None, None] * (mean_sign * mean_size)[None, :, :]
    result = result + jnp.where(side_index == 0, 0.0, value_mean[:, None, :, :])
    return result


def steps_of(stream_key, shape, pieces, low, high):
    def one(dim, blocks):
        steps = jax.random.uniform(jax.random.fold_in(jax.random.fold_in(stream_key, 6), dim), (blocks,), jnp.float32, low / len(pieces), high / len(pieces))
        return jnp.repeat(jnp.exp(steps), shape[dim] // blocks).reshape((-1,) + (1,) * (len(shape) - dim - 1))

    level = one(*pieces[0])
    for cut in pieces[1:]:
        level = level * one(*cut)
    return level


def bell_draw(key, shape, width, most, cuts=(), kind=jnp.bfloat16):
    entries = jax.random.normal(key, shape, jnp.float32) * width
    if len(cuts) > 0:
        entries = steps_of(key, shape, cuts, -0.22, 0.18) * entries
    return jnp.clip(entries, min=-most, max=most).astype(kind)


def setup_inputs(seed: int = 0) -> dict:
    key_of = jax.random.split(jax.random.key(seed), 8)
    queries = draw_queries(jax.random.fold_in(key_of[7], 71), 0)
    out_grad = bell_draw(key_of[1], (TOKENS, H, HD), 48.0, 288.0, ((0, 8),))
    self_lse = jnp.clip(5.0 + 6.0 * jax.random.uniform(key_of[2], (TOKENS, H), jnp.float32) ** steps_of(key_of[2], (TOKENS, H), ((0, 8),), -0.2, 0.2), 5.0, 11.0)
    self_dot = bell_draw(key_of[3], (TOKENS, H), 100.0, 600.0, ((0, 8),), jnp.float32)
    cache = draw_cache(jax.random.fold_in(key_of[7], 71), 0)
    first_moment = bell_draw(key_of[5], (CTOT, 2, G, HD), 0.5, 3.0, ((0, 32),), jnp.float32)
    second_moment = jnp.clip(jnp.exp(math.log(6.0) - 2.9957322 * jax.random.uniform(key_of[6], (CTOT, 2, G, HD), jnp.float32) ** steps_of(key_of[6], (CTOT, 2, G, HD), ((0, 32),), -0.2, 0.2)), 0.3, 6.0)
    return {"queries": queries, "out_grad": out_grad, "self_lse": self_lse, "self_dot": self_dot, "cache": cache, "first_moment": first_moment, "second_moment": second_moment}


learn_rate = 0.02
beta_first = 0.9
beta_second = 0.999
epsilon = 1e-08

def reference(queries, out_grad, self_lse, self_dot, cache, first_moment, second_moment):
    group_size = H // G
    score_scale = 1.0 / math.sqrt(HD)
    rounded = lax.optimization_barrier(cache.astype(jnp.bfloat16)).astype(jnp.float32)
    key_rows = rounded[:, 0]
    value_rows = rounded[:, 1]
    blocks = TOKENS // QBLOCK

    def visit_block(running, block_index):
        key_total, value_total = running
        row_start = (block_index * QBLOCK).astype(jnp.int32)
        queries_block = lax.dynamic_slice_in_dim(queries, row_start, QBLOCK, 0).astype(jnp.float32).reshape(QBLOCK, G, group_size, HD)
        grads_block = lax.dynamic_slice_in_dim(out_grad, row_start, QBLOCK, 0).astype(jnp.float32).reshape(QBLOCK, G, group_size, HD)
        side_lse = lax.dynamic_slice_in_dim(self_lse, row_start, QBLOCK, 0).reshape(QBLOCK, G, group_size)
        side_dot = lax.dynamic_slice_in_dim(self_dot, row_start, QBLOCK, 0).reshape(QBLOCK, G, group_size)
        scores = jnp.einsum('tgre,jge->tgrj', queries_block, key_rows) * score_scale
        slopes = jnp.einsum('tgre,jge->tgrj', grads_block, value_rows)
        row_peak = jnp.maximum(lax.optimization_barrier(jnp.max(scores, axis=-1)), side_lse)
        row_total = lax.optimization_barrier(jnp.sum(jnp.exp(scores - row_peak[..., None]), axis=-1)) + jnp.exp(side_lse - row_peak)
        log_total = row_peak + jnp.log(row_total)
        probability = jnp.exp(scores - log_total[..., None])
        row_delta = lax.optimization_barrier(jnp.sum(probability * slopes, axis=-1)) + jnp.exp(side_lse - log_total) * side_dot
        weights = lax.optimization_barrier(probability.astype(jnp.bfloat16)).astype(jnp.float32)
        dscore = lax.optimization_barrier((score_scale * probability * (slopes - row_delta[..., None])).astype(jnp.bfloat16)).astype(jnp.float32)
        key_total = key_total + jnp.einsum('tgrj,tgre->jge', dscore, queries_block)
        value_total = value_total + jnp.einsum('tgrj,tgre->jge', weights, grads_block)
        return ((key_total, value_total), block_index)
    zero_grad = jnp.zeros((CTOT, G, HD), jnp.float32)
    totals, unused = lax.scan(visit_block, (zero_grad, zero_grad), jnp.arange(blocks, dtype=jnp.int32))
    gradient = jnp.stack([totals[0], totals[1]], axis=1)
    new_first = beta_first * first_moment + (1.0 - beta_first) * gradient
    new_second = beta_second * second_moment + (1.0 - beta_second) * gradient * gradient
    first_hat = new_first / (1.0 - beta_first ** STEP)
    second_hat = new_second / (1.0 - beta_second ** STEP)
    new_cache = cache - learn_rate * first_hat / (jnp.sqrt(second_hat) + epsilon)
    return (new_cache, new_first, new_second)
```

```python
import functools
import math

import jax
import jax.numpy as jnp
from jax import lax
from jax.experimental import pallas as pl
from jax.experimental.pallas import tpu as pltpu
from jax.sharding import PartitionSpec as P

STEP = 200

learn_rate = 0.02
beta_first = 0.9
beta_second = 0.999
epsilon = 1e-08

ROW_TILE = 256


def attend_kernel(
    score_scale,
    row_tile,
    place_ref,
    kv_ref,
    queries_ref,
    grads_ref,
    lse_ref,
    dot_ref,
    out_ref,
    key_total,
    value_total,
):
    block = pl.program_id(1)

    @pl.when(block == 0)
    def _():
        key_total[...] = jnp.zeros_like(key_total)
        value_total[...] = jnp.zeros_like(value_total)

    senders, _, _, share, width = kv_ref.shape
    keys = kv_ref[:, 0, 0].reshape(senders * share, width)
    values = kv_ref[:, 1, 0].reshape(senders * share, width)
    tokens, _, heads, _ = queries_ref.shape
    tile_tokens = row_tile // heads
    across = (((1,), (1,)), ((), ()))
    along = (((1,), (0,)), ((), ()))
    for tile in range(tokens // tile_tokens):
        rows = pl.ds(tile * tile_tokens, tile_tokens)
        lanes = pl.ds(tile * row_tile, row_tile)
        queries = queries_ref[rows, 0].reshape(row_tile, width)
        grads = grads_ref[rows, 0].reshape(row_tile, width)
        side_lse = lse_ref[0, :, lanes]
        side_dot = dot_ref[0, :, lanes]
        scores = (
            lax.dot_general(keys, queries, across, preferred_element_type=jnp.float32)
            * score_scale
        )
        slopes = lax.dot_general(values, grads, across, preferred_element_type=jnp.float32)
        peak = jnp.maximum(jnp.max(scores, axis=0, keepdims=True), side_lse)
        shifted = jnp.exp(scores - peak)
        side = jnp.exp(side_lse - peak)
        inverse = 1.0 / (jnp.sum(shifted, axis=0, keepdims=True) + side)
        delta = (
            jnp.sum(shifted * slopes, axis=0, keepdims=True) + side * side_dot
        ) * inverse
        probability = shifted * inverse
        weights = probability.astype(jnp.bfloat16)
        dscore = (probability * ((slopes - delta) * score_scale)).astype(jnp.bfloat16)
        key_total[...] += lax.dot_general(
            dscore, queries, along, preferred_element_type=jnp.float32
        )
        value_total[...] += lax.dot_general(
            weights, grads, along, preferred_element_type=jnp.float32
        )

    @pl.when(block == pl.num_programs(1) - 1)
    def _():
        shape = (senders, share, width)
        out_ref[:, 0, 0] = key_total[...].astype(out_ref.dtype).reshape(shape)
        out_ref[:, 1, 0] = value_total[...].astype(out_ref.dtype).reshape(shape)


def attend(place, pairs, queries, out_grad, lse_rows, dot_rows, tokens, score_scale):
    senders, _, own, share, width = pairs.shape
    heads = queries.shape[2]
    rows = tokens * heads
    positions = senders * share
    block_tokens = min(tokens, 64)
    blocks = tokens // block_tokens
    pair_spec = pl.BlockSpec(
        (senders, 2, 1, share, width), lambda g, b, place: (0, 0, g, 0, 0)
    )
    token_spec = pl.BlockSpec(
        (block_tokens, 1, heads, width),
        lambda g, b, place: (place[1] * blocks + b, place[0] + g, 0, 0),
    )
    row_spec = pl.BlockSpec((1, 1, block_tokens * heads), lambda g, b, place: (g, 0, b))
    return pl.pallas_call(
        functools.partial(attend_kernel, score_scale, ROW_TILE),
        out_shape=jax.ShapeDtypeStruct(pairs.shape, jnp.bfloat16),
        grid_spec=pltpu.PrefetchScalarGridSpec(
            num_scalar_prefetch=1,
            grid=(own, blocks),
            in_specs=[pair_spec, token_spec, token_spec, row_spec, row_spec],
            out_specs=pair_spec,
            scratch_shapes=[
                pltpu.VMEM((positions, width), jnp.float32),
                pltpu.VMEM((positions, width), jnp.float32),
            ],
        ),
        compiler_params=pltpu.CompilerParams(vmem_limit_bytes=48 * 1024 * 1024),
        cost_estimate=pl.CostEstimate(
            flops=8 * own * rows * positions * width,
            bytes_accessed=4 * own * rows * width + 8 * own * positions * width,
            transcendentals=own * rows * positions,
        ),
    )(place, pairs, queries, out_grad, lse_rows, dot_rows)


def adam_kernel(parts_ref, cache_ref, first_ref, second_ref, new_cache, new_first, new_second):
    _, owners, _, own, _, _ = parts_ref.shape
    groups = cache_ref.shape[2]
    repeat = owners * own // groups
    for side in range(2):
        for group in range(groups):
            owner, slot = (group // own, group % own)
            gradient = jnp.sum(
                parts_ref[:, owner * repeat : (owner + 1) * repeat, side, slot].astype(
                    jnp.float32
                ),
                axis=(0, 1),
            )
            first = beta_first * first_ref[:, side, group] + (1.0 - beta_first) * gradient
            second = (
                beta_second * second_ref[:, side, group]
                + (1.0 - beta_second) * gradient * gradient
            )
            first_hat = first / (1.0 - beta_first**STEP)
            second_hat = second / (1.0 - beta_second**STEP)
            new_cache[:, side, group] = cache_ref[
                :, side, group
            ] - learn_rate * first_hat / (jnp.sqrt(second_hat) + epsilon)
            new_first[:, side, group] = first
            new_second[:, side, group] = second


def adam(parts, cache, first_moment, second_moment):
    shape = jax.ShapeDtypeStruct(cache.shape, jnp.float32)
    return pl.pallas_call(
        adam_kernel,
        out_shape=(shape, shape, shape),
        compiler_params=pltpu.CompilerParams(vmem_limit_bytes=32 * 1024 * 1024),
    )(parts, cache, first_moment, second_moment)


def per_device(
    dp_size, cache_size, queries, out_grad, self_lse, self_dot, cache, first_moment, second_moment
):
    share, _, groups, width = cache.shape
    tokens, heads, _ = queries.shape
    group_size = heads // groups
    score_scale = 1.0 / math.sqrt(width)
    own = max(1, groups // cache_size)
    repeat = own * cache_size // groups
    own_tokens = tokens // repeat
    column = lax.axis_index("cache")
    first_group = column // repeat * own
    token_part = column % repeat

    rounded = cache.astype(jnp.bfloat16).reshape(share, 2, groups // own, own, width)
    slices = jnp.repeat(rounded.transpose(2, 1, 3, 0, 4), repeat, axis=0)
    outgoing = jnp.broadcast_to(slices, (dp_size,) + slices.shape).reshape(
        (dp_size * cache_size,) + slices.shape[1:]
    )
    pairs = lax.all_to_all(outgoing, ("dp", "cache"), 0, 0, tiled=True)

    def rows_of(stat):
        part = lax.dynamic_slice(
            stat,
            (token_part * own_tokens, first_group * group_size),
            (own_tokens, own * group_size),
        )
        return (
            part.reshape(own_tokens, own, group_size)
            .transpose(1, 0, 2)
            .reshape(own, 1, own_tokens * group_size)
        )

    place = jnp.stack([first_group, token_part]).astype(jnp.int32)
    partial = attend(
        place,
        pairs,
        queries.reshape(tokens, groups, group_size, width),
        out_grad.reshape(tokens, groups, group_size, width),
        rows_of(self_lse),
        rows_of(self_dot),
        own_tokens,
        score_scale,
    )
    arrived = lax.all_to_all(partial, ("dp", "cache"), 0, 0, tiled=True)
    arrived = arrived.reshape((dp_size, cache_size) + arrived.shape[1:])
    return adam(arrived, cache, first_moment, second_moment)


def solution(mesh):
    in_specs = (
        P("dp", None, None),
        P("dp", None, None),
        P("dp", None),
        P("dp", None),
        P(("dp", "cache"), None, None, None),
        P(("dp", "cache"), None, None, None),
        P(("dp", "cache"), None, None, None),
    )
    out_specs = (
        P(("dp", "cache"), None, None, None),
        P(("dp", "cache"), None, None, None),
        P(("dp", "cache"), None, None, None),
    )
    return jax.shard_map(
        functools.partial(per_device, mesh.shape["dp"], mesh.shape["cache"]),
        mesh=mesh,
        in_specs=in_specs,
        out_specs=out_specs,
        check_vma=False,
    )
```

```python
import functools
import math

import jax
import jax.numpy as jnp
from jax import lax
from jax.experimental import pallas as pl
from jax.experimental.pallas import tpu as pltpu
from jax.sharding import PartitionSpec as P

STEP = 200

learn_rate = 0.02
beta_first = 0.9
beta_second = 0.999
epsilon = 1e-08

ROW_TILE = 256
CHUNK = 32
MIB = 1024 * 1024


def pack_kernel(columns, cache_ref, *refs):
    *outs, by_group = refs
    groups = cache_ref.shape[2]
    own = outs[0].shape[1]
    repeat = own * columns // groups
    for side in range(2):
        for group in range(groups):
            by_group[group, side] = cache_ref[:, side, group].astype(jnp.bfloat16)
    column = lax.axis_index("cache")
    for offset in range(columns):
        first = (column ^ offset) // repeat * own
        for slot in range(own):
            for side in range(2):
                outs[offset][side, slot] = by_group[first + slot, side]


def pack(cache, columns, own):
    share, _, groups, width = cache.shape
    slice_shape = jax.ShapeDtypeStruct((2, own, share, width), jnp.bfloat16)
    return pl.pallas_call(
        functools.partial(pack_kernel, columns),
        out_shape=[slice_shape] * columns,
        scratch_shapes=[pltpu.VMEM((groups, 2, share, width), jnp.bfloat16)],
        compiler_params=pltpu.CompilerParams(vmem_limit_bytes=16 * MIB),
        name="pack",
    )(cache)


def attend_kernel(score_scale, per_group, pieces, *refs):
    pair_refs, refs = refs[:pieces], refs[pieces:]
    queries_ref, grads_ref, lse_ref, dot_ref, mine_ref, mate_ref = refs[:6]
    keys, values, key_total, value_total = refs[6:10]
    even, odd = refs[10:14], refs[14:18]
    columns, _, own, share, width = pair_refs[0].shape
    length = columns * share
    positions = pieces * length
    tiles = queries_ref.shape[0]
    log2e = math.log2(math.e)
    factor = score_scale * log2e
    across = (((1,), (1,)), ((), ()))
    along = (((1,), (0,)), ((), ()))

    for piece, pair_ref in enumerate(pair_refs):
        at = pl.ds(piece * length, length)
        for slot in range(own):
            keys[slot, at] = pair_ref[:, 0, slot].reshape(length, width)
            values[slot, at] = pair_ref[:, 1, slot].reshape(length, width)
    key_total[...] = jnp.zeros_like(key_total)
    value_total[...] = jnp.zeros_like(value_total)

    def multiply(tile, buffers):
        scores, slopes, _, _ = buffers
        slot = tile // per_group
        scores[...] = lax.dot_general(
            keys[slot], queries_ref[tile], across, preferred_element_type=jnp.float32
        )
        slopes[...] = lax.dot_general(
            values[slot], grads_ref[tile], across, preferred_element_type=jnp.float32
        )

    def normalize(tile, buffers):
        scores, slopes, weights, dscores = buffers
        cuts = [pl.ds(start, CHUNK) for start in range(0, positions, CHUNK)]
        top = scores[cuts[0]]
        for cut in cuts[1:]:
            top = jnp.maximum(top, scores[cut])
        side_lse = lse_ref[tile] * log2e
        peak = jnp.maximum(jnp.max(top, axis=0, keepdims=True) * factor, side_lse)
        total = None
        dotted = None
        for cut in cuts:
            shifted = jnp.exp2(scores[cut] * factor - peak)
            product = shifted * slopes[cut]
            scores[cut] = shifted
            total = shifted if total is None else total + shifted
            dotted = product if dotted is None else dotted + product
        side = jnp.exp2(side_lse - peak)
        inverse = 1.0 / (jnp.sum(total, axis=0, keepdims=True) + side)
        delta = (jnp.sum(dotted, axis=0, keepdims=True) + side * dot_ref[tile]) * inverse
        for cut in cuts:
            probability = scores[cut] * inverse
            weights[cut] = probability.astype(jnp.bfloat16)
            dscores[cut] = (probability * (slopes[cut] - delta)).astype(jnp.bfloat16)

    def accumulate(tile, buffers):
        _, _, weights, dscores = buffers
        slot = tile // per_group
        key_total[slot] += lax.dot_general(
            dscores[...], queries_ref[tile], along, preferred_element_type=jnp.float32
        )
        value_total[slot] += lax.dot_general(
            weights[...], grads_ref[tile], along, preferred_element_type=jnp.float32
        )

    multiply(0, even)
    multiply(1, odd)
    normalize(0, even)

    def two_tiles(step, carry):
        tile = step * 2
        multiply(tile + 2, even)
        normalize(tile + 1, odd)
        accumulate(tile, even)
        multiply(tile + 3, odd)
        normalize(tile + 2, even)
        accumulate(tile + 1, odd)
        return carry

    lax.fori_loop(0, tiles // 2 - 1, two_tiles, 0)
    normalize(tiles - 1, odd)
    accumulate(tiles - 2, even)
    accumulate(tiles - 1, odd)

    half = positions // 2
    shape = mine_ref.shape[:2] + (share, width)
    for slot in range(own):
        key_sum = key_total[slot] * score_scale
        value_sum = value_total[slot]
        mine_ref[:, :, 0, slot] = key_sum[:half].reshape(shape)
        mine_ref[:, :, 1, slot] = value_sum[:half].reshape(shape)
        mate_ref[:, :, 0, slot] = key_sum[half:].astype(jnp.bfloat16).reshape(shape)
        mate_ref[:, :, 1, slot] = value_sum[half:].astype(jnp.bfloat16).reshape(shape)


def attend(pairs, queries, grads, lse_rows, dot_rows, score_scale):
    columns, _, own, share, width = pairs[0].shape
    pieces = len(pairs)
    positions = pieces * columns * share
    tiles, row_tile, _ = queries.shape
    rows = tiles * row_tile
    half = (pieces // 2, columns, 2, own, share, width)
    buffers = [
        pltpu.VMEM((positions, row_tile), jnp.float32),
        pltpu.VMEM((positions, row_tile), jnp.float32),
        pltpu.VMEM((positions, row_tile), jnp.bfloat16),
        pltpu.VMEM((positions, row_tile), jnp.bfloat16),
    ]
    return pl.pallas_call(
        functools.partial(attend_kernel, score_scale, tiles // own, pieces),
        out_shape=(
            jax.ShapeDtypeStruct(half, jnp.float32),
            jax.ShapeDtypeStruct(half, jnp.bfloat16),
        ),
        scratch_shapes=[
            pltpu.VMEM((own, positions, width), jnp.bfloat16),
            pltpu.VMEM((own, positions, width), jnp.bfloat16),
            pltpu.VMEM((own, positions, width), jnp.float32),
            pltpu.VMEM((own, positions, width), jnp.float32),
        ]
        + buffers
        + buffers,
        compiler_params=pltpu.CompilerParams(vmem_limit_bytes=44 * MIB),
        cost_estimate=pl.CostEstimate(
            flops=8 * rows * positions * width,
            bytes_accessed=4 * rows * width + 8 * own * positions * width,
            transcendentals=rows * positions,
        ),
        name="attend",
    )(*pairs, queries, grads, lse_rows, dot_rows)


def chip_sum_kernel(mine_ref, mate_ref, *outs):
    for offset, out in enumerate(outs):
        out[...] = (mine_ref[offset] + mate_ref[offset].astype(jnp.float32)).astype(out.dtype)


def chip_sum(mine, mate):
    chips = mine.shape[0]
    shape = mine.shape[1:]
    return pl.pallas_call(
        chip_sum_kernel,
        out_shape=[
            jax.ShapeDtypeStruct(shape, jnp.float32 if offset == 0 else jnp.bfloat16)
            for offset in range(chips)
        ],
        compiler_params=pltpu.CompilerParams(vmem_limit_bytes=16 * MIB),
        name="chip_sum",
    )(mine, mate)


def column_sum_kernel(away, mine_ref, *refs):
    others, outs = refs[:away], refs[away:]
    for offset, out in enumerate(outs):
        total = mine_ref[offset]
        for other in others:
            total = total + other[offset].astype(jnp.float32)
        out[...] = total.astype(out.dtype)


def column_sum(mine, others):
    columns = mine.shape[0]
    shape = mine.shape[1:]
    return pl.pallas_call(
        functools.partial(column_sum_kernel, len(others)),
        out_shape=[
            jax.ShapeDtypeStruct(shape, jnp.float32 if offset == 0 else jnp.bfloat16)
            for offset in range(columns)
        ],
        compiler_params=pltpu.CompilerParams(vmem_limit_bytes=16 * MIB),
        name="column_sum",
    )(mine, *others)


def adam_kernel(columns, *refs):
    parts, refs = refs[:columns], refs[columns:]
    cache_ref, first_ref, second_ref, new_cache, new_first, new_second, by_offset = refs
    groups = cache_ref.shape[2]
    own = parts[0].shape[1]
    repeat = own * columns // groups
    for offset, part in enumerate(parts):
        by_offset[offset] = part[...].astype(jnp.float32)
    column = lax.axis_index("cache")
    for side in range(2):
        for group in range(groups):
            first_owner = group // own * repeat
            slot = group % own
            gradient = by_offset[column ^ first_owner, side, slot]
            for owner in range(first_owner + 1, first_owner + repeat):
                gradient = gradient + by_offset[column ^ owner, side, slot]
            first = beta_first * first_ref[:, side, group] + (1.0 - beta_first) * gradient
            second = (
                beta_second * second_ref[:, side, group]
                + (1.0 - beta_second) * gradient * gradient
            )
            first_hat = first / (1.0 - beta_first**STEP)
            second_hat = second / (1.0 - beta_second**STEP)
            new_cache[:, side, group] = cache_ref[
                :, side, group
            ] - learn_rate * first_hat / (jnp.sqrt(second_hat) + epsilon)
            new_first[:, side, group] = first
            new_second[:, side, group] = second


def adam(parts, cache, first_moment, second_moment):
    shape = jax.ShapeDtypeStruct(cache.shape, jnp.float32)
    return pl.pallas_call(
        functools.partial(adam_kernel, len(parts)),
        out_shape=(shape, shape, shape),
        scratch_shapes=[pltpu.VMEM((len(parts),) + parts[0].shape, jnp.float32)],
        compiler_params=pltpu.CompilerParams(vmem_limit_bytes=16 * MIB),
        name="adam",
    )(*parts, cache, first_moment, second_moment)


def swap(value, axis, size, flip):
    return lax.ppermute(value, axis, [(place, place ^ flip) for place in range(size)])


def per_device(
    dp_size, columns, queries, out_grad, self_lse, self_dot, cache, first_moment, second_moment
):
    _, _, groups, width = cache.shape
    tokens, heads, _ = queries.shape
    chips = dp_size // 2
    group_size = heads // groups
    score_scale = 1.0 / math.sqrt(width)
    own = max(1, groups // columns)
    repeat = own * columns // groups
    own_tokens = tokens // repeat
    column = lax.axis_index("cache")
    first_group = column // repeat * own
    first_token = column % repeat * own_tokens

    slices = pack(cache, columns, own)
    gathered = jnp.stack(
        [slices[0]] + [swap(slices[k], "cache", columns, k) for k in range(1, columns)]
    )
    pairs = [gathered] + [swap(gathered, "dp", dp_size, 2 * k) for k in range(1, chips)]
    pairs = pairs + [swap(pair, "dp", dp_size, 1) for pair in pairs]

    def tiles_of(array):
        parts = array.reshape((tokens, groups, group_size) + array.shape[2:])
        part = lax.dynamic_slice_in_dim(parts, first_token, own_tokens, 0)
        part = lax.dynamic_slice_in_dim(part, first_group, own, 1)
        return jnp.moveaxis(part, 1, 0).reshape((-1, ROW_TILE) + array.shape[2:])

    mine, mate = attend(
        pairs,
        tiles_of(queries),
        tiles_of(out_grad),
        tiles_of(self_lse)[:, None],
        tiles_of(self_dot)[:, None],
        score_scale,
    )
    by_chip = chip_sum(mine, swap(mate, "dp", dp_size, 1))
    by_column = column_sum(
        by_chip[0], [swap(by_chip[k], "dp", dp_size, 2 * k) for k in range(1, chips)]
    )
    parts = [by_column[0]] + [
        swap(by_column[k], "cache", columns, k) for k in range(1, columns)
    ]
    return adam(parts, cache, first_moment, second_moment)


def solution(mesh):
    in_specs = (
        P("dp", None, None),
        P("dp", None, None),
        P("dp", None),
        P("dp", None),
        P(("dp", "cache"), None, None, None),
        P(("dp", "cache"), None, None, None),
        P(("dp", "cache"), None, None, None),
    )
    out_specs = (
        P(("dp", "cache"), None, None, None),
        P(("dp", "cache"), None, None, None),
        P(("dp", "cache"), None, None, None),
    )
    return jax.shard_map(
        functools.partial(per_device, mesh.shape["dp"], mesh.shape["cache"]),
        mesh=mesh,
        in_specs=in_specs,
        out_specs=out_specs,
        check_vma=False,
    )
```

```python
import functools
import math

import jax
import jax.numpy as jnp
from jax import lax
from jax.experimental import pallas as pl
from jax.experimental.pallas import tpu as pltpu
from jax.sharding import PartitionSpec as P

STEP = 200

learn_rate = 0.02
beta_first = 0.9
beta_second = 0.999
epsilon = 1e-08

ROW_TILE = 256
CHUNK = 32
MIB = 1024 * 1024


def pack_kernel(repeat, cache_ref, out_ref):
    columns, _, own, _, _ = out_ref.shape
    for column in range(columns):
        for side in range(2):
            for slot in range(own):
                group = column // repeat * own + slot
                out_ref[column, side, slot] = cache_ref[:, side, group].astype(jnp.bfloat16)


def pack(cache, columns, own):
    share, _, groups, width = cache.shape
    return pl.pallas_call(
        functools.partial(pack_kernel, own * columns // groups),
        out_shape=jax.ShapeDtypeStruct((columns, 2, own, share, width), jnp.bfloat16),
        compiler_params=pltpu.CompilerParams(vmem_limit_bytes=16 * MIB),
        name="pack",
    )(cache)


def attend_kernel(score_scale, per_group, *refs):
    pair_refs, refs = refs[:2], refs[2:]
    queries_ref, grads_ref, lse_ref, dot_ref, mine_ref, mate_ref = refs[:6]
    keys, values, key_total, value_total = refs[6:10]
    even, odd = refs[10:14], refs[14:18]
    chips, columns, _, own, share, width = pair_refs[0].shape
    half = chips * columns * share
    positions = 2 * half
    tiles = queries_ref.shape[0]
    log2e = math.log2(math.e)
    factor = score_scale * log2e
    across = (((1,), (1,)), ((), ()))
    along = (((1,), (0,)), ((), ()))

    for piece, pair_ref in enumerate(pair_refs):
        at = pl.ds(piece * half, half)
        for slot in range(own):
            keys[slot, at] = pair_ref[:, :, 0, slot].reshape(half, width)
            values[slot, at] = pair_ref[:, :, 1, slot].reshape(half, width)
    key_total[...] = jnp.zeros_like(key_total)
    value_total[...] = jnp.zeros_like(value_total)

    def multiply(tile, buffers):
        scores, slopes, _, _ = buffers
        slot = tile // per_group
        scores[...] = lax.dot_general(
            keys[slot], queries_ref[tile], across, preferred_element_type=jnp.float32
        )
        slopes[...] = lax.dot_general(
            values[slot], grads_ref[tile], across, preferred_element_type=jnp.float32
        )

    def normalize(tile, buffers):
        scores, slopes, weights, dscores = buffers
        cuts = [pl.ds(start, CHUNK) for start in range(0, positions, CHUNK)]
        top = scores[cuts[0]]
        for cut in cuts[1:]:
            top = jnp.maximum(top, scores[cut])
        side_lse = lse_ref[tile] * log2e
        peak = jnp.maximum(jnp.max(top, axis=0, keepdims=True) * factor, side_lse)
        total = None
        dotted = None
        for cut in cuts:
            shifted = jnp.exp2(scores[cut] * factor - peak)
            product = shifted * slopes[cut]
            scores[cut] = shifted
            total = shifted if total is None else total + shifted
            dotted = product if dotted is None else dotted + product
        side = jnp.exp2(side_lse - peak)
        inverse = 1.0 / (jnp.sum(total, axis=0, keepdims=True) + side)
        delta = (jnp.sum(dotted, axis=0, keepdims=True) + side * dot_ref[tile]) * inverse
        for cut in cuts:
            probability = scores[cut] * inverse
            weights[cut] = probability.astype(jnp.bfloat16)
            dscores[cut] = (probability * (slopes[cut] - delta)).astype(jnp.bfloat16)

    def accumulate(tile, buffers):
        _, _, weights, dscores = buffers
        slot = tile // per_group
        key_total[slot] += lax.dot_general(
            dscores[...], queries_ref[tile], along, preferred_element_type=jnp.float32
        )
        value_total[slot] += lax.dot_general(
            weights[...], grads_ref[tile], along, preferred_element_type=jnp.float32
        )

    multiply(0, even)
    multiply(1, odd)
    normalize(0, even)

    def two_tiles(step, carry):
        tile = step * 2
        multiply(tile + 2, even)
        normalize(tile + 1, odd)
        accumulate(tile, even)
        multiply(tile + 3, odd)
        normalize(tile + 2, even)
        accumulate(tile + 1, odd)
        return carry

    lax.fori_loop(0, tiles // 2 - 1, two_tiles, 0)
    normalize(tiles - 1, odd)
    accumulate(tiles - 2, even)
    accumulate(tiles - 1, odd)

    shape = mine_ref.shape[:2] + (share, width)
    for slot in range(own):
        key_sum = key_total[slot] * score_scale
        value_sum = value_total[slot]
        mine_ref[:, :, 0, slot] = key_sum[:half].reshape(shape)
        mine_ref[:, :, 1, slot] = value_sum[:half].reshape(shape)
        mate_ref[:, :, 0, slot] = key_sum[half:].astype(jnp.bfloat16).reshape(shape)
        mate_ref[:, :, 1, slot] = value_sum[half:].astype(jnp.bfloat16).reshape(shape)


def attend(pairs, queries, grads, lse_rows, dot_rows, score_scale):
    half = pairs[0].shape
    chips, columns, _, own, share, width = half
    positions = 2 * chips * columns * share
    tiles, row_tile, _ = queries.shape
    rows = tiles * row_tile
    buffers = [
        pltpu.VMEM((positions, row_tile), jnp.float32),
        pltpu.VMEM((positions, row_tile), jnp.float32),
        pltpu.VMEM((positions, row_tile), jnp.bfloat16),
        pltpu.VMEM((positions, row_tile), jnp.bfloat16),
    ]
    return pl.pallas_call(
        functools.partial(attend_kernel, score_scale, tiles // own),
        out_shape=(
            jax.ShapeDtypeStruct(half, jnp.float32),
            jax.ShapeDtypeStruct(half, jnp.bfloat16),
        ),
        scratch_shapes=[
            pltpu.VMEM((own, positions, width), jnp.bfloat16),
            pltpu.VMEM((own, positions, width), jnp.bfloat16),
            pltpu.VMEM((own, positions, width), jnp.float32),
            pltpu.VMEM((own, positions, width), jnp.float32),
        ]
        + buffers
        + buffers,
        compiler_params=pltpu.CompilerParams(vmem_limit_bytes=44 * MIB),
        cost_estimate=pl.CostEstimate(
            flops=8 * rows * positions * width,
            bytes_accessed=4 * rows * width + 8 * own * positions * width,
            transcendentals=rows * positions,
        ),
        name="attend",
    )(*pairs, queries, grads, lse_rows, dot_rows)


def core_sum_kernel(mine_ref, mate_ref, out_ref):
    out_ref[...] = (mine_ref[...] + mate_ref[...].astype(jnp.float32)).astype(out_ref.dtype)


def core_sum(mine, mate):
    return pl.pallas_call(
        core_sum_kernel,
        out_shape=jax.ShapeDtypeStruct(mate.shape, mate.dtype),
        compiler_params=pltpu.CompilerParams(vmem_limit_bytes=16 * MIB),
        name="core_sum",
    )(mine, mate)


def chip_sum_kernel(parts_ref, out_ref):
    total = parts_ref[0].astype(jnp.float32)
    for chip in range(1, parts_ref.shape[0]):
        total = total + parts_ref[chip].astype(jnp.float32)
    out_ref[...] = total.astype(out_ref.dtype)


def chip_sum(parts):
    return pl.pallas_call(
        chip_sum_kernel,
        out_shape=jax.ShapeDtypeStruct(parts.shape[1:], parts.dtype),
        compiler_params=pltpu.CompilerParams(vmem_limit_bytes=16 * MIB),
        name="chip_sum",
    )(parts)


def adam_kernel(parts_ref, cache_ref, first_ref, second_ref, new_cache, new_first, new_second):
    columns, _, own, _, _ = parts_ref.shape
    groups = cache_ref.shape[2]
    repeat = own * columns // groups
    for side in range(2):
        for group in range(groups):
            owner, slot = group // own * repeat, group % own
            gradient = parts_ref[owner, side, slot].astype(jnp.float32)
            for other in range(owner + 1, owner + repeat):
                gradient = gradient + parts_ref[other, side, slot].astype(jnp.float32)
            first = beta_first * first_ref[:, side, group] + (1.0 - beta_first) * gradient
            second = (
                beta_second * second_ref[:, side, group]
                + (1.0 - beta_second) * gradient * gradient
            )
            first_hat = first / (1.0 - beta_first**STEP)
            second_hat = second / (1.0 - beta_second**STEP)
            new_cache[:, side, group] = cache_ref[
                :, side, group
            ] - learn_rate * first_hat / (jnp.sqrt(second_hat) + epsilon)
            new_first[:, side, group] = first
            new_second[:, side, group] = second


def adam(parts, cache, first_moment, second_moment):
    shape = jax.ShapeDtypeStruct(cache.shape, jnp.float32)
    return pl.pallas_call(
        adam_kernel,
        out_shape=(shape, shape, shape),
        compiler_params=pltpu.CompilerParams(vmem_limit_bytes=16 * MIB),
        name="adam",
    )(parts, cache, first_moment, second_moment)


def core_swap(value, dp_size):
    return lax.ppermute(value, "dp", [(place, place ^ 1) for place in range(dp_size)])


def chips_exchange(value, dp_size):
    same_core = [list(range(core, dp_size, 2)) for core in range(2)]
    return lax.all_to_all(value, "dp", 0, 0, axis_index_groups=same_core, tiled=True)


def per_device(
    dp_size, columns, queries, out_grad, self_lse, self_dot, cache, first_moment, second_moment
):
    _, _, groups, width = cache.shape
    tokens, heads, _ = queries.shape
    chips = dp_size // 2
    group_size = heads // groups
    score_scale = 1.0 / math.sqrt(width)
    own = max(1, groups // columns)
    repeat = own * columns // groups
    own_tokens = tokens // repeat
    column = lax.axis_index("cache")
    first_group = column // repeat * own
    first_token = column % repeat * own_tokens

    column_pairs = lax.all_to_all(pack(cache, columns, own), "cache", 0, 0, tiled=True)
    copies = jnp.broadcast_to(column_pairs, (chips,) + column_pairs.shape)
    core_pairs = chips_exchange(copies, dp_size)
    pairs = (core_pairs, core_swap(core_pairs, dp_size))

    def tiles_of(array):
        parts = array.reshape((tokens, groups, group_size) + array.shape[2:])
        part = lax.dynamic_slice_in_dim(parts, first_token, own_tokens, 0)
        part = lax.dynamic_slice_in_dim(part, first_group, own, 1)
        return jnp.moveaxis(part, 1, 0).reshape((-1, ROW_TILE) + array.shape[2:])

    mine, mate = attend(
        pairs,
        tiles_of(queries),
        tiles_of(out_grad),
        tiles_of(self_lse)[:, None],
        tiles_of(self_dot)[:, None],
        score_scale,
    )
    by_chip = chips_exchange(core_sum(mine, core_swap(mate, dp_size)), dp_size)
    by_column = lax.all_to_all(chip_sum(by_chip), "cache", 0, 0, tiled=True)
    return adam(by_column, cache, first_moment, second_moment)


def solution(mesh):
    in_specs = (
        P("dp", None, None),
        P("dp", None, None),
        P("dp", None),
        P("dp", None),
        P(("dp", "cache"), None, None, None),
        P(("dp", "cache"), None, None, None),
        P(("dp", "cache"), None, None, None),
    )
    out_specs = (
        P(("dp", "cache"), None, None, None),
        P(("dp", "cache"), None, None, None),
        P(("dp", "cache"), None, None, None),
    )
    return jax.shard_map(
        functools.partial(per_device, mesh.shape["dp"], mesh.shape["cache"]),
        mesh=mesh,
        in_specs=in_specs,
        out_specs=out_specs,
        check_vma=False,
    )
```

```python
import functools
import math

import jax
import jax.numpy as jnp
from jax import lax
from jax.experimental import pallas as pl
from jax.experimental.pallas import tpu as pltpu
from jax.sharding import PartitionSpec as P

STEP = 200

learn_rate = 0.02
beta_first = 0.9
beta_second = 0.999
epsilon = 1e-08

ROW_TILE = 512
CHUNK = 16
MIB = 1024 * 1024


def flips(size):
    return list(range(size - 1, -1, -1))


def pack_kernel(columns, cache_ref, *refs):
    *outs, by_group = refs
    groups = cache_ref.shape[2]
    own = outs[0].shape[1]
    repeat = own * columns // groups
    for side in range(2):
        for group in range(groups):
            by_group[group, side] = cache_ref[:, side, group].astype(jnp.bfloat16)
    column = lax.axis_index("cache")
    for out, flip in zip(outs, flips(columns)):
        first = (column ^ flip) // repeat * own
        for slot in range(own):
            for side in range(2):
                out[side, slot] = by_group[first + slot, side]


def pack(cache, columns, own):
    share, _, groups, width = cache.shape
    slice_shape = jax.ShapeDtypeStruct((2, own, share, width), jnp.bfloat16)
    return pl.pallas_call(
        functools.partial(pack_kernel, columns),
        out_shape=[slice_shape] * columns,
        scratch_shapes=[pltpu.VMEM((groups, 2, share, width), jnp.bfloat16)],
        compiler_params=pltpu.CompilerParams(vmem_limit_bytes=16 * MIB),
        name="pack",
    )(cache)


def attend_kernel(score_scale, per_group, pieces, *refs):
    pair_refs, refs = refs[:pieces], refs[pieces:]
    queries_ref, grads_ref, lse_ref, dot_ref, mine_ref, mate_ref = refs[:6]
    keys, values, key_total, value_total = refs[6:10]
    even, odd = refs[10:14], refs[14:18]
    columns, _, own, share, width = pair_refs[0].shape
    length = columns * share
    positions = pieces * length
    tiles = queries_ref.shape[0]
    log2e = math.log2(math.e)
    factor = score_scale * log2e
    across = (((1,), (1,)), ((), ()))
    along = (((1,), (0,)), ((), ()))

    for piece, pair_ref in enumerate(pair_refs):
        at = pl.ds(piece * length, length)
        for slot in range(own):
            keys[slot, at] = pair_ref[:, 0, slot].reshape(length, width)
            values[slot, at] = pair_ref[:, 1, slot].reshape(length, width)
    key_total[...] = jnp.zeros_like(key_total)
    value_total[...] = jnp.zeros_like(value_total)

    def multiply(tile, buffers):
        scores, slopes, _, _ = buffers
        slot = tile // per_group
        scores[...] = lax.dot_general(
            keys[slot], queries_ref[tile], across, preferred_element_type=jnp.float32
        )
        slopes[...] = lax.dot_general(
            values[slot], grads_ref[tile], across, preferred_element_type=jnp.float32
        )

    def normalize(tile, buffers):
        scores, slopes, weights, dscores = buffers
        cuts = [pl.ds(start, CHUNK) for start in range(0, positions, CHUNK)]
        top = scores[cuts[0]]
        for cut in cuts[1:]:
            top = jnp.maximum(top, scores[cut])
        side_lse = lse_ref[tile] * log2e
        peak = jnp.maximum(jnp.max(top, axis=0, keepdims=True) * factor, side_lse)
        total = None
        dotted = None
        for cut in cuts:
            shifted = jnp.exp2(scores[cut] * factor - peak)
            product = shifted * slopes[cut]
            scores[cut] = shifted
            total = shifted if total is None else total + shifted
            dotted = product if dotted is None else dotted + product
        side = jnp.exp2(side_lse - peak)
        inverse = 1.0 / (jnp.sum(total, axis=0, keepdims=True) + side)
        delta = (jnp.sum(dotted, axis=0, keepdims=True) + side * dot_ref[tile]) * inverse
        for cut in cuts:
            probability = scores[cut] * inverse
            weights[cut] = probability.astype(jnp.bfloat16)
            dscores[cut] = (probability * (slopes[cut] - delta)).astype(jnp.bfloat16)

    def accumulate(tile, buffers):
        _, _, weights, dscores = buffers
        slot = tile // per_group
        key_total[slot] += lax.dot_general(
            dscores[...], queries_ref[tile], along, preferred_element_type=jnp.float32
        )
        value_total[slot] += lax.dot_general(
            weights[...], grads_ref[tile], along, preferred_element_type=jnp.float32
        )

    multiply(0, even)
    multiply(1, odd)
    normalize(0, even)

    def two_tiles(step, carry):
        tile = step * 2
        multiply(tile + 2, even)
        normalize(tile + 1, odd)
        accumulate(tile, even)
        multiply(tile + 3, odd)
        normalize(tile + 2, even)
        accumulate(tile + 1, odd)
        return carry

    lax.fori_loop(0, tiles // 2 - 1, two_tiles, 0)
    normalize(tiles - 1, odd)
    accumulate(tiles - 2, even)
    accumulate(tiles - 1, odd)

    half = positions // 2
    shape = mine_ref.shape[:2] + (share, width)
    for slot in range(own):
        key_sum = key_total[slot] * score_scale
        value_sum = value_total[slot]
        mine_ref[:, :, 0, slot] = key_sum[:half].reshape(shape)
        mine_ref[:, :, 1, slot] = value_sum[:half].reshape(shape)
        mate_ref[:, :, 0, slot] = key_sum[half:].astype(jnp.bfloat16).reshape(shape)
        mate_ref[:, :, 1, slot] = value_sum[half:].astype(jnp.bfloat16).reshape(shape)


def attend(pairs, queries, grads, lse_rows, dot_rows, score_scale):
    columns, _, own, share, width = pairs[0].shape
    pieces = len(pairs)
    positions = pieces * columns * share
    tiles, row_tile, _ = queries.shape
    rows = tiles * row_tile
    half = (pieces // 2, columns, 2, own, share, width)
    buffers = [
        pltpu.VMEM((positions, row_tile), jnp.float32),
        pltpu.VMEM((positions, row_tile), jnp.float32),
        pltpu.VMEM((positions, row_tile), jnp.bfloat16),
        pltpu.VMEM((positions, row_tile), jnp.bfloat16),
    ]
    return pl.pallas_call(
        functools.partial(attend_kernel, score_scale, tiles // own, pieces),
        out_shape=(
            jax.ShapeDtypeStruct(half, jnp.float32),
            jax.ShapeDtypeStruct(half, jnp.bfloat16),
        ),
        scratch_shapes=[
            pltpu.VMEM((own, positions, width), jnp.bfloat16),
            pltpu.VMEM((own, positions, width), jnp.bfloat16),
            pltpu.VMEM((own, positions, width), jnp.float32),
            pltpu.VMEM((own, positions, width), jnp.float32),
        ]
        + buffers
        + buffers,
        compiler_params=pltpu.CompilerParams(vmem_limit_bytes=44 * MIB),
        cost_estimate=pl.CostEstimate(
            flops=8 * rows * positions * width,
            bytes_accessed=4 * rows * width + 8 * own * positions * width,
            transcendentals=rows * positions,
        ),
        name="attend",
    )(*pairs, queries, grads, lse_rows, dot_rows)


def chip_sum_kernel(mine_ref, mate_ref, *outs):
    for offset, out in enumerate(outs):
        out[...] = (mine_ref[offset] + mate_ref[offset].astype(jnp.float32)).astype(out.dtype)


def chip_sum(mine, mate):
    chips = mine.shape[0]
    shape = mine.shape[1:]
    return pl.pallas_call(
        chip_sum_kernel,
        out_shape=[
            jax.ShapeDtypeStruct(shape, jnp.bfloat16 if flip else jnp.float32)
            for flip in flips(chips)
        ],
        compiler_params=pltpu.CompilerParams(vmem_limit_bytes=16 * MIB),
        name="chip_sum",
    )(mine, mate)


def column_sum_kernel(away, mine_ref, *refs):
    others, outs = refs[:away], refs[away:]
    for offset, out in enumerate(outs):
        total = mine_ref[offset]
        for other in others:
            total = total + other[offset].astype(jnp.float32)
        out[...] = total.astype(out.dtype)


def column_sum(mine, others):
    columns = mine.shape[0]
    shape = mine.shape[1:]
    return pl.pallas_call(
        functools.partial(column_sum_kernel, len(others)),
        out_shape=[
            jax.ShapeDtypeStruct(shape, jnp.bfloat16 if flip else jnp.float32)
            for flip in flips(columns)
        ],
        compiler_params=pltpu.CompilerParams(vmem_limit_bytes=16 * MIB),
        name="column_sum",
    )(mine, *others)


def adam_kernel(columns, *refs):
    parts, refs = refs[:columns], refs[columns:]
    cache_ref, first_ref, second_ref, new_cache, new_first, new_second, by_flip = refs
    groups = cache_ref.shape[2]
    own = parts[0].shape[1]
    repeat = own * columns // groups
    for part, flip in zip(parts, flips(columns)):
        by_flip[flip] = part[...].astype(jnp.float32)
    column = lax.axis_index("cache")
    for side in range(2):
        for group in range(groups):
            first_owner = group // own * repeat
            slot = group % own
            gradient = by_flip[column ^ first_owner, side, slot]
            for owner in range(first_owner + 1, first_owner + repeat):
                gradient = gradient + by_flip[column ^ owner, side, slot]
            first = beta_first * first_ref[:, side, group] + (1.0 - beta_first) * gradient
            second = (
                beta_second * second_ref[:, side, group]
                + (1.0 - beta_second) * gradient * gradient
            )
            first_hat = first / (1.0 - beta_first**STEP)
            second_hat = second / (1.0 - beta_second**STEP)
            new_cache[:, side, group] = cache_ref[
                :, side, group
            ] - learn_rate * first_hat / (jnp.sqrt(second_hat) + epsilon)
            new_first[:, side, group] = first
            new_second[:, side, group] = second


def adam(parts, cache, first_moment, second_moment):
    shape = jax.ShapeDtypeStruct(cache.shape, jnp.float32)
    return pl.pallas_call(
        functools.partial(adam_kernel, len(parts)),
        out_shape=(shape, shape, shape),
        scratch_shapes=[pltpu.VMEM((len(parts),) + parts[0].shape, jnp.float32)],
        compiler_params=pltpu.CompilerParams(vmem_limit_bytes=16 * MIB),
        name="adam",
    )(*parts, cache, first_moment, second_moment)


def swap(value, axis, size, flip):
    return lax.ppermute(value, axis, [(place, place ^ flip) for place in range(size)])


def swap_all(values, axis, size, stride):
    return [
        swap(value, axis, size, flip * stride) if flip else value
        for value, flip in zip(values, flips(len(values)))
    ]


def per_device(
    dp_size, columns, queries, out_grad, self_lse, self_dot, cache, first_moment, second_moment
):
    _, _, groups, width = cache.shape
    tokens, heads, _ = queries.shape
    chips = dp_size // 2
    group_size = heads // groups
    score_scale = 1.0 / math.sqrt(width)
    own = max(1, groups // columns)
    repeat = own * columns // groups
    own_tokens = tokens // repeat
    column = lax.axis_index("cache")
    first_group = column // repeat * own
    first_token = column % repeat * own_tokens

    slices = pack(cache, columns, own)
    gathered = jnp.stack(swap_all(slices, "cache", columns, 1))
    pairs = swap_all([gathered] * chips, "dp", dp_size, 2)
    pairs = pairs + [swap(pair, "dp", dp_size, 1) for pair in pairs]

    def tiles_of(array):
        parts = array.reshape((tokens, groups, group_size) + array.shape[2:])
        part = lax.dynamic_slice_in_dim(parts, first_token, own_tokens, 0)
        part = lax.dynamic_slice_in_dim(part, first_group, own, 1)
        return jnp.moveaxis(part, 1, 0).reshape((-1, ROW_TILE) + array.shape[2:])

    mine, mate = attend(
        pairs,
        tiles_of(queries),
        tiles_of(out_grad),
        tiles_of(self_lse)[:, None],
        tiles_of(self_dot)[:, None],
        score_scale,
    )
    by_chip = chip_sum(mine, swap(mate, "dp", dp_size, 1))
    *away, home = swap_all(by_chip, "dp", dp_size, 2)
    by_column = column_sum(home, away)
    parts = swap_all(by_column, "cache", columns, 1)
    return adam(parts, cache, first_moment, second_moment)


def solution(mesh):
    in_specs = (
        P("dp", None, None),
        P("dp", None, None),
        P("dp", None),
        P("dp", None),
        P(("dp", "cache"), None, None, None),
        P(("dp", "cache"), None, None, None),
        P(("dp", "cache"), None, None, None),
    )
    out_specs = (
        P(("dp", "cache"), None, None, None),
        P(("dp", "cache"), None, None, None),
        P(("dp", "cache"), None, None, None),
    )
    return jax.shard_map(
        functools.partial(per_device, mesh.shape["dp"], mesh.shape["cache"]),
        mesh=mesh,
        in_specs=in_specs,
        out_specs=out_specs,
        check_vma=False,
    )
```

```python
import functools
import math

import jax
import jax.numpy as jnp
from jax import lax
from jax.experimental import pallas as pl
from jax.experimental.pallas import tpu as pltpu
from jax.sharding import PartitionSpec as P

STEP = 200

learn_rate = 0.02
beta_first = 0.9
beta_second = 0.999
epsilon = 1e-08

ROW_TILE = 512
CHUNK = 16
MIB = 1024 * 1024


def flips(size):
    return list(range(size - 1, -1, -1))


def pack_kernel(columns, cache_ref, keep_ref, send_ref, by_group):
    groups = cache_ref.shape[2]
    own = keep_ref.shape[3]
    repeat = own * columns // groups
    for side in range(2):
        for group in range(groups):
            by_group[group, side] = cache_ref[:, side, group].astype(jnp.bfloat16)
    column = lax.axis_index("cache")
    for flip in range(columns):
        first = (column ^ flip) // repeat * own
        out_ref = send_ref if flip % 2 else keep_ref
        for slot in range(own):
            for side in range(2):
                out_ref[flip // 2, 0, side, slot] = by_group[first + slot, side]


def pack(cache, columns, own):
    share, _, groups, width = cache.shape
    half = jax.ShapeDtypeStruct((columns // 2, 1, 2, own, share, width), jnp.bfloat16)
    return pl.pallas_call(
        functools.partial(pack_kernel, columns),
        out_shape=(half, half),
        scratch_shapes=[pltpu.VMEM((groups, 2, share, width), jnp.bfloat16)],
        compiler_params=pltpu.CompilerParams(vmem_limit_bytes=16 * MIB),
        name="pack",
    )(cache)


def attend_kernel(score_scale, per_group, pieces, *refs):
    pair_refs, refs = refs[:pieces], refs[pieces:]
    queries_ref, grads_ref, lse_ref, dot_ref, mate_ref, weights_ref, dscores_ref = refs[:7]
    keys, values, key_total, value_total = refs[7:11]
    even, odd = refs[11:15], refs[15:19]
    columns, _, own, share, width = pair_refs[0].shape
    length = columns * share
    positions = pieces * length
    half = positions // 2
    tiles = queries_ref.shape[0]
    log2e = math.log2(math.e)
    factor = score_scale * log2e
    across = (((1,), (1,)), ((), ()))
    along = (((1,), (0,)), ((), ()))

    for piece, pair_ref in enumerate(pair_refs):
        at = pl.ds(piece * length, length)
        for slot in range(own):
            keys[slot, at] = pair_ref[:, 0, slot].reshape(length, width)
            values[slot, at] = pair_ref[:, 1, slot].reshape(length, width)
    key_total[...] = jnp.zeros_like(key_total)
    value_total[...] = jnp.zeros_like(value_total)

    def multiply(tile, buffers):
        scores, slopes, _, _ = buffers
        slot = tile // per_group
        scores[...] = lax.dot_general(
            keys[slot], queries_ref[tile], across, preferred_element_type=jnp.float32
        )
        slopes[...] = lax.dot_general(
            values[slot], grads_ref[tile], across, preferred_element_type=jnp.float32
        )

    def normalize(tile, buffers):
        scores, slopes, weights, dscores = buffers
        cuts = [pl.ds(start, CHUNK) for start in range(0, positions, CHUNK)]
        top = scores[cuts[0]]
        for cut in cuts[1:]:
            top = jnp.maximum(top, scores[cut])
        side_lse = lse_ref[tile] * log2e
        peak = jnp.maximum(jnp.max(top, axis=0, keepdims=True) * factor, side_lse)
        total = None
        dotted = None
        for cut in cuts:
            shifted = jnp.exp2(scores[cut] * factor - peak)
            product = shifted * slopes[cut]
            scores[cut] = shifted
            total = shifted if total is None else total + shifted
            dotted = product if dotted is None else dotted + product
        side = jnp.exp2(side_lse - peak)
        inverse = 1.0 / (jnp.sum(total, axis=0, keepdims=True) + side)
        delta = (jnp.sum(dotted, axis=0, keepdims=True) + side * dot_ref[tile]) * inverse
        for start, cut in zip(range(0, positions, CHUNK), cuts):
            probability = scores[cut] * inverse
            weight = probability.astype(jnp.bfloat16)
            dscore = (probability * (slopes[cut] - delta)).astype(jnp.bfloat16)
            if start < half:
                weights_ref[tile, cut] = weight
                dscores_ref[tile, cut] = dscore
            else:
                weights[pl.ds(start - half, CHUNK)] = weight
                dscores[pl.ds(start - half, CHUNK)] = dscore

    def accumulate(tile, buffers):
        _, _, weights, dscores = buffers
        slot = tile // per_group
        key_total[slot] += lax.dot_general(
            dscores[...], queries_ref[tile], along, preferred_element_type=jnp.float32
        )
        value_total[slot] += lax.dot_general(
            weights[...], grads_ref[tile], along, preferred_element_type=jnp.float32
        )

    multiply(0, even)
    multiply(1, odd)
    normalize(0, even)

    def two_tiles(step, carry):
        tile = step * 2
        multiply(tile + 2, even)
        normalize(tile + 1, odd)
        accumulate(tile, even)
        multiply(tile + 3, odd)
        normalize(tile + 2, even)
        accumulate(tile + 1, odd)
        return carry

    lax.fori_loop(0, tiles // 2 - 1, two_tiles, 0)
    normalize(tiles - 1, odd)
    accumulate(tiles - 2, even)
    accumulate(tiles - 1, odd)

    shape = mate_ref.shape[:2] + (share, width)
    for slot in range(own):
        key_sum = key_total[slot] * score_scale
        mate_ref[:, :, 0, slot] = key_sum.astype(jnp.bfloat16).reshape(shape)
        mate_ref[:, :, 1, slot] = value_total[slot].astype(jnp.bfloat16).reshape(shape)


def attend(pairs, queries, grads, lse_rows, dot_rows, score_scale):
    columns, _, own, share, width = pairs[0].shape
    pieces = len(pairs)
    positions = pieces * columns * share
    half = positions // 2
    tiles, row_tile, _ = queries.shape
    rows = tiles * row_tile
    buffers = [
        pltpu.VMEM((positions, row_tile), jnp.float32),
        pltpu.VMEM((positions, row_tile), jnp.float32),
        pltpu.VMEM((half, row_tile), jnp.bfloat16),
        pltpu.VMEM((half, row_tile), jnp.bfloat16),
    ]
    kept = jax.ShapeDtypeStruct((tiles, half, row_tile), jnp.bfloat16)
    return pl.pallas_call(
        functools.partial(attend_kernel, score_scale, tiles // own, pieces),
        out_shape=(
            jax.ShapeDtypeStruct((pieces // 2,) + pairs[0].shape, jnp.bfloat16),
            kept,
            kept,
        ),
        scratch_shapes=[
            pltpu.VMEM((own, positions, width), jnp.bfloat16),
            pltpu.VMEM((own, positions, width), jnp.bfloat16),
            pltpu.VMEM((own, half, width), jnp.float32),
            pltpu.VMEM((own, half, width), jnp.float32),
        ]
        + buffers
        + buffers,
        compiler_params=pltpu.CompilerParams(vmem_limit_bytes=40 * MIB),
        cost_estimate=pl.CostEstimate(
            flops=6 * rows * positions * width,
            bytes_accessed=4 * rows * width + 8 * own * positions * width,
            transcendentals=rows * positions,
        ),
        name="attend",
    )(*pairs, queries, grads, lse_rows, dot_rows)


def own_half_kernel(
    score_scale, per_group, weights_ref, dscores_ref, queries_ref, grads_ref, out_ref
):
    tiles = queries_ref.shape[0]
    chips, columns, _, own, share, width = out_ref.shape
    along = (((1,), (0,)), ((), ()))
    for slot in range(own):
        key_sum = None
        value_sum = None
        for tile in range(slot * per_group, (slot + 1) * per_group):
            key_part = lax.dot_general(
                dscores_ref[tile], queries_ref[tile], along, preferred_element_type=jnp.float32
            )
            value_part = lax.dot_general(
                weights_ref[tile], grads_ref[tile], along, preferred_element_type=jnp.float32
            )
            key_sum = key_part if key_sum is None else key_sum + key_part
            value_sum = value_part if value_sum is None else value_sum + value_part
        shape = (chips, columns, share, width)
        out_ref[:, :, 0, slot] = (key_sum * score_scale).reshape(shape)
        out_ref[:, :, 1, slot] = value_sum.reshape(shape)


def own_half(weights, dscores, queries, grads, shape, score_scale):
    tiles, half, row_tile = weights.shape
    width = shape[-1]
    own = shape[3]
    return pl.pallas_call(
        functools.partial(own_half_kernel, score_scale, tiles // own),
        out_shape=jax.ShapeDtypeStruct(shape, jnp.float32),
        compiler_params=pltpu.CompilerParams(vmem_limit_bytes=24 * MIB),
        cost_estimate=pl.CostEstimate(
            flops=4 * tiles * row_tile * half * width,
            bytes_accessed=4 * tiles * row_tile * (half + width),
            transcendentals=0,
        ),
        name="own_half",
    )(weights, dscores, queries, grads)


def chip_sum_kernel(mine_ref, mate_ref, *outs):
    for offset, out in enumerate(outs):
        out[...] = (mine_ref[offset] + mate_ref[offset].astype(jnp.float32)).astype(out.dtype)


def chip_sum(mine, mate):
    chips = mine.shape[0]
    shape = mine.shape[1:]
    return pl.pallas_call(
        chip_sum_kernel,
        out_shape=[
            jax.ShapeDtypeStruct(shape, jnp.bfloat16 if flip else jnp.float32)
            for flip in flips(chips)
        ],
        compiler_params=pltpu.CompilerParams(vmem_limit_bytes=16 * MIB),
        name="chip_sum",
    )(mine, mate)


def column_sum_kernel(away, mine_ref, *refs):
    others, (keep_ref, send_ref) = refs[:away], refs[away:]
    for flip in range(mine_ref.shape[0]):
        total = mine_ref[flip]
        for other in others:
            total = total + other[flip].astype(jnp.float32)
        out_ref = send_ref if flip % 2 else keep_ref
        out_ref[flip // 2, 0] = total.astype(jnp.bfloat16)


def column_sum(mine, others):
    columns = mine.shape[0]
    half = jax.ShapeDtypeStruct((columns // 2, 1) + mine.shape[1:], jnp.bfloat16)
    return pl.pallas_call(
        functools.partial(column_sum_kernel, len(others)),
        out_shape=(half, half),
        compiler_params=pltpu.CompilerParams(vmem_limit_bytes=16 * MIB),
        name="column_sum",
    )(mine, *others)


def adam_kernel(columns, pieces, *refs):
    parts, refs = refs[:pieces], refs[pieces:]
    cache_ref, first_ref, second_ref, new_cache, new_first, new_second, by_flip = refs
    groups = cache_ref.shape[2]
    own = by_flip.shape[2]
    repeat = own * columns // groups
    flip = 0
    for part in parts:
        sources = part.shape[1]
        by_flip[flip : flip + sources] = part[0].astype(jnp.float32)
        flip += sources
    column = lax.axis_index("cache")
    for side in range(2):
        for group in range(groups):
            first_owner = group // own * repeat
            slot = group % own
            gradient = by_flip[column ^ first_owner, side, slot]
            for owner in range(first_owner + 1, first_owner + repeat):
                gradient = gradient + by_flip[column ^ owner, side, slot]
            first = beta_first * first_ref[:, side, group] + (1.0 - beta_first) * gradient
            second = (
                beta_second * second_ref[:, side, group]
                + (1.0 - beta_second) * gradient * gradient
            )
            first_hat = first / (1.0 - beta_first**STEP)
            second_hat = second / (1.0 - beta_second**STEP)
            new_cache[:, side, group] = cache_ref[
                :, side, group
            ] - learn_rate * first_hat / (jnp.sqrt(second_hat) + epsilon)
            new_first[:, side, group] = first
            new_second[:, side, group] = second


def adam(parts, columns, cache, first_moment, second_moment):
    shape = jax.ShapeDtypeStruct(cache.shape, jnp.float32)
    return pl.pallas_call(
        functools.partial(adam_kernel, columns, len(parts)),
        out_shape=(shape, shape, shape),
        scratch_shapes=[pltpu.VMEM((columns,) + parts[0].shape[2:], jnp.float32)],
        compiler_params=pltpu.CompilerParams(vmem_limit_bytes=16 * MIB),
        name="adam",
    )(*parts, cache, first_moment, second_moment)


def swap(value, axis, size, flip):
    return lax.ppermute(value, axis, [(place, place ^ flip) for place in range(size)])


def swap_all(values, axis, size, stride):
    return [
        swap(value, axis, size, flip * stride) if flip else value
        for value, flip in zip(values, flips(len(values)))
    ]


def column_exchange(keep, send, columns):
    arrived = swap(send, "cache", columns, 1)
    bit = 2
    pieces = [keep, arrived]
    while bit < columns:
        evens = [piece[0::2] for piece in pieces]
        odds = [piece[1::2] for piece in pieces]
        arrived = swap(jnp.concatenate(odds, axis=1), "cache", columns, bit)
        pieces = evens + [arrived]
        bit *= 2
    return pieces


def per_device(
    dp_size, columns, queries, out_grad, self_lse, self_dot, cache, first_moment, second_moment
):
    _, _, groups, width = cache.shape
    tokens, heads, _ = queries.shape
    chips = dp_size // 2
    group_size = heads // groups
    score_scale = 1.0 / math.sqrt(width)
    own = max(1, groups // columns)
    repeat = own * columns // groups
    own_tokens = tokens // repeat
    column = lax.axis_index("cache")
    first_group = column // repeat * own
    first_token = column % repeat * own_tokens

    pieces = column_exchange(*pack(cache, columns, own), columns)
    gathered = jnp.concatenate([piece[0] for piece in pieces])
    pairs = swap_all([gathered] * chips, "dp", dp_size, 2)
    pairs = pairs + [swap(pair, "dp", dp_size, 1) for pair in pairs]

    def tiles_of(array):
        parts = array.reshape((tokens, groups, group_size) + array.shape[2:])
        part = lax.dynamic_slice_in_dim(parts, first_token, own_tokens, 0)
        part = lax.dynamic_slice_in_dim(part, first_group, own, 1)
        return jnp.moveaxis(part, 1, 0).reshape((-1, ROW_TILE) + array.shape[2:])

    query_tiles, grad_tiles = tiles_of(queries), tiles_of(out_grad)
    mate, weights, dscores = attend(
        pairs,
        query_tiles,
        grad_tiles,
        tiles_of(self_lse)[:, None],
        tiles_of(self_dot)[:, None],
        score_scale,
    )
    from_mate = swap(mate, "dp", dp_size, 1)
    mine = own_half(weights, dscores, query_tiles, grad_tiles, mate.shape, score_scale)
    *away, home = swap_all(chip_sum(mine, from_mate), "dp", dp_size, 2)
    parts = column_exchange(*column_sum(home, away), columns)
    return adam(parts, columns, cache, first_moment, second_moment)


def solution(mesh):
    in_specs = (
        P("dp", None, None),
        P("dp", None, None),
        P("dp", None),
        P("dp", None),
        P(("dp", "cache"), None, None, None),
        P(("dp", "cache"), None, None, None),
        P(("dp", "cache"), None, None, None),
    )
    out_specs = (
        P(("dp", "cache"), None, None, None),
        P(("dp", "cache"), None, None, None),
        P(("dp", "cache"), None, None, None),
    )
    return jax.shard_map(
        functools.partial(per_device, mesh.shape["dp"], mesh.shape["cache"]),
        mesh=mesh,
        in_specs=in_specs,
        out_specs=out_specs,
        check_vma=False,
    )
```

```python
import functools
import math

import jax
import jax.numpy as jnp
from jax import lax
from jax.experimental import pallas as pl
from jax.experimental.pallas import tpu as pltpu
from jax.sharding import PartitionSpec as P

STEP = 200

learn_rate = 0.02
beta_first = 0.9
beta_second = 0.999
epsilon = 1e-08

ROW_TILE = 512
LANES = 256
CHUNK = 32
MIB = 1024 * 1024


def flips(size):
    return list(range(size - 1, -1, -1))


def pack_kernel(columns, cache_ref, *refs):
    *outs, by_group = refs
    groups = cache_ref.shape[2]
    own = outs[0].shape[1]
    repeat = own * columns // groups
    for side in range(2):
        for group in range(groups):
            by_group[group, side] = cache_ref[:, side, group].astype(jnp.bfloat16)
    column = lax.axis_index("cache")
    for out, flip in zip(outs, flips(columns)):
        first = (column ^ flip) // repeat * own
        for slot in range(own):
            for side in range(2):
                out[side, slot] = by_group[first + slot, side]


def pack(cache, columns, own):
    share, _, groups, width = cache.shape
    slice_shape = jax.ShapeDtypeStruct((2, own, share, width), jnp.bfloat16)
    return pl.pallas_call(
        functools.partial(pack_kernel, columns),
        out_shape=[slice_shape] * columns,
        scratch_shapes=[pltpu.VMEM((groups, 2, share, width), jnp.bfloat16)],
        compiler_params=pltpu.CompilerParams(vmem_limit_bytes=16 * MIB),
        name="pack",
    )(cache)


def attend_kernel(score_scale, per_group, pieces, *refs):
    pair_refs, refs = refs[:pieces], refs[pieces:]
    queries_ref, grads_ref, lse_ref, dot_ref, mine_ref, mate_ref = refs[:6]
    keys, values, key_total, value_total = refs[6:10]
    even, odd = refs[10:14], refs[14:18]
    columns, _, own, share, width = pair_refs[0].shape
    length = columns * share
    positions = pieces * length
    tiles = queries_ref.shape[0]
    log2e = math.log2(math.e)
    factor = score_scale * log2e
    across = (((1,), (1,)), ((), ()))
    along = (((1,), (0,)), ((), ()))

    for piece, pair_ref in enumerate(pair_refs):
        at = pl.ds(piece * length, length)
        for slot in range(own):
            keys[slot, at] = pair_ref[:, 0, slot].reshape(length, width)
            values[slot, at] = pair_ref[:, 1, slot].reshape(length, width)
    key_total[...] = jnp.zeros_like(key_total)
    value_total[...] = jnp.zeros_like(value_total)

    def multiply(tile, buffers):
        scores, slopes, _, _ = buffers
        slot = tile // per_group
        scores[...] = lax.dot_general(
            keys[slot], queries_ref[tile], across, preferred_element_type=jnp.float32
        )
        slopes[...] = lax.dot_general(
            values[slot], grads_ref[tile], across, preferred_element_type=jnp.float32
        )

    def normalize(tile, buffers):
        scores, slopes, weights, dscores = buffers
        cuts = [pl.ds(start, CHUNK) for start in range(0, positions, CHUNK)]
        blocks = [pl.ds(start, LANES) for start in range(0, scores.shape[1], LANES)]

        def largest(top, cut, lanes):
            here = scores[cut, lanes]
            return here if top is None else jnp.maximum(top, here)

        top = None
        for cut in cuts:
            top = largest(top, cut, blocks[0])
        for number, lanes in enumerate(blocks):
            following = blocks[number + 1] if number + 1 < len(blocks) else None
            side_lse = lse_ref[tile, :, lanes] * log2e
            peak = jnp.maximum(jnp.max(top, axis=0, keepdims=True) * factor, side_lse)
            total = None
            dotted = None
            for cut in cuts:
                shifted = jnp.exp2(scores[cut, lanes] * factor - peak)
                product = shifted * slopes[cut, lanes]
                scores[cut, lanes] = shifted
                total = shifted if total is None else total + shifted
                dotted = product if dotted is None else dotted + product
            side = jnp.exp2(side_lse - peak)
            inverse = 1.0 / (jnp.sum(total, axis=0, keepdims=True) + side)
            delta = jnp.sum(dotted, axis=0, keepdims=True) + side * dot_ref[tile, :, lanes]
            delta = delta * inverse
            top = None
            for cut in cuts:
                if following is not None:
                    top = largest(top, cut, following)
                probability = scores[cut, lanes] * inverse
                weights[cut, lanes] = probability.astype(jnp.bfloat16)
                dscores[cut, lanes] = (probability * (slopes[cut, lanes] - delta)).astype(
                    jnp.bfloat16
                )

    def accumulate(tile, buffers):
        _, _, weights, dscores = buffers
        slot = tile // per_group
        key_total[slot] += lax.dot_general(
            dscores[...], queries_ref[tile], along, preferred_element_type=jnp.float32
        )
        value_total[slot] += lax.dot_general(
            weights[...], grads_ref[tile], along, preferred_element_type=jnp.float32
        )

    multiply(0, even)
    multiply(1, odd)
    normalize(0, even)

    def two_tiles(step, carry):
        tile = step * 2
        multiply(tile + 2, even)
        normalize(tile + 1, odd)
        accumulate(tile, even)
        multiply(tile + 3, odd)
        normalize(tile + 2, even)
        accumulate(tile + 1, odd)
        return carry

    lax.fori_loop(0, tiles // 2 - 1, two_tiles, 0)
    normalize(tiles - 1, odd)
    accumulate(tiles - 2, even)
    accumulate(tiles - 1, odd)

    half = positions // 2
    shape = mine_ref.shape[:2] + (share, width)
    for slot in range(own):
        key_sum = key_total[slot] * score_scale
        value_sum = value_total[slot]
        mine_ref[:, :, 0, slot] = key_sum[:half].reshape(shape)
        mine_ref[:, :, 1, slot] = value_sum[:half].reshape(shape)
        mate_ref[:, :, 0, slot] = key_sum[half:].astype(jnp.bfloat16).reshape(shape)
        mate_ref[:, :, 1, slot] = value_sum[half:].astype(jnp.bfloat16).reshape(shape)


def attend(pairs, queries, grads, lse_rows, dot_rows, score_scale):
    columns, _, own, share, width = pairs[0].shape
    pieces = len(pairs)
    positions = pieces * columns * share
    tiles, row_tile, _ = queries.shape
    rows = tiles * row_tile
    half = (pieces // 2, columns, 2, own, share, width)
    buffers = [
        pltpu.VMEM((positions, row_tile), jnp.float32),
        pltpu.VMEM((positions, row_tile), jnp.float32),
        pltpu.VMEM((positions, row_tile), jnp.bfloat16),
        pltpu.VMEM((positions, row_tile), jnp.bfloat16),
    ]
    return pl.pallas_call(
        functools.partial(attend_kernel, score_scale, tiles // own, pieces),
        out_shape=(
            jax.ShapeDtypeStruct(half, jnp.float32),
            jax.ShapeDtypeStruct(half, jnp.bfloat16),
        ),
        scratch_shapes=[
            pltpu.VMEM((own, positions, width), jnp.bfloat16),
            pltpu.VMEM((own, positions, width), jnp.bfloat16),
            pltpu.VMEM((own, positions, width), jnp.float32),
            pltpu.VMEM((own, positions, width), jnp.float32),
        ]
        + buffers
        + buffers,
        compiler_params=pltpu.CompilerParams(vmem_limit_bytes=44 * MIB),
        cost_estimate=pl.CostEstimate(
            flops=8 * rows * positions * width,
            bytes_accessed=4 * rows * width + 8 * own * positions * width,
            transcendentals=rows * positions,
        ),
        name="attend",
    )(*pairs, queries, grads, lse_rows, dot_rows)


def chip_sum_kernel(mine_ref, mate_ref, *outs):
    for offset, out in enumerate(outs):
        out[...] = (mine_ref[offset] + mate_ref[offset].astype(jnp.float32)).astype(out.dtype)


def chip_sum(mine, mate):
    chips = mine.shape[0]
    shape = mine.shape[1:]
    return pl.pallas_call(
        chip_sum_kernel,
        out_shape=[
            jax.ShapeDtypeStruct(shape, jnp.bfloat16 if flip else jnp.float32)
            for flip in flips(chips)
        ],
        compiler_params=pltpu.CompilerParams(vmem_limit_bytes=16 * MIB),
        name="chip_sum",
    )(mine, mate)


def column_sum_kernel(away, mine_ref, *refs):
    others, outs = refs[:away], refs[away:]
    for offset, out in enumerate(outs):
        total = mine_ref[offset]
        for other in others:
            total = total + other[offset].astype(jnp.float32)
        out[...] = total.astype(out.dtype)


def column_sum(mine, others):
    columns = mine.shape[0]
    shape = mine.shape[1:]
    return pl.pallas_call(
        functools.partial(column_sum_kernel, len(others)),
        out_shape=[
            jax.ShapeDtypeStruct(shape, jnp.bfloat16 if flip else jnp.float32)
            for flip in flips(columns)
        ],
        compiler_params=pltpu.CompilerParams(vmem_limit_bytes=16 * MIB),
        name="column_sum",
    )(mine, *others)


def adam_kernel(columns, *refs):
    parts, refs = refs[:columns], refs[columns:]
    cache_ref, first_ref, second_ref, new_cache, new_first, new_second, by_flip = refs
    groups = cache_ref.shape[2]
    own = parts[0].shape[1]
    repeat = own * columns // groups
    for part, flip in zip(parts, flips(columns)):
        by_flip[flip] = part[...].astype(jnp.float32)
    column = lax.axis_index("cache")
    for side in range(2):
        for group in range(groups):
            first_owner = group // own * repeat
            slot = group % own
            gradient = by_flip[column ^ first_owner, side, slot]
            for owner in range(first_owner + 1, first_owner + repeat):
                gradient = gradient + by_flip[column ^ owner, side, slot]
            first = beta_first * first_ref[:, side, group] + (1.0 - beta_first) * gradient
            second = (
                beta_second * second_ref[:, side, group]
                + (1.0 - beta_second) * gradient * gradient
            )
            first_hat = first / (1.0 - beta_first**STEP)
            second_hat = second / (1.0 - beta_second**STEP)
            new_cache[:, side, group] = cache_ref[
                :, side, group
            ] - learn_rate * first_hat / (jnp.sqrt(second_hat) + epsilon)
            new_first[:, side, group] = first
            new_second[:, side, group] = second


def adam(parts, cache, first_moment, second_moment):
    shape = jax.ShapeDtypeStruct(cache.shape, jnp.float32)
    return pl.pallas_call(
        functools.partial(adam_kernel, len(parts)),
        out_shape=(shape, shape, shape),
        scratch_shapes=[pltpu.VMEM((len(parts),) + parts[0].shape, jnp.float32)],
        compiler_params=pltpu.CompilerParams(vmem_limit_bytes=16 * MIB),
        name="adam",
    )(*parts, cache, first_moment, second_moment)


def swap(value, axis, size, flip):
    return lax.ppermute(value, axis, [(place, place ^ flip) for place in range(size)])


def swap_all(values, axis, size, stride):
    return [
        swap(value, axis, size, flip * stride) if flip else value
        for value, flip in zip(values, flips(len(values)))
    ]


def per_device(
    dp_size, columns, queries, out_grad, self_lse, self_dot, cache, first_moment, second_moment
):
    _, _, groups, width = cache.shape
    tokens, heads, _ = queries.shape
    chips = dp_size // 2
    group_size = heads // groups
    score_scale = 1.0 / math.sqrt(width)
    own = max(1, groups // columns)
    repeat = own * columns // groups
    own_tokens = tokens // repeat
    column = lax.axis_index("cache")
    first_group = column // repeat * own
    first_token = column % repeat * own_tokens

    slices = pack(cache, columns, own)
    gathered = jnp.stack(swap_all(slices, "cache", columns, 1))
    pairs = swap_all([gathered] * chips, "dp", dp_size, 2)
    pairs = pairs + [swap(pair, "dp", dp_size, 1) for pair in pairs]

    def tiles_of(array):
        parts = array.reshape((tokens, groups, group_size) + array.shape[2:])
        part = lax.dynamic_slice_in_dim(parts, first_token, own_tokens, 0)
        part = lax.dynamic_slice_in_dim(part, first_group, own, 1)
        return jnp.moveaxis(part, 1, 0).reshape((-1, ROW_TILE) + array.shape[2:])

    mine, mate = attend(
        pairs,
        tiles_of(queries),
        tiles_of(out_grad),
        tiles_of(self_lse)[:, None],
        tiles_of(self_dot)[:, None],
        score_scale,
    )
    by_chip = chip_sum(mine, swap(mate, "dp", dp_size, 1))
    *away, home = swap_all(by_chip, "dp", dp_size, 2)
    by_column = column_sum(home, away)
    parts = swap_all(by_column, "cache", columns, 1)
    return adam(parts, cache, first_moment, second_moment)


def solution(mesh):
    in_specs = (
        P("dp", None, None),
        P("dp", None, None),
        P("dp", None),
        P("dp", None),
        P(("dp", "cache"), None, None, None),
        P(("dp", "cache"), None, None, None),
        P(("dp", "cache"), None, None, None),
    )
    out_specs = (
        P(("dp", "cache"), None, None, None),
        P(("dp", "cache"), None, None, None),
        P(("dp", "cache"), None, None, None),
    )
    return jax.shard_map(
        functools.partial(per_device, mesh.shape["dp"], mesh.shape["cache"]),
        mesh=mesh,
        in_specs=in_specs,
        out_specs=out_specs,
        check_vma=False,
    )
```

```python
import functools
import math

import jax
import jax.numpy as jnp
from jax import lax
from jax.experimental import pallas as pl
from jax.experimental.pallas import tpu as pltpu
from jax.sharding import PartitionSpec as P

STEP = 200

learn_rate = 0.02
beta_first = 0.9
beta_second = 0.999
epsilon = 1e-08

ROW_TILE = 512
CHUNK = 16
MIB = 1024 * 1024


def flips(size):
    return list(range(size - 1, -1, -1))


def pack_kernel(columns, cache_ref, *refs):
    *outs, by_group = refs
    groups = cache_ref.shape[2]
    own = outs[0].shape[1]
    repeat = own * columns // groups
    for side in range(2):
        for group in range(groups):
            by_group[group, side] = cache_ref[:, side, group].astype(jnp.bfloat16)
    column = lax.axis_index("cache")
    for out, flip in zip(outs, flips(columns)):
        first = (column ^ flip) // repeat * own
        for slot in range(own):
            for side in range(2):
                out[side, slot] = by_group[first + slot, side]


def pack(cache, columns, own):
    share, _, groups, width = cache.shape
    slice_shape = jax.ShapeDtypeStruct((2, own, share, width), jnp.bfloat16)
    return pl.pallas_call(
        functools.partial(pack_kernel, columns),
        out_shape=[slice_shape] * columns,
        scratch_shapes=[pltpu.VMEM((groups, 2, share, width), jnp.bfloat16)],
        compiler_params=pltpu.CompilerParams(vmem_limit_bytes=16 * MIB),
        name="pack",
    )(cache)


def attend_kernel(score_scale, per_group, pieces, *refs):
    pair_refs, refs = refs[:pieces], refs[pieces:]
    queries_ref, grads_ref, lse_ref, dot_ref, mine_ref, mate_ref = refs[:6]
    keys, values, key_total, value_total = refs[6:10]
    even, odd = refs[10:14], refs[14:18]
    columns, _, own, share, width = pair_refs[0].shape
    length = columns * share
    positions = pieces * length
    tiles = queries_ref.shape[0]
    factor = score_scale
    across = (((1,), (1,)), ((), ()))
    along = (((1,), (0,)), ((), ()))

    for piece, pair_ref in enumerate(pair_refs):
        at = pl.ds(piece * length, length)
        for slot in range(own):
            keys[slot, at] = pair_ref[:, 0, slot].reshape(length, width)
            values[slot, at] = pair_ref[:, 1, slot].reshape(length, width)
    key_total[...] = jnp.zeros_like(key_total)
    value_total[...] = jnp.zeros_like(value_total)

    def multiply(tile, buffers):
        scores, slopes, _, _ = buffers
        slot = tile // per_group
        scores[...] = lax.dot_general(
            keys[slot], queries_ref[tile], across, preferred_element_type=jnp.float32
        )
        slopes[...] = lax.dot_general(
            values[slot], grads_ref[tile], across, preferred_element_type=jnp.float32
        )

    def normalize(tile, buffers):
        scores, slopes, weights, dscores = buffers
        cuts = [pl.ds(start, CHUNK) for start in range(0, positions, CHUNK)]
        top = scores[cuts[0]]
        for cut in cuts[1:]:
            top = jnp.maximum(top, scores[cut])
        side_lse = lse_ref[tile]
        peak = jnp.maximum(jnp.max(top, axis=0, keepdims=True) * factor, side_lse)
        total = None
        dotted = None
        for cut in cuts:
            shifted = jnp.exp(scores[cut] * factor - peak)
            product = shifted * slopes[cut]
            scores[cut] = shifted
            total = shifted if total is None else total + shifted
            dotted = product if dotted is None else dotted + product
        side = jnp.exp(side_lse - peak)
        inverse = 1.0 / (jnp.sum(total, axis=0, keepdims=True) + side)
        delta = (jnp.sum(dotted, axis=0, keepdims=True) + side * dot_ref[tile]) * inverse
        for cut in cuts:
            probability = scores[cut] * inverse
            weights[cut] = probability.astype(jnp.bfloat16)
            dscores[cut] = (probability * (slopes[cut] - delta)).astype(jnp.bfloat16)

    def accumulate(tile, buffers):
        _, _, weights, dscores = buffers
        slot = tile // per_group
        key_total[slot] += lax.dot_general(
            dscores[...], queries_ref[tile], along, preferred_element_type=jnp.float32
        )
        value_total[slot] += lax.dot_general(
            weights[...], grads_ref[tile], along, preferred_element_type=jnp.float32
        )

    multiply(0, even)
    multiply(1, odd)
    normalize(0, even)

    def two_tiles(step, carry):
        tile = step * 2
        multiply(tile + 2, even)
        normalize(tile + 1, odd)
        accumulate(tile, even)
        multiply(tile + 3, odd)
        normalize(tile + 2, even)
        accumulate(tile + 1, odd)
        return carry

    lax.fori_loop(0, tiles // 2 - 1, two_tiles, 0)
    normalize(tiles - 1, odd)
    accumulate(tiles - 2, even)
    accumulate(tiles - 1, odd)

    half = positions // 2
    shape = mine_ref.shape[:2] + (share, width)
    for slot in range(own):
        key_sum = key_total[slot] * score_scale
        value_sum = value_total[slot]
        mine_ref[:, :, 0, slot] = key_sum[:half].reshape(shape)
        mine_ref[:, :, 1, slot] = value_sum[:half].reshape(shape)
        mate_ref[:, :, 0, slot] = key_sum[half:].astype(jnp.bfloat16).reshape(shape)
        mate_ref[:, :, 1, slot] = value_sum[half:].astype(jnp.bfloat16).reshape(shape)


def attend(pairs, queries, grads, lse_rows, dot_rows, score_scale):
    columns, _, own, share, width = pairs[0].shape
    pieces = len(pairs)
    positions = pieces * columns * share
    tiles, row_tile, _ = queries.shape
    rows = tiles * row_tile
    half = (pieces // 2, columns, 2, own, share, width)
    buffers = [
        pltpu.VMEM((positions, row_tile), jnp.float32),
        pltpu.VMEM((positions, row_tile), jnp.float32),
        pltpu.VMEM((positions, row_tile), jnp.bfloat16),
        pltpu.VMEM((positions, row_tile), jnp.bfloat16),
    ]
    return pl.pallas_call(
        functools.partial(attend_kernel, score_scale, tiles // own, pieces),
        out_shape=(
            jax.ShapeDtypeStruct(half, jnp.float32),
            jax.ShapeDtypeStruct(half, jnp.bfloat16),
        ),
        scratch_shapes=[
            pltpu.VMEM((own, positions, width), jnp.bfloat16),
            pltpu.VMEM((own, positions, width), jnp.bfloat16),
            pltpu.VMEM((own, positions, width), jnp.float32),
            pltpu.VMEM((own, positions, width), jnp.float32),
        ]
        + buffers
        + buffers,
        compiler_params=pltpu.CompilerParams(vmem_limit_bytes=44 * MIB),
        cost_estimate=pl.CostEstimate(
            flops=8 * rows * positions * width,
            bytes_accessed=4 * rows * width + 8 * own * positions * width,
            transcendentals=rows * positions,
        ),
        name="attend",
    )(*pairs, queries, grads, lse_rows, dot_rows)


def chip_sum_kernel(mine_ref, mate_ref, *outs):
    for offset, out in enumerate(outs):
        out[...] = (mine_ref[offset] + mate_ref[offset].astype(jnp.float32)).astype(out.dtype)


def chip_sum(mine, mate):
    chips = mine.shape[0]
    shape = mine.shape[1:]
    return pl.pallas_call(
        chip_sum_kernel,
        out_shape=[
            jax.ShapeDtypeStruct(shape, jnp.bfloat16 if flip else jnp.float32)
            for flip in flips(chips)
        ],
        compiler_params=pltpu.CompilerParams(vmem_limit_bytes=16 * MIB),
        name="chip_sum",
    )(mine, mate)


def column_sum_kernel(away, mine_ref, *refs):
    others, outs = refs[:away], refs[away:]
    for offset, out in enumerate(outs):
        total = mine_ref[offset]
        for other in others:
            total = total + other[offset].astype(jnp.float32)
        out[...] = total.astype(out.dtype)


def column_sum(mine, others):
    columns = mine.shape[0]
    shape = mine.shape[1:]
    return pl.pallas_call(
        functools.partial(column_sum_kernel, len(others)),
        out_shape=[
            jax.ShapeDtypeStruct(shape, jnp.bfloat16 if flip else jnp.float32)
            for flip in flips(columns)
        ],
        compiler_params=pltpu.CompilerParams(vmem_limit_bytes=16 * MIB),
        name="column_sum",
    )(mine, *others)


def adam_kernel(columns, *refs):
    parts, refs = refs[:columns], refs[columns:]
    cache_ref, first_ref, second_ref, new_cache, new_first, new_second, by_flip = refs
    groups = cache_ref.shape[2]
    own = parts[0].shape[1]
    repeat = own * columns // groups
    for part, flip in zip(parts, flips(columns)):
        by_flip[flip] = part[...].astype(jnp.float32)
    column = lax.axis_index("cache")
    for side in range(2):
        for group in range(groups):
            first_owner = group // own * repeat
            slot = group % own
            gradient = by_flip[column ^ first_owner, side, slot]
            for owner in range(first_owner + 1, first_owner + repeat):
                gradient = gradient + by_flip[column ^ owner, side, slot]
            first = beta_first * first_ref[:, side, group] + (1.0 - beta_first) * gradient
            second = (
                beta_second * second_ref[:, side, group]
                + (1.0 - beta_second) * gradient * gradient
            )
            first_hat = first / (1.0 - beta_first**STEP)
            second_hat = second / (1.0 - beta_second**STEP)
            new_cache[:, side, group] = cache_ref[
                :, side, group
            ] - learn_rate * first_hat / (jnp.sqrt(second_hat) + epsilon)
            new_first[:, side, group] = first
            new_second[:, side, group] = second


def adam(parts, cache, first_moment, second_moment):
    shape = jax.ShapeDtypeStruct(cache.shape, jnp.float32)
    return pl.pallas_call(
        functools.partial(adam_kernel, len(parts)),
        out_shape=(shape, shape, shape),
        scratch_shapes=[pltpu.VMEM((len(parts),) + parts[0].shape, jnp.float32)],
        compiler_params=pltpu.CompilerParams(vmem_limit_bytes=16 * MIB),
        name="adam",
    )(*parts, cache, first_moment, second_moment)


def swap(value, axis, size, flip):
    return lax.ppermute(value, axis, [(place, place ^ flip) for place in range(size)])


def swap_all(values, axis, size, stride):
    return [
        swap(value, axis, size, flip * stride) if flip else value
        for value, flip in zip(values, flips(len(values)))
    ]


def per_device(
    dp_size, columns, queries, out_grad, self_lse, self_dot, cache, first_moment, second_moment
):
    _, _, groups, width = cache.shape
    tokens, heads, _ = queries.shape
    chips = dp_size // 2
    group_size = heads // groups
    score_scale = 1.0 / math.sqrt(width)
    own = max(1, groups // columns)
    repeat = own * columns // groups
    own_tokens = tokens // repeat
    column = lax.axis_index("cache")
    first_group = column // repeat * own
    first_token = column % repeat * own_tokens

    slices = pack(cache, columns, own)
    gathered = jnp.stack(swap_all(slices, "cache", columns, 1))
    pairs = swap_all([gathered] * chips, "dp", dp_size, 2)
    pairs = pairs + [swap(pair, "dp", dp_size, 1) for pair in pairs]

    def tiles_of(array):
        parts = array.reshape((tokens, groups, group_size) + array.shape[2:])
        part = lax.dynamic_slice_in_dim(parts, first_token, own_tokens, 0)
        part = lax.dynamic_slice_in_dim(part, first_group, own, 1)
        return jnp.moveaxis(part, 1, 0).reshape((-1, ROW_TILE) + array.shape[2:])

    mine, mate = attend(
        pairs,
        tiles_of(queries),
        tiles_of(out_grad),
        tiles_of(self_lse)[:, None],
        tiles_of(self_dot)[:, None],
        score_scale,
    )
    by_chip = chip_sum(mine, swap(mate, "dp", dp_size, 1))
    *away, home = swap_all(by_chip, "dp", dp_size, 2)
    by_column = column_sum(home, away)
    parts = swap_all(by_column, "cache", columns, 1)
    return adam(parts, cache, first_moment, second_moment)


def solution(mesh):
    in_specs = (
        P("dp", None, None),
        P("dp", None, None),
        P("dp", None),
        P("dp", None),
        P(("dp", "cache"), None, None, None),
        P(("dp", "cache"), None, None, None),
        P(("dp", "cache"), None, None, None),
    )
    out_specs = (
        P(("dp", "cache"), None, None, None),
        P(("dp", "cache"), None, None, None),
        P(("dp", "cache"), None, None, None),
    )
    return jax.shard_map(
        functools.partial(per_device, mesh.shape["dp"], mesh.shape["cache"]),
        mesh=mesh,
        in_specs=in_specs,
        out_specs=out_specs,
        check_vma=False,
    )
```

```python
import functools
import math

import jax
import jax.numpy as jnp
from jax import lax
from jax.experimental import pallas as pl
from jax.experimental.pallas import tpu as pltpu
from jax.sharding import PartitionSpec as P

STEP = 200

learn_rate = 0.02
beta_first = 0.9
beta_second = 0.999
epsilon = 1e-08

ROW_TILE = 512
CHUNK = 16
MIB = 1024 * 1024


def flips(size):
    return list(range(size - 1, -1, -1))


def pack_kernel(columns, cache_ref, *refs):
    *outs, by_group = refs
    groups = cache_ref.shape[2]
    own = outs[0].shape[1]
    repeat = own * columns // groups
    for side in range(2):
        for group in range(groups):
            by_group[group, side] = cache_ref[:, side, group].astype(jnp.bfloat16)
    column = lax.axis_index("cache")
    for out, flip in zip(outs, flips(columns)):
        first = (column ^ flip) // repeat * own
        for slot in range(own):
            for side in range(2):
                out[side, slot] = by_group[first + slot, side]


def pack(cache, columns, own):
    share, _, groups, width = cache.shape
    slice_shape = jax.ShapeDtypeStruct((2, own, share, width), jnp.bfloat16)
    return pl.pallas_call(
        functools.partial(pack_kernel, columns),
        out_shape=[slice_shape] * columns,
        scratch_shapes=[pltpu.VMEM((groups, 2, share, width), jnp.bfloat16)],
        compiler_params=pltpu.CompilerParams(vmem_limit_bytes=16 * MIB),
        name="pack",
    )(cache)


LOG2E = math.log2(math.e)
ACROSS = (((1,), (1,)), ((), ()))
ALONG = (((1,), (0,)), ((), ()))


def load_pairs(pair_refs, keys, values):
    columns, _, own, share, width = pair_refs[0].shape
    length = columns * share
    for piece, pair_ref in enumerate(pair_refs):
        at = pl.ds(piece * length, length)
        for slot in range(own):
            keys[slot, at] = pair_ref[:, 0, slot].reshape(length, width)
            values[slot, at] = pair_ref[:, 1, slot].reshape(length, width)


def multiply(keys, values, queries, grads, scores, slopes):
    scores[...] = lax.dot_general(keys, queries, ACROSS, preferred_element_type=jnp.float32)
    slopes[...] = lax.dot_general(values, grads, ACROSS, preferred_element_type=jnp.float32)


def cuts_of(ref):
    return [pl.ds(start, CHUNK) for start in range(0, ref.shape[0], CHUNK)]


def largest(scores):
    cuts = cuts_of(scores)
    top = scores[cuts[0]]
    for cut in cuts[1:]:
        top = jnp.maximum(top, scores[cut])
    return jnp.max(top, axis=0, keepdims=True)


def exponentiate(scores, slopes, factor, peak):
    total = None
    dotted = None
    for cut in cuts_of(scores):
        shifted = jnp.exp2(scores[cut] * factor - peak)
        product = shifted * slopes[cut]
        scores[cut] = shifted
        total = shifted if total is None else total + shifted
        dotted = product if dotted is None else dotted + product
    return jnp.sum(total, axis=0, keepdims=True), jnp.sum(dotted, axis=0, keepdims=True)


def weigh(shifted, slopes, inverse, delta, weights, dscores):
    for cut in cuts_of(weights):
        probability = shifted[cut] * inverse
        weights[cut] = probability.astype(jnp.bfloat16)
        dscores[cut] = (probability * (slopes[cut] - delta)).astype(jnp.bfloat16)


def accumulate(key_total, value_total, slot, weights, dscores, queries, grads):
    key_total[slot] += lax.dot_general(
        dscores[...], queries, ALONG, preferred_element_type=jnp.float32
    )
    value_total[slot] += lax.dot_general(
        weights[...], grads, ALONG, preferred_element_type=jnp.float32
    )


def first_half_kernel(score_scale, per_group, pieces, *refs):
    pair_refs, refs = refs[:pieces], refs[pieces:]
    queries_ref, grads_ref, lse_ref, dot_ref = refs[:4]
    kept, (peak_ref, total_ref, dotted_ref, keys, values) = refs[4:8], refs[8:]
    tiles = queries_ref.shape[0]
    factor = score_scale * LOG2E
    load_pairs(pair_refs, keys, values)

    def place(tile, parity, step):
        return kept[2 * parity].at[step], kept[2 * parity + 1].at[step]

    def products(tile, parity, step):
        slot = tile // per_group
        multiply(
            keys[slot], values[slot], queries_ref[tile], grads_ref[tile], *place(tile, parity, step)
        )

    def normalize(tile, parity, step):
        scores, slopes = place(tile, parity, step)
        side_lse = lse_ref[pl.ds(tile, 1)] * LOG2E
        peak = jnp.maximum(largest(scores) * factor, side_lse)
        total, dotted = exponentiate(scores, slopes, factor, peak)
        side = jnp.exp2(side_lse - peak)
        peak_ref[tile] = peak
        total_ref[tile] = total + side
        dotted_ref[tile] = dotted + side * dot_ref[pl.ds(tile, 1)]

    products(0, 0, 0)

    def two_tiles(step, carry):
        products(2 * step + 1, 1, step)
        normalize(2 * step, 0, step)
        products(2 * step + 2, 0, step + 1)
        normalize(2 * step + 1, 1, step)
        return carry

    last = tiles // 2 - 1
    lax.fori_loop(0, last, two_tiles, 0)
    products(tiles - 1, 1, last)
    normalize(tiles - 2, 0, last)
    normalize(tiles - 1, 1, last)


def first_half(pairs, queries, grads, lse_rows, dot_rows, score_scale):
    columns, _, own, share, width = pairs[0].shape
    positions = len(pairs) * columns * share
    tiles, row_tile, _ = queries.shape
    kept = jax.ShapeDtypeStruct((tiles // 2, positions, row_tile), jnp.float32)
    stat = jax.ShapeDtypeStruct((tiles, 1, row_tile), jnp.float32)
    return pl.pallas_call(
        functools.partial(first_half_kernel, score_scale, tiles // own, len(pairs)),
        out_shape=[kept] * 4 + [stat] * 3,
        scratch_shapes=[
            pltpu.VMEM((own, positions, width), jnp.bfloat16),
            pltpu.VMEM((own, positions, width), jnp.bfloat16),
        ],
        compiler_params=pltpu.CompilerParams(vmem_limit_bytes=30 * MIB),
        cost_estimate=pl.CostEstimate(
            flops=4 * tiles * row_tile * positions * width,
            bytes_accessed=8 * tiles * row_tile * positions,
            transcendentals=tiles * row_tile * positions,
        ),
        name="first_half",
    )(*pairs, queries, grads, lse_rows, dot_rows)


def second_half_kernel(score_scale, per_group, pieces, *refs):
    pair_refs, refs = refs[:pieces], refs[pieces:]
    queries_ref, grads_ref, peak_ref, total_ref, dotted_ref = refs[:5]
    out_ref, inverse_ref, delta_ref = refs[5:8]
    keys, values, key_total, value_total = refs[8:12]
    even, odd = refs[12:16], refs[16:20]
    _, columns, _, own, share, width = out_ref.shape
    tiles = queries_ref.shape[0]
    factor = score_scale * LOG2E
    load_pairs(pair_refs, keys, values)
    key_total[...] = jnp.zeros_like(key_total)
    value_total[...] = jnp.zeros_like(value_total)

    def products(tile, buffers):
        slot = tile // per_group
        multiply(keys[slot], values[slot], queries_ref[tile], grads_ref[tile], *buffers[:2])

    def normalize(tile, buffers):
        scores, slopes, weights, dscores = buffers
        first_peak = peak_ref[tile]
        peak = jnp.maximum(largest(scores) * factor, first_peak)
        total, dotted = exponentiate(scores, slopes, factor, peak)
        rescale = jnp.exp2(first_peak - peak)
        inverse = 1.0 / (total + total_ref[tile] * rescale)
        delta = (dotted + dotted_ref[tile] * rescale) * inverse
        inverse_ref[tile] = inverse * rescale
        delta_ref[tile] = delta
        weigh(scores, slopes, inverse, delta, weights, dscores)

    def gather(tile, buffers):
        accumulate(
            key_total,
            value_total,
            tile // per_group,
            buffers[2],
            buffers[3],
            queries_ref[tile],
            grads_ref[tile],
        )

    products(0, even)
    products(1, odd)
    normalize(0, even)

    def two_tiles(step, carry):
        tile = step * 2
        products(tile + 2, even)
        normalize(tile + 1, odd)
        gather(tile, even)
        products(tile + 3, odd)
        normalize(tile + 2, even)
        gather(tile + 1, odd)
        return carry

    lax.fori_loop(0, tiles // 2 - 1, two_tiles, 0)
    normalize(tiles - 1, odd)
    gather(tiles - 2, even)
    gather(tiles - 1, odd)
    shape = out_ref.shape[:2] + (share, width)
    for slot in range(own):
        key_sum = key_total[slot] * score_scale
        out_ref[:, :, 0, slot] = key_sum.astype(jnp.bfloat16).reshape(shape)
        out_ref[:, :, 1, slot] = value_total[slot].astype(jnp.bfloat16).reshape(shape)


def second_half(pairs, queries, grads, stats, score_scale):
    columns, _, own, share, width = pairs[0].shape
    positions = len(pairs) * columns * share
    tiles, row_tile, _ = queries.shape
    stat = jax.ShapeDtypeStruct((tiles, 1, row_tile), jnp.float32)
    buffers = [
        pltpu.VMEM((positions, row_tile), jnp.float32),
        pltpu.VMEM((positions, row_tile), jnp.float32),
        pltpu.VMEM((positions, row_tile), jnp.bfloat16),
        pltpu.VMEM((positions, row_tile), jnp.bfloat16),
    ]
    return pl.pallas_call(
        functools.partial(second_half_kernel, score_scale, tiles // own, len(pairs)),
        out_shape=(
            jax.ShapeDtypeStruct((len(pairs),) + pairs[0].shape, jnp.bfloat16),
            stat,
            stat,
        ),
        scratch_shapes=[
            pltpu.VMEM((own, positions, width), jnp.bfloat16),
            pltpu.VMEM((own, positions, width), jnp.bfloat16),
            pltpu.VMEM((own, positions, width), jnp.float32),
            pltpu.VMEM((own, positions, width), jnp.float32),
        ]
        + buffers
        + buffers,
        compiler_params=pltpu.CompilerParams(vmem_limit_bytes=30 * MIB),
        cost_estimate=pl.CostEstimate(
            flops=8 * tiles * row_tile * positions * width,
            bytes_accessed=4 * tiles * row_tile * width,
            transcendentals=tiles * row_tile * positions,
        ),
        name="second_half",
    )(*pairs, queries, grads, *stats)


def finish_kernel(score_scale, per_group, *refs):
    kept, refs = refs[:4], refs[4:]
    queries_ref, grads_ref, inverse_ref, delta_ref, out_ref = refs[:5]
    key_total, value_total = refs[5:7]
    even, odd = refs[7:9], refs[9:11]
    _, columns, _, own, share, width = out_ref.shape
    tiles = queries_ref.shape[0]
    key_total[...] = jnp.zeros_like(key_total)
    value_total[...] = jnp.zeros_like(value_total)

    def spread(tile, parity, step, buffers):
        weigh(
            kept[2 * parity].at[step],
            kept[2 * parity + 1].at[step],
            inverse_ref[tile],
            delta_ref[tile],
            *buffers,
        )

    def gather(tile, buffers):
        accumulate(
            key_total,
            value_total,
            tile // per_group,
            *buffers,
            queries_ref[tile],
            grads_ref[tile],
        )

    spread(0, 0, 0, even)

    def two_tiles(step, carry):
        spread(2 * step + 1, 1, step, odd)
        gather(2 * step, even)
        spread(2 * step + 2, 0, step + 1, even)
        gather(2 * step + 1, odd)
        return carry

    last = tiles // 2 - 1
    lax.fori_loop(0, last, two_tiles, 0)
    spread(tiles - 1, 1, last, odd)
    gather(tiles - 2, even)
    gather(tiles - 1, odd)
    shape = out_ref.shape[:2] + (share, width)
    for slot in range(own):
        out_ref[:, :, 0, slot] = (key_total[slot] * score_scale).reshape(shape)
        out_ref[:, :, 1, slot] = value_total[slot].reshape(shape)


def finish(kept, queries, grads, inverse, delta, shape, score_scale):
    _, positions, row_tile = kept[0].shape
    own, width = shape[3], shape[5]
    tiles = queries.shape[0]
    buffers = [pltpu.VMEM((positions, row_tile), jnp.bfloat16)] * 4
    return pl.pallas_call(
        functools.partial(finish_kernel, score_scale, tiles // own),
        out_shape=jax.ShapeDtypeStruct(shape, jnp.float32),
        scratch_shapes=[
            pltpu.VMEM((own, positions, width), jnp.float32),
            pltpu.VMEM((own, positions, width), jnp.float32),
        ]
        + buffers,
        compiler_params=pltpu.CompilerParams(vmem_limit_bytes=30 * MIB),
        cost_estimate=pl.CostEstimate(
            flops=4 * tiles * row_tile * positions * width,
            bytes_accessed=8 * tiles * row_tile * positions,
            transcendentals=0,
        ),
        name="finish",
    )(*kept, queries, grads, inverse, delta)


def chip_sum_kernel(mine_ref, mate_ref, *outs):
    for offset, out in enumerate(outs):
        out[...] = (mine_ref[offset] + mate_ref[offset].astype(jnp.float32)).astype(out.dtype)


def chip_sum(mine, mate):
    chips = mine.shape[0]
    shape = mine.shape[1:]
    return pl.pallas_call(
        chip_sum_kernel,
        out_shape=[
            jax.ShapeDtypeStruct(shape, jnp.bfloat16 if flip else jnp.float32)
            for flip in flips(chips)
        ],
        compiler_params=pltpu.CompilerParams(vmem_limit_bytes=16 * MIB),
        name="chip_sum",
    )(mine, mate)


def column_sum_kernel(away, mine_ref, *refs):
    others, outs = refs[:away], refs[away:]
    for offset, out in enumerate(outs):
        total = mine_ref[offset]
        for other in others:
            total = total + other[offset].astype(jnp.float32)
        out[...] = total.astype(out.dtype)


def column_sum(mine, others):
    columns = mine.shape[0]
    shape = mine.shape[1:]
    return pl.pallas_call(
        functools.partial(column_sum_kernel, len(others)),
        out_shape=[
            jax.ShapeDtypeStruct(shape, jnp.bfloat16 if flip else jnp.float32)
            for flip in flips(columns)
        ],
        compiler_params=pltpu.CompilerParams(vmem_limit_bytes=16 * MIB),
        name="column_sum",
    )(mine, *others)


def adam_kernel(columns, *refs):
    parts, refs = refs[:columns], refs[columns:]
    cache_ref, first_ref, second_ref, new_cache, new_first, new_second, by_flip = refs
    groups = cache_ref.shape[2]
    own = parts[0].shape[1]
    repeat = own * columns // groups
    for part, flip in zip(parts, flips(columns)):
        by_flip[flip] = part[...].astype(jnp.float32)
    column = lax.axis_index("cache")
    for side in range(2):
        for group in range(groups):
            first_owner = group // own * repeat
            slot = group % own
            gradient = by_flip[column ^ first_owner, side, slot]
            for owner in range(first_owner + 1, first_owner + repeat):
                gradient = gradient + by_flip[column ^ owner, side, slot]
            first = beta_first * first_ref[:, side, group] + (1.0 - beta_first) * gradient
            second = (
                beta_second * second_ref[:, side, group]
                + (1.0 - beta_second) * gradient * gradient
            )
            first_hat = first / (1.0 - beta_first**STEP)
            second_hat = second / (1.0 - beta_second**STEP)
            new_cache[:, side, group] = cache_ref[
                :, side, group
            ] - learn_rate * first_hat / (jnp.sqrt(second_hat) + epsilon)
            new_first[:, side, group] = first
            new_second[:, side, group] = second


def adam(parts, cache, first_moment, second_moment):
    shape = jax.ShapeDtypeStruct(cache.shape, jnp.float32)
    return pl.pallas_call(
        functools.partial(adam_kernel, len(parts)),
        out_shape=(shape, shape, shape),
        scratch_shapes=[pltpu.VMEM((len(parts),) + parts[0].shape, jnp.float32)],
        compiler_params=pltpu.CompilerParams(vmem_limit_bytes=16 * MIB),
        name="adam",
    )(*parts, cache, first_moment, second_moment)


def swap(value, axis, size, flip):
    return lax.ppermute(value, axis, [(place, place ^ flip) for place in range(size)])


def swap_all(values, axis, size, stride):
    return [
        swap(value, axis, size, flip * stride) if flip else value
        for value, flip in zip(values, flips(len(values)))
    ]


def per_device(
    dp_size, columns, queries, out_grad, self_lse, self_dot, cache, first_moment, second_moment
):
    _, _, groups, width = cache.shape
    tokens, heads, _ = queries.shape
    chips = dp_size // 2
    group_size = heads // groups
    score_scale = 1.0 / math.sqrt(width)
    own = max(1, groups // columns)
    repeat = own * columns // groups
    own_tokens = tokens // repeat
    column = lax.axis_index("cache")
    first_group = column // repeat * own
    first_token = column % repeat * own_tokens

    slices = pack(cache, columns, own)
    gathered = jnp.stack(swap_all(slices, "cache", columns, 1))
    pairs = swap_all([gathered] * chips, "dp", dp_size, 2)
    def tiles_of(array):
        parts = array.reshape((tokens, groups, group_size) + array.shape[2:])
        part = lax.dynamic_slice_in_dim(parts, first_token, own_tokens, 0)
        part = lax.dynamic_slice_in_dim(part, first_group, own, 1)
        return jnp.moveaxis(part, 1, 0).reshape((-1, ROW_TILE) + array.shape[2:])

    tiles = [tiles_of(queries), tiles_of(out_grad)]
    tiles += [tiles_of(self_lse), tiles_of(self_dot)]
    own_pair, tiles = lax.optimization_barrier((pairs[-1], tiles))
    query_tiles, grad_tiles, lse_rows, dot_rows = tiles
    mate_pairs = [swap(pair, "dp", dp_size, 1) for pair in pairs[:-1] + [own_pair]]
    *kept, peak, total, dotted = first_half(
        pairs, query_tiles, grad_tiles, lse_rows, dot_rows, score_scale
    )
    mate, inverse, delta = second_half(
        mate_pairs, query_tiles, grad_tiles, (peak, total, dotted), score_scale
    )
    from_mate = swap(mate, "dp", dp_size, 1)
    mine = finish(kept, query_tiles, grad_tiles, inverse, delta, mate.shape, score_scale)
    by_chip = chip_sum(mine, from_mate)
    *away, home = swap_all(by_chip, "dp", dp_size, 2)
    by_column = column_sum(home, away)
    parts = swap_all(by_column, "cache", columns, 1)
    return adam(parts, cache, first_moment, second_moment)


def solution(mesh):
    in_specs = (
        P("dp", None, None),
        P("dp", None, None),
        P("dp", None),
        P("dp", None),
        P(("dp", "cache"), None, None, None),
        P(("dp", "cache"), None, None, None),
        P(("dp", "cache"), None, None, None),
    )
    out_specs = (
        P(("dp", "cache"), None, None, None),
        P(("dp", "cache"), None, None, None),
        P(("dp", "cache"), None, None, None),
    )
    return jax.shard_map(
        functools.partial(per_device, mesh.shape["dp"], mesh.shape["cache"]),
        mesh=mesh,
        in_specs=in_specs,
        out_specs=out_specs,
        check_vma=False,
    )
```

```python
import functools
import math

import jax
import jax.numpy as jnp
from jax import lax
from jax.experimental import pallas as pl
from jax.experimental.pallas import tpu as pltpu
from jax.sharding import PartitionSpec as P

STEP = 200

learn_rate = 0.02
beta_first = 0.9
beta_second = 0.999
epsilon = 1e-08

ROW_TILE = 512
CHUNK = 16
MIB = 1024 * 1024


def flips(size):
    return list(range(size - 1, -1, -1))


def pack_kernel(columns, cache_ref, *refs):
    *outs, by_group = refs
    groups = cache_ref.shape[2]
    own = outs[0].shape[1]
    repeat = own * columns // groups
    for side in range(2):
        for group in range(groups):
            by_group[group, side] = cache_ref[:, side, group].astype(jnp.bfloat16)
    column = lax.axis_index("cache")
    for out, flip in zip(outs, flips(columns)):
        first = (column ^ flip) // repeat * own
        for slot in range(own):
            for side in range(2):
                out[side, slot] = by_group[first + slot, side]


def pack(cache, columns, own):
    share, _, groups, width = cache.shape
    slice_shape = jax.ShapeDtypeStruct((2, own, share, width), jnp.bfloat16)
    return pl.pallas_call(
        functools.partial(pack_kernel, columns),
        out_shape=[slice_shape] * columns,
        scratch_shapes=[pltpu.VMEM((groups, 2, share, width), jnp.bfloat16)],
        compiler_params=pltpu.CompilerParams(vmem_limit_bytes=16 * MIB),
        name="pack",
    )(cache)


LOG2E = math.log2(math.e)
ACROSS = (((1,), (1,)), ((), ()))
ALONG = (((1,), (0,)), ((), ()))


def load_pairs(pair_refs, keys, values):
    columns, _, own, share, width = pair_refs[0].shape
    length = columns * share
    for piece, pair_ref in enumerate(pair_refs):
        at = pl.ds(piece * length, length)
        for slot in range(own):
            keys[slot, at] = pair_ref[:, 0, slot].reshape(length, width)
            values[slot, at] = pair_ref[:, 1, slot].reshape(length, width)


def multiply(keys, values, queries, grads, scores, slopes):
    scores[...] = lax.dot_general(keys, queries, ACROSS, preferred_element_type=jnp.float32)
    slopes[...] = lax.dot_general(values, grads, ACROSS, preferred_element_type=jnp.float32)


def cuts_of(ref):
    return [pl.ds(start, CHUNK) for start in range(0, ref.shape[0], CHUNK)]


def largest(scores):
    cuts = cuts_of(scores)
    top = scores[cuts[0]]
    for cut in cuts[1:]:
        top = jnp.maximum(top, scores[cut])
    return jnp.max(top, axis=0, keepdims=True)


def exponentiate(scores, slopes, factor, peak):
    total = None
    dotted = None
    for cut in cuts_of(scores):
        shifted = jnp.exp2(scores[cut] * factor - peak)
        product = shifted * slopes[cut]
        scores[cut] = shifted
        total = shifted if total is None else total + shifted
        dotted = product if dotted is None else dotted + product
    return jnp.sum(total, axis=0, keepdims=True), jnp.sum(dotted, axis=0, keepdims=True)


def weigh(shifted, slopes, inverse, delta, weights, dscores):
    for cut in cuts_of(weights):
        probability = shifted[cut] * inverse
        weights[cut] = probability.astype(jnp.bfloat16)
        dscores[cut] = (probability * (slopes[cut] - delta)).astype(jnp.bfloat16)


def accumulate(key_total, value_total, slot, weights, dscores, queries, grads):
    key_total[slot] += lax.dot_general(
        dscores[...], queries, ALONG, preferred_element_type=jnp.float32
    )
    value_total[slot] += lax.dot_general(
        weights[...], grads, ALONG, preferred_element_type=jnp.float32
    )


def first_half_kernel(score_scale, per_group, pieces, *refs):
    pair_refs, refs = refs[:pieces][::-1], refs[pieces:]
    queries_ref, grads_ref, lse_ref, dot_ref = refs[:4]
    kept, (peak_ref, total_ref, dotted_ref, keys, values) = refs[4:8], refs[8:]
    tiles = queries_ref.shape[0]
    factor = score_scale * LOG2E
    load_pairs(pair_refs, keys, values)

    def place(tile, parity, step):
        return kept[2 * parity].at[step], kept[2 * parity + 1].at[step]

    def products(tile, parity, step):
        slot = tile // per_group
        multiply(
            keys[slot], values[slot], queries_ref[tile], grads_ref[tile], *place(tile, parity, step)
        )

    def normalize(tile, parity, step):
        scores, slopes = place(tile, parity, step)
        side_lse = lse_ref[pl.ds(tile, 1)] * LOG2E
        peak = jnp.maximum(largest(scores) * factor, side_lse)
        total, dotted = exponentiate(scores, slopes, factor, peak)
        side = jnp.exp2(side_lse - peak)
        peak_ref[tile] = peak
        total_ref[tile] = total + side
        dotted_ref[tile] = dotted + side * dot_ref[pl.ds(tile, 1)]

    products(0, 0, 0)

    def two_tiles(step, carry):
        products(2 * step + 1, 1, step)
        normalize(2 * step, 0, step)
        products(2 * step + 2, 0, step + 1)
        normalize(2 * step + 1, 1, step)
        return carry

    last = tiles // 2 - 1
    lax.fori_loop(0, last, two_tiles, 0)
    products(tiles - 1, 1, last)
    normalize(tiles - 2, 0, last)
    normalize(tiles - 1, 1, last)


def first_half(pairs, queries, grads, lse_rows, dot_rows, score_scale):
    columns, _, own, share, width = pairs[0].shape
    positions = len(pairs) * columns * share
    tiles, row_tile, _ = queries.shape
    kept = jax.ShapeDtypeStruct((tiles // 2, positions, row_tile), jnp.float32)
    stat = jax.ShapeDtypeStruct((tiles, 1, row_tile), jnp.float32)
    return pl.pallas_call(
        functools.partial(first_half_kernel, score_scale, tiles // own, len(pairs)),
        out_shape=[kept] * 4 + [stat] * 3,
        scratch_shapes=[
            pltpu.VMEM((own, positions, width), jnp.bfloat16),
            pltpu.VMEM((own, positions, width), jnp.bfloat16),
        ],
        compiler_params=pltpu.CompilerParams(vmem_limit_bytes=30 * MIB),
        cost_estimate=pl.CostEstimate(
            flops=4 * tiles * row_tile * positions * width,
            bytes_accessed=8 * tiles * row_tile * positions,
            transcendentals=tiles * row_tile * positions,
        ),
        name="first_half",
    )(*pairs[::-1], queries, grads, lse_rows, dot_rows)


def second_half_kernel(score_scale, per_group, pieces, *refs):
    pair_refs, refs = refs[:pieces], refs[pieces:]
    queries_ref, grads_ref, peak_ref, total_ref, dotted_ref = refs[:5]
    out_ref, inverse_ref, delta_ref = refs[5:8]
    keys, values, key_total, value_total = refs[8:12]
    even, odd = refs[12:16], refs[16:20]
    _, columns, _, own, share, width = out_ref.shape
    tiles = queries_ref.shape[0]
    factor = score_scale * LOG2E
    load_pairs(pair_refs, keys, values)
    key_total[...] = jnp.zeros_like(key_total)
    value_total[...] = jnp.zeros_like(value_total)

    def products(tile, buffers):
        slot = tile // per_group
        multiply(keys[slot], values[slot], queries_ref[tile], grads_ref[tile], *buffers[:2])

    def normalize(tile, buffers):
        scores, slopes, weights, dscores = buffers
        first_peak = peak_ref[tile]
        peak = jnp.maximum(largest(scores) * factor, first_peak)
        total, dotted = exponentiate(scores, slopes, factor, peak)
        rescale = jnp.exp2(first_peak - peak)
        inverse = 1.0 / (total + total_ref[tile] * rescale)
        delta = (dotted + dotted_ref[tile] * rescale) * inverse
        inverse_ref[tile] = inverse * rescale
        delta_ref[tile] = delta
        weigh(scores, slopes, inverse, delta, weights, dscores)

    def gather(tile, buffers):
        accumulate(
            key_total,
            value_total,
            tile // per_group,
            buffers[2],
            buffers[3],
            queries_ref[tile],
            grads_ref[tile],
        )

    products(0, even)
    products(1, odd)
    normalize(0, even)

    def two_tiles(step, carry):
        tile = step * 2
        products(tile + 2, even)
        normalize(tile + 1, odd)
        gather(tile, even)
        products(tile + 3, odd)
        normalize(tile + 2, even)
        gather(tile + 1, odd)
        return carry

    lax.fori_loop(0, tiles // 2 - 1, two_tiles, 0)
    normalize(tiles - 1, odd)
    gather(tiles - 2, even)
    gather(tiles - 1, odd)
    shape = out_ref.shape[:2] + (share, width)
    for slot in range(own):
        key_sum = key_total[slot] * score_scale
        out_ref[:, :, 0, slot] = key_sum.astype(jnp.bfloat16).reshape(shape)
        out_ref[:, :, 1, slot] = value_total[slot].astype(jnp.bfloat16).reshape(shape)


def second_half(pairs, queries, grads, stats, score_scale):
    columns, _, own, share, width = pairs[0].shape
    positions = len(pairs) * columns * share
    tiles, row_tile, _ = queries.shape
    stat = jax.ShapeDtypeStruct((tiles, 1, row_tile), jnp.float32)
    buffers = [
        pltpu.VMEM((positions, row_tile), jnp.float32),
        pltpu.VMEM((positions, row_tile), jnp.float32),
        pltpu.VMEM((positions, row_tile), jnp.bfloat16),
        pltpu.VMEM((positions, row_tile), jnp.bfloat16),
    ]
    return pl.pallas_call(
        functools.partial(second_half_kernel, score_scale, tiles // own, len(pairs)),
        out_shape=(
            jax.ShapeDtypeStruct((len(pairs),) + pairs[0].shape, jnp.bfloat16),
            stat,
            stat,
        ),
        scratch_shapes=[
            pltpu.VMEM((own, positions, width), jnp.bfloat16),
            pltpu.VMEM((own, positions, width), jnp.bfloat16),
            pltpu.VMEM((own, positions, width), jnp.float32),
            pltpu.VMEM((own, positions, width), jnp.float32),
        ]
        + buffers
        + buffers,
        compiler_params=pltpu.CompilerParams(vmem_limit_bytes=30 * MIB),
        cost_estimate=pl.CostEstimate(
            flops=8 * tiles * row_tile * positions * width,
            bytes_accessed=4 * tiles * row_tile * width,
            transcendentals=tiles * row_tile * positions,
        ),
        name="second_half",
    )(*pairs, queries, grads, *stats)


def finish_kernel(score_scale, per_group, *refs):
    kept, refs = refs[:4], refs[4:]
    queries_ref, grads_ref, inverse_ref, delta_ref, out_ref = refs[:5]
    key_total, value_total = refs[5:7]
    even, odd = refs[7:9], refs[9:11]
    _, columns, _, own, share, width = out_ref.shape
    tiles = queries_ref.shape[0]
    key_total[...] = jnp.zeros_like(key_total)
    value_total[...] = jnp.zeros_like(value_total)

    def spread(tile, parity, step, buffers):
        weigh(
            kept[2 * parity].at[step],
            kept[2 * parity + 1].at[step],
            inverse_ref[tile],
            delta_ref[tile],
            *buffers,
        )

    def gather(tile, buffers):
        accumulate(
            key_total,
            value_total,
            tile // per_group,
            *buffers,
            queries_ref[tile],
            grads_ref[tile],
        )

    spread(0, 0, 0, even)

    def two_tiles(step, carry):
        spread(2 * step + 1, 1, step, odd)
        gather(2 * step, even)
        spread(2 * step + 2, 0, step + 1, even)
        gather(2 * step + 1, odd)
        return carry

    last = tiles // 2 - 1
    lax.fori_loop(0, last, two_tiles, 0)
    spread(tiles - 1, 1, last, odd)
    gather(tiles - 2, even)
    gather(tiles - 1, odd)
    shape = out_ref.shape[:2] + (share, width)
    for slot in range(own):
        out_ref[:, :, 0, slot] = (key_total[slot] * score_scale).reshape(shape)
        out_ref[:, :, 1, slot] = value_total[slot].reshape(shape)


def finish(kept, queries, grads, inverse, delta, shape, score_scale):
    _, positions, row_tile = kept[0].shape
    own, width = shape[3], shape[5]
    tiles = queries.shape[0]
    buffers = [pltpu.VMEM((positions, row_tile), jnp.bfloat16)] * 4
    return pl.pallas_call(
        functools.partial(finish_kernel, score_scale, tiles // own),
        out_shape=jax.ShapeDtypeStruct(shape, jnp.float32),
        scratch_shapes=[
            pltpu.VMEM((own, positions, width), jnp.float32),
            pltpu.VMEM((own, positions, width), jnp.float32),
        ]
        + buffers,
        compiler_params=pltpu.CompilerParams(vmem_limit_bytes=30 * MIB),
        cost_estimate=pl.CostEstimate(
            flops=4 * tiles * row_tile * positions * width,
            bytes_accessed=8 * tiles * row_tile * positions,
            transcendentals=0,
        ),
        name="finish",
    )(*kept, queries, grads, inverse, delta)


def chip_sum_kernel(mine_ref, mate_ref, *outs):
    for offset, out in enumerate(outs):
        out[...] = (mine_ref[offset] + mate_ref[offset].astype(jnp.float32)).astype(out.dtype)


def chip_sum(mine, mate):
    chips = mine.shape[0]
    shape = mine.shape[1:]
    return pl.pallas_call(
        chip_sum_kernel,
        out_shape=[
            jax.ShapeDtypeStruct(shape, jnp.bfloat16 if flip else jnp.float32)
            for flip in flips(chips)
        ],
        compiler_params=pltpu.CompilerParams(vmem_limit_bytes=16 * MIB),
        name="chip_sum",
    )(mine, mate)


def column_sum_kernel(away, mine_ref, *refs):
    others, outs = refs[:away], refs[away:]
    for offset, out in enumerate(outs):
        total = mine_ref[offset]
        for other in others:
            total = total + other[offset].astype(jnp.float32)
        out[...] = total.astype(out.dtype)


def column_sum(mine, others):
    columns = mine.shape[0]
    shape = mine.shape[1:]
    return pl.pallas_call(
        functools.partial(column_sum_kernel, len(others)),
        out_shape=[
            jax.ShapeDtypeStruct(shape, jnp.bfloat16 if flip else jnp.float32)
            for flip in flips(columns)
        ],
        compiler_params=pltpu.CompilerParams(vmem_limit_bytes=16 * MIB),
        name="column_sum",
    )(mine, *others)


def adam_kernel(columns, *refs):
    parts, refs = refs[:columns], refs[columns:]
    cache_ref, first_ref, second_ref, new_cache, new_first, new_second = refs[:6]
    by_flip, gathered = refs[6:]
    groups = cache_ref.shape[2]
    own = parts[0].shape[1]
    repeat = own * columns // groups
    for part, flip in zip(parts, flips(columns)):
        by_flip[flip] = part[...].astype(jnp.float32)
    column = lax.axis_index("cache")
    for side in range(2):
        for group in range(groups):
            first_owner = group // own * repeat
            slot = group % own
            total = by_flip[column ^ first_owner, side, slot]
            for owner in range(first_owner + 1, first_owner + repeat):
                total = total + by_flip[column ^ owner, side, slot]
            gathered[:, side, group] = total
    gradient = gathered[...]
    first = beta_first * first_ref[...] + (1.0 - beta_first) * gradient
    second = beta_second * second_ref[...] + (1.0 - beta_second) * gradient * gradient
    first_hat = first / (1.0 - beta_first**STEP)
    second_hat = second / (1.0 - beta_second**STEP)
    new_cache[...] = cache_ref[...] - learn_rate * first_hat / (jnp.sqrt(second_hat) + epsilon)
    new_first[...] = first
    new_second[...] = second


def adam(parts, cache, first_moment, second_moment):
    shape = jax.ShapeDtypeStruct(cache.shape, jnp.float32)
    return pl.pallas_call(
        functools.partial(adam_kernel, len(parts)),
        out_shape=(shape, shape, shape),
        scratch_shapes=[
            pltpu.VMEM((len(parts),) + parts[0].shape, jnp.float32),
            pltpu.VMEM(cache.shape, jnp.float32),
        ],
        compiler_params=pltpu.CompilerParams(vmem_limit_bytes=16 * MIB),
        name="adam",
    )(*parts, cache, first_moment, second_moment)


def swap(value, axis, size, flip):
    return lax.ppermute(value, axis, [(place, place ^ flip) for place in range(size)])


def swap_all(values, axis, size, stride):
    return [
        swap(value, axis, size, flip * stride) if flip else value
        for value, flip in zip(values, flips(len(values)))
    ]


def per_device(
    dp_size, columns, queries, out_grad, self_lse, self_dot, cache, first_moment, second_moment
):
    _, _, groups, width = cache.shape
    tokens, heads, _ = queries.shape
    chips = dp_size // 2
    group_size = heads // groups
    score_scale = 1.0 / math.sqrt(width)
    own = max(1, groups // columns)
    repeat = own * columns // groups
    own_tokens = tokens // repeat
    column = lax.axis_index("cache")
    first_group = column // repeat * own
    first_token = column % repeat * own_tokens

    slices = pack(cache, columns, own)
    gathered = jnp.stack(swap_all(slices, "cache", columns, 1))
    pairs = swap_all([gathered] * chips, "dp", dp_size, 2)
    def tiles_of(array):
        parts = array.reshape((tokens, groups, group_size) + array.shape[2:])
        part = lax.dynamic_slice_in_dim(parts, first_token, own_tokens, 0)
        part = lax.dynamic_slice_in_dim(part, first_group, own, 1)
        return jnp.moveaxis(part, 1, 0).reshape((-1, ROW_TILE) + array.shape[2:])

    tiles = [tiles_of(queries), tiles_of(out_grad)]
    tiles += [tiles_of(self_lse), tiles_of(self_dot)]
    own_pair, tiles = lax.optimization_barrier((pairs[-1], tiles))
    query_tiles, grad_tiles, lse_rows, dot_rows = tiles
    mate_pairs = [swap(pair, "dp", dp_size, 1) for pair in pairs[:-1] + [own_pair]]
    *kept, peak, total, dotted = first_half(
        pairs, query_tiles, grad_tiles, lse_rows, dot_rows, score_scale
    )
    mate, inverse, delta = second_half(
        mate_pairs, query_tiles, grad_tiles, (peak, total, dotted), score_scale
    )
    from_mate = swap(mate, "dp", dp_size, 1)
    mine = finish(kept, query_tiles, grad_tiles, inverse, delta, mate.shape, score_scale)
    by_chip = chip_sum(mine, from_mate)
    *away, home = swap_all(by_chip, "dp", dp_size, 2)
    by_column = column_sum(home, away)
    parts = swap_all(by_column, "cache", columns, 1)
    return adam(parts, cache, first_moment, second_moment)


def solution(mesh):
    in_specs = (
        P("dp", None, None),
        P("dp", None, None),
        P("dp", None),
        P("dp", None),
        P(("dp", "cache"), None, None, None),
        P(("dp", "cache"), None, None, None),
        P(("dp", "cache"), None, None, None),
    )
    out_specs = (
        P(("dp", "cache"), None, None, None),
        P(("dp", "cache"), None, None, None),
        P(("dp", "cache"), None, None, None),
    )
    return jax.shard_map(
        functools.partial(per_device, mesh.shape["dp"], mesh.shape["cache"]),
        mesh=mesh,
        in_specs=in_specs,
        out_specs=out_specs,
        check_vma=False,
    )
```

```python
import functools
import math

import jax
import jax.numpy as jnp
from jax import lax
from jax.experimental import pallas as pl
from jax.experimental.pallas import tpu as pltpu
from jax.sharding import PartitionSpec as P

STEP = 200

learn_rate = 0.02
beta_first = 0.9
beta_second = 0.999
epsilon = 1e-08

ROW_TILE = 512
CHUNK = 16
DOT_ROWS = 256
MIB = 1024 * 1024


def flips(size):
    return list(range(size - 1, -1, -1))


def pack_kernel(columns, cache_ref, *refs):
    *outs, by_group = refs
    groups = cache_ref.shape[2]
    own = outs[0].shape[1]
    repeat = own * columns // groups
    for side in range(2):
        for group in range(groups):
            by_group[group, side] = cache_ref[:, side, group].astype(jnp.bfloat16)
    column = lax.axis_index("cache")
    for out, flip in zip(outs, flips(columns)):
        first = (column ^ flip) // repeat * own
        for slot in range(own):
            for side in range(2):
                out[side, slot] = by_group[first + slot, side]


def pack(cache, columns, own):
    share, _, groups, width = cache.shape
    slice_shape = jax.ShapeDtypeStruct((2, own, share, width), jnp.bfloat16)
    return pl.pallas_call(
        functools.partial(pack_kernel, columns),
        out_shape=[slice_shape] * columns,
        scratch_shapes=[pltpu.VMEM((groups, 2, share, width), jnp.bfloat16)],
        compiler_params=pltpu.CompilerParams(vmem_limit_bytes=16 * MIB),
        name="pack",
    )(cache)


LOG2E = math.log2(math.e)
ACROSS = (((1,), (1,)), ((), ()))
ALONG = (((1,), (0,)), ((), ()))


def load_pairs(pair_refs, keys, values):
    columns, _, own, share, width = pair_refs[0].shape
    length = columns * share
    for piece, pair_ref in enumerate(pair_refs):
        at = pl.ds(piece * length, length)
        for slot in range(own):
            keys[slot, at] = pair_ref[:, 0, slot].reshape(length, width)
            values[slot, at] = pair_ref[:, 1, slot].reshape(length, width)


def interleave(passes, *products):
    products = [product for some in products for product in some]
    steps = passes[0]
    done = 0
    for number, step in enumerate(passes[1]):
        while done < len(products) and done * steps <= number * len(products):
            products[done]()
            done += 1
    for product in products[done:]:
        product()


def score_products(keys, values, slot, queries_ref, grads_ref, tile, scores, slopes):
    def product(rows, left, right_ref, out):
        def run():
            out[:, rows] = lax.dot_general(
                left[slot], right_ref[tile, rows], ACROSS, preferred_element_type=jnp.float32
            )

        return run

    products = []
    for start in range(0, scores.shape[1], DOT_ROWS):
        rows = pl.ds(start, DOT_ROWS)
        products.append(product(rows, keys, queries_ref, scores))
        products.append(product(rows, values, grads_ref, slopes))
    return products


def gradient_products(key_total, value_total, slot, weights, dscores, queries_ref, grads_ref, tile):
    def product(total, left, right_ref):
        def run():
            total[slot] += lax.dot_general(
                left[...], right_ref[tile], ALONG, preferred_element_type=jnp.float32
            )

        return run

    return [
        product(key_total, dscores, queries_ref),
        product(value_total, weights, grads_ref),
    ]


def cuts_of(ref):
    return [pl.ds(start, CHUNK) for start in range(0, ref.shape[0], CHUNK)]


def largest(scores, result):
    top = None
    for cut in cuts_of(scores):
        top = scores[cut] if top is None else jnp.maximum(top, scores[cut])
        yield
    result.append(jnp.max(top, axis=0, keepdims=True))


def exponentiate(scores, slopes, factor, peak, result):
    total = None
    dotted = None
    for cut in cuts_of(scores):
        shifted = jnp.exp2(scores[cut] * factor - peak)
        product = shifted * slopes[cut]
        scores[cut] = shifted
        total = shifted if total is None else total + shifted
        dotted = product if dotted is None else dotted + product
        yield
    result.append(jnp.sum(total, axis=0, keepdims=True))
    result.append(jnp.sum(dotted, axis=0, keepdims=True))


def weigh(shifted, slopes, inverse, delta, weights, dscores):
    for cut in cuts_of(weights):
        probability = shifted[cut] * inverse
        weights[cut] = probability.astype(jnp.bfloat16)
        dscores[cut] = (probability * (slopes[cut] - delta)).astype(jnp.bfloat16)
        yield


def first_half_kernel(score_scale, per_group, pieces, *refs):
    pair_refs, refs = refs[:pieces][::-1], refs[pieces:]
    queries_ref, grads_ref, lse_ref, dot_ref = refs[:4]
    kept, (peak_ref, total_ref, dotted_ref, keys, values) = refs[4:8], refs[8:]
    tiles = queries_ref.shape[0]
    factor = score_scale * LOG2E
    load_pairs(pair_refs, keys, values)

    def place(tile, parity, step):
        return kept[2 * parity].at[step], kept[2 * parity + 1].at[step]

    def products(tile, parity, step):
        slot = tile // per_group
        return score_products(
            keys, values, slot, queries_ref, grads_ref, tile, *place(tile, parity, step)
        )

    def normalize(tile, parity, step):
        scores, slopes = place(tile, parity, step)

        def passes():
            side_lse = lse_ref[pl.ds(tile, 1)] * LOG2E
            found = []
            yield from largest(scores, found)
            peak = jnp.maximum(found[0] * factor, side_lse)
            sums = []
            yield from exponentiate(scores, slopes, factor, peak, sums)
            side = jnp.exp2(side_lse - peak)
            peak_ref[tile] = peak
            total_ref[tile] = sums[0] + side
            dotted_ref[tile] = sums[1] + side * dot_ref[pl.ds(tile, 1)]

        return 2 * len(cuts_of(scores)), passes()

    for product in products(0, 0, 0):
        product()

    def two_tiles(step, carry):
        interleave(normalize(2 * step, 0, step), products(2 * step + 1, 1, step))
        interleave(normalize(2 * step + 1, 1, step), products(2 * step + 2, 0, step + 1))
        return carry

    last = tiles // 2 - 1
    lax.fori_loop(0, last, two_tiles, 0)
    interleave(normalize(tiles - 2, 0, last), products(tiles - 1, 1, last))
    interleave(normalize(tiles - 1, 1, last))


def first_half(pairs, queries, grads, lse_rows, dot_rows, score_scale):
    columns, _, own, share, width = pairs[0].shape
    positions = len(pairs) * columns * share
    tiles, row_tile, _ = queries.shape
    kept = jax.ShapeDtypeStruct((tiles // 2, positions, row_tile), jnp.float32)
    stat = jax.ShapeDtypeStruct((tiles, 1, row_tile), jnp.float32)
    return pl.pallas_call(
        functools.partial(first_half_kernel, score_scale, tiles // own, len(pairs)),
        out_shape=[kept] * 4 + [stat] * 3,
        scratch_shapes=[
            pltpu.VMEM((own, positions, width), jnp.bfloat16),
            pltpu.VMEM((own, positions, width), jnp.bfloat16),
        ],
        compiler_params=pltpu.CompilerParams(vmem_limit_bytes=30 * MIB),
        cost_estimate=pl.CostEstimate(
            flops=4 * tiles * row_tile * positions * width,
            bytes_accessed=8 * tiles * row_tile * positions,
            transcendentals=tiles * row_tile * positions,
        ),
        name="first_half",
    )(*pairs[::-1], queries, grads, lse_rows, dot_rows)


def second_half_kernel(score_scale, per_group, pieces, *refs):
    pair_refs, refs = refs[:pieces], refs[pieces:]
    queries_ref, grads_ref, peak_ref, total_ref, dotted_ref = refs[:5]
    out_ref, inverse_ref, delta_ref = refs[5:8]
    keys, values, key_total, value_total = refs[8:12]
    even, odd = refs[12:16], refs[16:20]
    _, columns, _, own, share, width = out_ref.shape
    tiles = queries_ref.shape[0]
    factor = score_scale * LOG2E
    load_pairs(pair_refs, keys, values)
    key_total[...] = jnp.zeros_like(key_total)
    value_total[...] = jnp.zeros_like(value_total)

    def products(tile, buffers):
        slot = tile // per_group
        return score_products(keys, values, slot, queries_ref, grads_ref, tile, *buffers[:2])

    def normalize(tile, buffers):
        scores, slopes, weights, dscores = buffers

        def passes():
            found = []
            yield from largest(scores, found)
            first_peak = peak_ref[tile]
            peak = jnp.maximum(found[0] * factor, first_peak)
            sums = []
            yield from exponentiate(scores, slopes, factor, peak, sums)
            rescale = jnp.exp2(first_peak - peak)
            inverse = 1.0 / (sums[0] + total_ref[tile] * rescale)
            delta = (sums[1] + dotted_ref[tile] * rescale) * inverse
            inverse_ref[tile] = inverse * rescale
            delta_ref[tile] = delta
            yield from weigh(scores, slopes, inverse, delta, weights, dscores)

        return 3 * len(cuts_of(scores)), passes()

    def gather(tile, buffers):
        return gradient_products(
            key_total,
            value_total,
            tile // per_group,
            buffers[2],
            buffers[3],
            queries_ref,
            grads_ref,
            tile,
        )

    for product in products(0, even):
        product()
    interleave(normalize(0, even), products(1, odd))

    def two_tiles(step, carry):
        tile = step * 2
        interleave(normalize(tile + 1, odd), products(tile + 2, even), gather(tile, even))
        interleave(normalize(tile + 2, even), products(tile + 3, odd), gather(tile + 1, odd))
        return carry

    lax.fori_loop(0, tiles // 2 - 1, two_tiles, 0)
    interleave(normalize(tiles - 1, odd), gather(tiles - 2, even))
    for product in gather(tiles - 1, odd):
        product()
    shape = out_ref.shape[:2] + (share, width)
    for slot in range(own):
        key_sum = key_total[slot] * score_scale
        out_ref[:, :, 0, slot] = key_sum.astype(jnp.bfloat16).reshape(shape)
        out_ref[:, :, 1, slot] = value_total[slot].astype(jnp.bfloat16).reshape(shape)


def second_half(pairs, queries, grads, stats, score_scale):
    columns, _, own, share, width = pairs[0].shape
    positions = len(pairs) * columns * share
    tiles, row_tile, _ = queries.shape
    stat = jax.ShapeDtypeStruct((tiles, 1, row_tile), jnp.float32)
    buffers = [
        pltpu.VMEM((positions, row_tile), jnp.float32),
        pltpu.VMEM((positions, row_tile), jnp.float32),
        pltpu.VMEM((positions, row_tile), jnp.bfloat16),
        pltpu.VMEM((positions, row_tile), jnp.bfloat16),
    ]
    return pl.pallas_call(
        functools.partial(second_half_kernel, score_scale, tiles // own, len(pairs)),
        out_shape=(
            jax.ShapeDtypeStruct((len(pairs),) + pairs[0].shape, jnp.bfloat16),
            stat,
            stat,
        ),
        scratch_shapes=[
            pltpu.VMEM((own, positions, width), jnp.bfloat16),
            pltpu.VMEM((own, positions, width), jnp.bfloat16),
            pltpu.VMEM((own, positions, width), jnp.float32),
            pltpu.VMEM((own, positions, width), jnp.float32),
        ]
        + buffers
        + buffers,
        compiler_params=pltpu.CompilerParams(vmem_limit_bytes=30 * MIB),
        cost_estimate=pl.CostEstimate(
            flops=8 * tiles * row_tile * positions * width,
            bytes_accessed=4 * tiles * row_tile * width,
            transcendentals=tiles * row_tile * positions,
        ),
        name="second_half",
    )(*pairs, queries, grads, *stats)


def finish_kernel(score_scale, per_group, *refs):
    kept, refs = refs[:4], refs[4:]
    queries_ref, grads_ref, inverse_ref, delta_ref, out_ref = refs[:5]
    key_total, value_total = refs[5:7]
    even, odd = refs[7:9], refs[9:11]
    _, columns, _, own, share, width = out_ref.shape
    tiles = queries_ref.shape[0]
    key_total[...] = jnp.zeros_like(key_total)
    value_total[...] = jnp.zeros_like(value_total)

    def spread(tile, parity, step, buffers):
        steps = weigh(
            kept[2 * parity].at[step],
            kept[2 * parity + 1].at[step],
            inverse_ref[tile],
            delta_ref[tile],
            *buffers,
        )
        return len(cuts_of(buffers[0])), steps

    def gather(tile, buffers):
        return gradient_products(
            key_total, value_total, tile // per_group, *buffers, queries_ref, grads_ref, tile
        )

    interleave(spread(0, 0, 0, even))

    def two_tiles(step, carry):
        interleave(spread(2 * step + 1, 1, step, odd), gather(2 * step, even))
        interleave(spread(2 * step + 2, 0, step + 1, even), gather(2 * step + 1, odd))
        return carry

    last = tiles // 2 - 1
    lax.fori_loop(0, last, two_tiles, 0)
    interleave(spread(tiles - 1, 1, last, odd), gather(tiles - 2, even))
    for product in gather(tiles - 1, odd):
        product()
    shape = out_ref.shape[:2] + (share, width)
    for slot in range(own):
        out_ref[:, :, 0, slot] = (key_total[slot] * score_scale).reshape(shape)
        out_ref[:, :, 1, slot] = value_total[slot].reshape(shape)


def finish(kept, queries, grads, inverse, delta, shape, score_scale):
    _, positions, row_tile = kept[0].shape
    own, width = shape[3], shape[5]
    tiles = queries.shape[0]
    buffers = [pltpu.VMEM((positions, row_tile), jnp.bfloat16)] * 4
    return pl.pallas_call(
        functools.partial(finish_kernel, score_scale, tiles // own),
        out_shape=jax.ShapeDtypeStruct(shape, jnp.float32),
        scratch_shapes=[
            pltpu.VMEM((own, positions, width), jnp.float32),
            pltpu.VMEM((own, positions, width), jnp.float32),
        ]
        + buffers,
        compiler_params=pltpu.CompilerParams(vmem_limit_bytes=30 * MIB),
        cost_estimate=pl.CostEstimate(
            flops=4 * tiles * row_tile * positions * width,
            bytes_accessed=8 * tiles * row_tile * positions,
            transcendentals=0,
        ),
        name="finish",
    )(*kept, queries, grads, inverse, delta)


def chip_sum_kernel(mine_ref, mate_ref, *outs):
    for offset, out in enumerate(outs):
        out[...] = (mine_ref[offset] + mate_ref[offset].astype(jnp.float32)).astype(out.dtype)


def chip_sum(mine, mate):
    chips = mine.shape[0]
    shape = mine.shape[1:]
    return pl.pallas_call(
        chip_sum_kernel,
        out_shape=[
            jax.ShapeDtypeStruct(shape, jnp.bfloat16 if flip else jnp.float32)
            for flip in flips(chips)
        ],
        compiler_params=pltpu.CompilerParams(vmem_limit_bytes=16 * MIB),
        name="chip_sum",
    )(mine, mate)


def column_sum_kernel(away, mine_ref, *refs):
    others, outs = refs[:away], refs[away:]
    for offset, out in enumerate(outs):
        total = mine_ref[offset]
        for other in others:
            total = total + other[offset].astype(jnp.float32)
        out[...] = total.astype(out.dtype)


def column_sum(mine, others):
    columns = mine.shape[0]
    shape = mine.shape[1:]
    return pl.pallas_call(
        functools.partial(column_sum_kernel, len(others)),
        out_shape=[
            jax.ShapeDtypeStruct(shape, jnp.bfloat16 if flip else jnp.float32)
            for flip in flips(columns)
        ],
        compiler_params=pltpu.CompilerParams(vmem_limit_bytes=16 * MIB),
        name="column_sum",
    )(mine, *others)


def adam_kernel(columns, *refs):
    parts, refs = refs[:columns], refs[columns:]
    cache_ref, first_ref, second_ref, new_cache, new_first, new_second = refs[:6]
    by_flip, gathered = refs[6:]
    groups = cache_ref.shape[2]
    own = parts[0].shape[1]
    repeat = own * columns // groups
    for part, flip in zip(parts, flips(columns)):
        by_flip[flip] = part[...].astype(jnp.float32)
    column = lax.axis_index("cache")
    for side in range(2):
        for group in range(groups):
            first_owner = group // own * repeat
            slot = group % own
            total = by_flip[column ^ first_owner, side, slot]
            for owner in range(first_owner + 1, first_owner + repeat):
                total = total + by_flip[column ^ owner, side, slot]
            gathered[:, side, group] = total
    gradient = gathered[...]
    first = beta_first * first_ref[...] + (1.0 - beta_first) * gradient
    second = beta_second * second_ref[...] + (1.0 - beta_second) * gradient * gradient
    first_hat = first / (1.0 - beta_first**STEP)
    second_hat = second / (1.0 - beta_second**STEP)
    new_cache[...] = cache_ref[...] - learn_rate * first_hat / (jnp.sqrt(second_hat) + epsilon)
    new_first[...] = first
    new_second[...] = second


def adam(parts, cache, first_moment, second_moment):
    shape = jax.ShapeDtypeStruct(cache.shape, jnp.float32)
    return pl.pallas_call(
        functools.partial(adam_kernel, len(parts)),
        out_shape=(shape, shape, shape),
        scratch_shapes=[
            pltpu.VMEM((len(parts),) + parts[0].shape, jnp.float32),
            pltpu.VMEM(cache.shape, jnp.float32),
        ],
        compiler_params=pltpu.CompilerParams(vmem_limit_bytes=16 * MIB),
        name="adam",
    )(*parts, cache, first_moment, second_moment)


def swap(value, axis, size, flip):
    return lax.ppermute(value, axis, [(place, place ^ flip) for place in range(size)])


def swap_all(values, axis, size, stride):
    return [
        swap(value, axis, size, flip * stride) if flip else value
        for value, flip in zip(values, flips(len(values)))
    ]


def per_device(
    dp_size, columns, queries, out_grad, self_lse, self_dot, cache, first_moment, second_moment
):
    _, _, groups, width = cache.shape
    tokens, heads, _ = queries.shape
    chips = dp_size // 2
    group_size = heads // groups
    score_scale = 1.0 / math.sqrt(width)
    own = max(1, groups // columns)
    repeat = own * columns // groups
    own_tokens = tokens // repeat
    column = lax.axis_index("cache")
    first_group = column // repeat * own
    first_token = column % repeat * own_tokens

    slices = pack(cache, columns, own)
    gathered = jnp.stack(swap_all(slices, "cache", columns, 1))
    pairs = swap_all([gathered] * chips, "dp", dp_size, 2)
    def tiles_of(array):
        parts = array.reshape((tokens, groups, group_size) + array.shape[2:])
        part = lax.dynamic_slice_in_dim(parts, first_token, own_tokens, 0)
        part = lax.dynamic_slice_in_dim(part, first_group, own, 1)
        return jnp.moveaxis(part, 1, 0).reshape((-1, ROW_TILE) + array.shape[2:])

    tiles = [tiles_of(queries), tiles_of(out_grad)]
    tiles += [tiles_of(self_lse), tiles_of(self_dot)]
    own_pair, tiles = lax.optimization_barrier((pairs[-1], tiles))
    query_tiles, grad_tiles, lse_rows, dot_rows = tiles
    mate_pairs = [swap(pair, "dp", dp_size, 1) for pair in pairs[:-1] + [own_pair]]
    *kept, peak, total, dotted = first_half(
        pairs, query_tiles, grad_tiles, lse_rows, dot_rows, score_scale
    )
    mate, inverse, delta = second_half(
        mate_pairs, query_tiles, grad_tiles, (peak, total, dotted), score_scale
    )
    from_mate = swap(mate, "dp", dp_size, 1)
    mine = finish(kept, query_tiles, grad_tiles, inverse, delta, mate.shape, score_scale)
    by_chip = chip_sum(mine, from_mate)
    *away, home = swap_all(by_chip, "dp", dp_size, 2)
    by_column = column_sum(home, away)
    parts = swap_all(by_column, "cache", columns, 1)
    return adam(parts, cache, first_moment, second_moment)


def solution(mesh):
    in_specs = (
        P("dp", None, None),
        P("dp", None, None),
        P("dp", None),
        P("dp", None),
        P(("dp", "cache"), None, None, None),
        P(("dp", "cache"), None, None, None),
        P(("dp", "cache"), None, None, None),
    )
    out_specs = (
        P(("dp", "cache"), None, None, None),
        P(("dp", "cache"), None, None, None),
        P(("dp", "cache"), None, None, None),
    )
    return jax.shard_map(
        functools.partial(per_device, mesh.shape["dp"], mesh.shape["cache"]),
        mesh=mesh,
        in_specs=in_specs,
        out_specs=out_specs,
        check_vma=False,
    )
```

```python
import functools
import math

import jax
import jax.numpy as jnp
from jax import lax
from jax.experimental import pallas as pl
from jax.experimental.pallas import tpu as pltpu
from jax.sharding import PartitionSpec as P

STEP = 200

learn_rate = 0.02
beta_first = 0.9
beta_second = 0.999
epsilon = 1e-08

ROW_TILE = 512
CHUNK = 16
DOT_ROWS = 256
MIB = 1024 * 1024


def flips(size):
    return list(range(size - 1, -1, -1))


def pack_kernel(columns, cache_ref, *refs):
    *outs, by_group = refs
    groups = cache_ref.shape[2]
    own = outs[0].shape[1]
    repeat = own * columns // groups
    for side in range(2):
        for group in range(groups):
            by_group[group, side] = cache_ref[:, side, group].astype(jnp.bfloat16)
    column = lax.axis_index("cache")
    for out, flip in zip(outs, flips(columns)):
        first = (column ^ flip) // repeat * own
        for slot in range(own):
            for side in range(2):
                out[side, slot] = by_group[first + slot, side]


def pack(cache, columns, own):
    share, _, groups, width = cache.shape
    slice_shape = jax.ShapeDtypeStruct((2, own, share, width), jnp.bfloat16)
    return pl.pallas_call(
        functools.partial(pack_kernel, columns),
        out_shape=[slice_shape] * columns,
        scratch_shapes=[pltpu.VMEM((groups, 2, share, width), jnp.bfloat16)],
        compiler_params=pltpu.CompilerParams(vmem_limit_bytes=16 * MIB),
        name="pack",
    )(cache)


LOG2E = math.log2(math.e)
ACROSS = (((1,), (1,)), ((), ()))
ALONG = (((1,), (0,)), ((), ()))


def load_pairs(pair_refs, keys, values):
    columns, _, own, share, width = pair_refs[0].shape
    length = columns * share
    for piece, pair_ref in enumerate(pair_refs):
        at = pl.ds(piece * length, length)
        for slot in range(own):
            keys[slot, at] = pair_ref[:, 0, slot].reshape(length, width)
            values[slot, at] = pair_ref[:, 1, slot].reshape(length, width)


def interleave(passes, *products):
    products = [product for some in products for product in some]
    steps = passes[0]
    done = 0
    for number, step in enumerate(passes[1]):
        while done < len(products) and done * steps <= number * len(products):
            products[done]()
            done += 1
    for product in products[done:]:
        product()


def score_products(keys, values, slot, queries_ref, grads_ref, tile, scores, slopes, tops):
    def product(rows, left, right_ref, out):
        def run():
            found = lax.dot_general(
                left[slot], right_ref[tile, rows], ACROSS, preferred_element_type=jnp.float32
            )
            out[:, rows] = found
            if out is scores:
                tops[:, rows] = jnp.max(found.reshape(-1, 8, found.shape[1]), axis=0)

        return run

    products = []
    for start in range(0, scores.shape[1], DOT_ROWS):
        rows = pl.ds(start, DOT_ROWS)
        products.append(product(rows, keys, queries_ref, scores))
        products.append(product(rows, values, grads_ref, slopes))
    return products


def gradient_products(key_total, value_total, slot, weights, dscores, queries_ref, grads_ref, tile):
    def product(total, left, right_ref):
        def run():
            total[slot] += lax.dot_general(
                left[...], right_ref[tile], ALONG, preferred_element_type=jnp.float32
            )

        return run

    return [
        product(key_total, dscores, queries_ref),
        product(value_total, weights, grads_ref),
    ]


def cuts_of(ref):
    return [pl.ds(start, CHUNK) for start in range(0, ref.shape[0], CHUNK)]


def exponentiate(scores, slopes, factor, peak, kept, result):
    total = None
    dotted = None
    for cut in cuts_of(scores):
        shifted = jnp.exp2(scores[cut] * factor - peak)
        product = shifted * slopes[cut]
        kept[cut] = shifted.astype(jnp.bfloat16)
        total = shifted if total is None else total + shifted
        dotted = product if dotted is None else dotted + product
        yield
    result.append(jnp.sum(total, axis=0, keepdims=True))
    result.append(jnp.sum(dotted, axis=0, keepdims=True))


def weigh(kept, slopes, inverse, delta, weights, dscores):
    for cut in cuts_of(weights):
        probability = kept[cut].astype(jnp.float32) * inverse
        weights[cut] = probability.astype(jnp.bfloat16)
        dscores[cut] = (probability * (slopes[cut] - delta)).astype(jnp.bfloat16)
        yield


def first_half_kernel(score_scale, per_group, pieces, *refs):
    pair_refs, refs = refs[:pieces][::-1], refs[pieces:]
    queries_ref, grads_ref, lse_ref, dot_ref = refs[:4]
    kept, (peak_ref, total_ref, dotted_ref, keys, values) = refs[4:8], refs[8:13]
    even, odd = refs[13:15], refs[15:17]
    tiles = queries_ref.shape[0]
    factor = score_scale * LOG2E
    load_pairs(pair_refs, keys, values)

    def place(parity, step):
        scores, tops = odd if parity else even
        return scores, kept[2 * parity].at[step], kept[2 * parity + 1].at[step], tops

    def products(tile, parity, step):
        scores, _, slopes, tops = place(parity, step)
        slot = tile // per_group
        return score_products(
            keys, values, slot, queries_ref, grads_ref, tile, scores, slopes, tops
        )

    def normalize(tile, parity, step):
        scores, shifted, slopes, tops = place(parity, step)

        def passes():
            side_lse = lse_ref[pl.ds(tile, 1)] * LOG2E
            peak = jnp.max(tops[...], axis=0, keepdims=True) * factor
            peak = jnp.maximum(peak, side_lse)
            sums = []
            yield from exponentiate(scores, slopes, factor, peak, shifted, sums)
            side = jnp.exp2(side_lse - peak)
            peak_ref[tile] = peak
            total_ref[tile] = sums[0] + side
            dotted_ref[tile] = sums[1] + side * dot_ref[pl.ds(tile, 1)]

        return len(cuts_of(scores)), passes()

    for product in products(0, 0, 0):
        product()

    def two_tiles(step, carry):
        interleave(normalize(2 * step, 0, step), products(2 * step + 1, 1, step))
        interleave(normalize(2 * step + 1, 1, step), products(2 * step + 2, 0, step + 1))
        return carry

    last = tiles // 2 - 1
    lax.fori_loop(0, last, two_tiles, 0)
    interleave(normalize(tiles - 2, 0, last), products(tiles - 1, 1, last))
    interleave(normalize(tiles - 1, 1, last))


def first_half(pairs, queries, grads, lse_rows, dot_rows, score_scale):
    columns, _, own, share, width = pairs[0].shape
    positions = len(pairs) * columns * share
    tiles, row_tile, _ = queries.shape
    kept = [
        jax.ShapeDtypeStruct((tiles // 2, positions, row_tile), kind)
        for kind in (jnp.bfloat16, jnp.float32)
    ]
    buffers = [
        pltpu.VMEM((positions, row_tile), jnp.float32),
        pltpu.VMEM((8, row_tile), jnp.float32),
    ]
    stat = jax.ShapeDtypeStruct((tiles, 1, row_tile), jnp.float32)
    return pl.pallas_call(
        functools.partial(first_half_kernel, score_scale, tiles // own, len(pairs)),
        out_shape=kept + kept + [stat] * 3,
        scratch_shapes=[
            pltpu.VMEM((own, positions, width), jnp.bfloat16),
            pltpu.VMEM((own, positions, width), jnp.bfloat16),
        ]
        + buffers
        + buffers,
        compiler_params=pltpu.CompilerParams(vmem_limit_bytes=30 * MIB),
        cost_estimate=pl.CostEstimate(
            flops=4 * tiles * row_tile * positions * width,
            bytes_accessed=8 * tiles * row_tile * positions,
            transcendentals=tiles * row_tile * positions,
        ),
        name="first_half",
    )(*pairs[::-1], queries, grads, lse_rows, dot_rows)


def second_half_kernel(score_scale, per_group, pieces, *refs):
    pair_refs, refs = refs[:pieces], refs[pieces:]
    queries_ref, grads_ref, peak_ref, total_ref, dotted_ref = refs[:5]
    out_ref, inverse_ref, delta_ref = refs[5:8]
    keys, values, key_total, value_total = refs[8:12]
    even, odd = refs[12:18], refs[18:24]
    _, columns, _, own, share, width = out_ref.shape
    tiles = queries_ref.shape[0]
    factor = score_scale * LOG2E
    load_pairs(pair_refs, keys, values)
    key_total[...] = jnp.zeros_like(key_total)
    value_total[...] = jnp.zeros_like(value_total)

    def products(tile, buffers):
        slot = tile // per_group
        return score_products(keys, values, slot, queries_ref, grads_ref, tile, *buffers[:3])

    def normalize(tile, buffers):
        scores, slopes, tops, shifted, weights, dscores = buffers

        def passes():
            first_peak = peak_ref[tile]
            peak = jnp.max(tops[...], axis=0, keepdims=True) * factor
            peak = jnp.maximum(peak, first_peak)
            sums = []
            yield from exponentiate(scores, slopes, factor, peak, shifted, sums)
            rescale = jnp.exp2(first_peak - peak)
            inverse = 1.0 / (sums[0] + total_ref[tile] * rescale)
            delta = (sums[1] + dotted_ref[tile] * rescale) * inverse
            inverse_ref[tile] = inverse * rescale
            delta_ref[tile] = delta
            yield from weigh(shifted, slopes, inverse, delta, weights, dscores)

        return 2 * len(cuts_of(scores)), passes()

    def gather(tile, buffers):
        return gradient_products(
            key_total,
            value_total,
            tile // per_group,
            *buffers[4:],
            queries_ref,
            grads_ref,
            tile,
        )

    for product in products(0, even):
        product()
    interleave(normalize(0, even), products(1, odd))

    def two_tiles(step, carry):
        tile = step * 2
        interleave(normalize(tile + 1, odd), products(tile + 2, even), gather(tile, even))
        interleave(normalize(tile + 2, even), products(tile + 3, odd), gather(tile + 1, odd))
        return carry

    lax.fori_loop(0, tiles // 2 - 1, two_tiles, 0)
    interleave(normalize(tiles - 1, odd), gather(tiles - 2, even))
    for product in gather(tiles - 1, odd):
        product()
    shape = out_ref.shape[:2] + (share, width)
    for slot in range(own):
        key_sum = key_total[slot] * score_scale
        out_ref[:, :, 0, slot] = key_sum.astype(jnp.bfloat16).reshape(shape)
        out_ref[:, :, 1, slot] = value_total[slot].astype(jnp.bfloat16).reshape(shape)


def second_half(pairs, queries, grads, stats, score_scale):
    columns, _, own, share, width = pairs[0].shape
    positions = len(pairs) * columns * share
    tiles, row_tile, _ = queries.shape
    stat = jax.ShapeDtypeStruct((tiles, 1, row_tile), jnp.float32)
    buffers = [
        pltpu.VMEM((positions, row_tile), jnp.float32),
        pltpu.VMEM((positions, row_tile), jnp.float32),
        pltpu.VMEM((8, row_tile), jnp.float32),
        pltpu.VMEM((positions, row_tile), jnp.bfloat16),
        pltpu.VMEM((positions, row_tile), jnp.bfloat16),
        pltpu.VMEM((positions, row_tile), jnp.bfloat16),
    ]
    return pl.pallas_call(
        functools.partial(second_half_kernel, score_scale, tiles // own, len(pairs)),
        out_shape=(
            jax.ShapeDtypeStruct((len(pairs),) + pairs[0].shape, jnp.bfloat16),
            stat,
            stat,
        ),
        scratch_shapes=[
            pltpu.VMEM((own, positions, width), jnp.bfloat16),
            pltpu.VMEM((own, positions, width), jnp.bfloat16),
            pltpu.VMEM((own, positions, width), jnp.float32),
            pltpu.VMEM((own, positions, width), jnp.float32),
        ]
        + buffers
        + buffers,
        compiler_params=pltpu.CompilerParams(vmem_limit_bytes=30 * MIB),
        cost_estimate=pl.CostEstimate(
            flops=8 * tiles * row_tile * positions * width,
            bytes_accessed=4 * tiles * row_tile * width,
            transcendentals=tiles * row_tile * positions,
        ),
        name="second_half",
    )(*pairs, queries, grads, *stats)


def finish_kernel(score_scale, per_group, *refs):
    kept, refs = refs[:4], refs[4:]
    queries_ref, grads_ref, inverse_ref, delta_ref, out_ref = refs[:5]
    key_total, value_total = refs[5:7]
    even, odd = refs[7:9], refs[9:11]
    _, columns, _, own, share, width = out_ref.shape
    tiles = queries_ref.shape[0]
    key_total[...] = jnp.zeros_like(key_total)
    value_total[...] = jnp.zeros_like(value_total)

    def spread(tile, parity, step, buffers):
        steps = weigh(
            kept[2 * parity].at[step],
            kept[2 * parity + 1].at[step],
            inverse_ref[tile],
            delta_ref[tile],
            *buffers,
        )
        return len(cuts_of(buffers[0])), steps

    def gather(tile, buffers):
        return gradient_products(
            key_total, value_total, tile // per_group, *buffers, queries_ref, grads_ref, tile
        )

    interleave(spread(0, 0, 0, even))

    def two_tiles(step, carry):
        interleave(spread(2 * step + 1, 1, step, odd), gather(2 * step, even))
        interleave(spread(2 * step + 2, 0, step + 1, even), gather(2 * step + 1, odd))
        return carry

    last = tiles // 2 - 1
    lax.fori_loop(0, last, two_tiles, 0)
    interleave(spread(tiles - 1, 1, last, odd), gather(tiles - 2, even))
    for product in gather(tiles - 1, odd):
        product()
    shape = out_ref.shape[:2] + (share, width)
    for slot in range(own):
        out_ref[:, :, 0, slot] = (key_total[slot] * score_scale).reshape(shape)
        out_ref[:, :, 1, slot] = value_total[slot].reshape(shape)


def finish(kept, queries, grads, inverse, delta, shape, score_scale):
    _, positions, row_tile = kept[0].shape
    own, width = shape[3], shape[5]
    tiles = queries.shape[0]
    buffers = [pltpu.VMEM((positions, row_tile), jnp.bfloat16)] * 4
    return pl.pallas_call(
        functools.partial(finish_kernel, score_scale, tiles // own),
        out_shape=jax.ShapeDtypeStruct(shape, jnp.float32),
        scratch_shapes=[
            pltpu.VMEM((own, positions, width), jnp.float32),
            pltpu.VMEM((own, positions, width), jnp.float32),
        ]
        + buffers,
        compiler_params=pltpu.CompilerParams(vmem_limit_bytes=30 * MIB),
        cost_estimate=pl.CostEstimate(
            flops=4 * tiles * row_tile * positions * width,
            bytes_accessed=8 * tiles * row_tile * positions,
            transcendentals=0,
        ),
        name="finish",
    )(*kept, queries, grads, inverse, delta)


def chip_sum_kernel(mine_ref, mate_ref, *outs):
    for offset, out in enumerate(outs):
        out[...] = (mine_ref[offset] + mate_ref[offset].astype(jnp.float32)).astype(out.dtype)


def chip_sum(mine, mate):
    chips = mine.shape[0]
    shape = mine.shape[1:]
    return pl.pallas_call(
        chip_sum_kernel,
        out_shape=[
            jax.ShapeDtypeStruct(shape, jnp.bfloat16 if flip else jnp.float32)
            for flip in flips(chips)
        ],
        compiler_params=pltpu.CompilerParams(vmem_limit_bytes=16 * MIB),
        name="chip_sum",
    )(mine, mate)


def column_sum_kernel(away, mine_ref, *refs):
    others, outs = refs[:away], refs[away:]
    for offset, out in enumerate(outs):
        total = mine_ref[offset]
        for other in others:
            total = total + other[offset].astype(jnp.float32)
        out[...] = total.astype(out.dtype)


def column_sum(mine, others):
    columns = mine.shape[0]
    shape = mine.shape[1:]
    return pl.pallas_call(
        functools.partial(column_sum_kernel, len(others)),
        out_shape=[
            jax.ShapeDtypeStruct(shape, jnp.bfloat16 if flip else jnp.float32)
            for flip in flips(columns)
        ],
        compiler_params=pltpu.CompilerParams(vmem_limit_bytes=16 * MIB),
        name="column_sum",
    )(mine, *others)


def adam_kernel(columns, *refs):
    parts, refs = refs[:columns], refs[columns:]
    cache_ref, first_ref, second_ref, new_cache, new_first, new_second = refs[:6]
    by_flip, gathered = refs[6:]
    groups = cache_ref.shape[2]
    own = parts[0].shape[1]
    repeat = own * columns // groups
    for part, flip in zip(parts, flips(columns)):
        by_flip[flip] = part[...].astype(jnp.float32)
    column = lax.axis_index("cache")
    for side in range(2):
        for group in range(groups):
            first_owner = group // own * repeat
            slot = group % own
            total = by_flip[column ^ first_owner, side, slot]
            for owner in range(first_owner + 1, first_owner + repeat):
                total = total + by_flip[column ^ owner, side, slot]
            gathered[:, side, group] = total
    gradient = gathered[...]
    first = beta_first * first_ref[...] + (1.0 - beta_first) * gradient
    second = beta_second * second_ref[...] + (1.0 - beta_second) * gradient * gradient
    first_hat = first / (1.0 - beta_first**STEP)
    second_hat = second / (1.0 - beta_second**STEP)
    new_cache[...] = cache_ref[...] - learn_rate * first_hat / (jnp.sqrt(second_hat) + epsilon)
    new_first[...] = first
    new_second[...] = second


def adam(parts, cache, first_moment, second_moment):
    shape = jax.ShapeDtypeStruct(cache.shape, jnp.float32)
    return pl.pallas_call(
        functools.partial(adam_kernel, len(parts)),
        out_shape=(shape, shape, shape),
        scratch_shapes=[
            pltpu.VMEM((len(parts),) + parts[0].shape, jnp.float32),
            pltpu.VMEM(cache.shape, jnp.float32),
        ],
        compiler_params=pltpu.CompilerParams(vmem_limit_bytes=16 * MIB),
        name="adam",
    )(*parts, cache, first_moment, second_moment)


def swap(value, axis, size, flip):
    return lax.ppermute(value, axis, [(place, place ^ flip) for place in range(size)])


def swap_all(values, axis, size, stride):
    return [
        swap(value, axis, size, flip * stride) if flip else value
        for value, flip in zip(values, flips(len(values)))
    ]


def per_device(
    dp_size, columns, queries, out_grad, self_lse, self_dot, cache, first_moment, second_moment
):
    _, _, groups, width = cache.shape
    tokens, heads, _ = queries.shape
    chips = dp_size // 2
    group_size = heads // groups
    score_scale = 1.0 / math.sqrt(width)
    own = max(1, groups // columns)
    repeat = own * columns // groups
    own_tokens = tokens // repeat
    column = lax.axis_index("cache")
    first_group = column // repeat * own
    first_token = column % repeat * own_tokens

    slices = pack(cache, columns, own)
    gathered = jnp.stack(swap_all(slices, "cache", columns, 1))
    pairs = swap_all([gathered] * chips, "dp", dp_size, 2)
    def tiles_of(array):
        parts = array.reshape((tokens, groups, group_size) + array.shape[2:])
        part = lax.dynamic_slice_in_dim(parts, first_token, own_tokens, 0)
        part = lax.dynamic_slice_in_dim(part, first_group, own, 1)
        return jnp.moveaxis(part, 1, 0).reshape((-1, ROW_TILE) + array.shape[2:])

    tiles = [tiles_of(queries), tiles_of(out_grad)]
    tiles += [tiles_of(self_lse), tiles_of(self_dot)]
    own_pair, tiles = lax.optimization_barrier((pairs[-1], tiles))
    query_tiles, grad_tiles, lse_rows, dot_rows = tiles
    mate_pairs = [swap(pair, "dp", dp_size, 1) for pair in pairs[:-1] + [own_pair]]
    *kept, peak, total, dotted = first_half(
        pairs, query_tiles, grad_tiles, lse_rows, dot_rows, score_scale
    )
    mate, inverse, delta = second_half(
        mate_pairs, query_tiles, grad_tiles, (peak, total, dotted), score_scale
    )
    from_mate = swap(mate, "dp", dp_size, 1)
    mine = finish(kept, query_tiles, grad_tiles, inverse, delta, mate.shape, score_scale)
    by_chip = chip_sum(mine, from_mate)
    *away, home = swap_all(by_chip, "dp", dp_size, 2)
    by_column = column_sum(home, away)
    parts = swap_all(by_column, "cache", columns, 1)
    return adam(parts, cache, first_moment, second_moment)


def solution(mesh):
    in_specs = (
        P("dp", None, None),
        P("dp", None, None),
        P("dp", None),
        P("dp", None),
        P(("dp", "cache"), None, None, None),
        P(("dp", "cache"), None, None, None),
        P(("dp", "cache"), None, None, None),
    )
    out_specs = (
        P(("dp", "cache"), None, None, None),
        P(("dp", "cache"), None, None, None),
        P(("dp", "cache"), None, None, None),
    )
    return jax.shard_map(
        functools.partial(per_device, mesh.shape["dp"], mesh.shape["cache"]),
        mesh=mesh,
        in_specs=in_specs,
        out_specs=out_specs,
        check_vma=False,
    )
```

```python
import functools
import math

import jax
import jax.numpy as jnp
from jax import lax
from jax.experimental import pallas as pl
from jax.experimental.pallas import tpu as pltpu
from jax.sharding import PartitionSpec as P

STEP = 200

learn_rate = 0.02
beta_first = 0.9
beta_second = 0.999
epsilon = 1e-08

ROW_TILE = 512
CHUNK = 16
DOT_ROWS = 256
MIB = 1024 * 1024


def flips(size):
    return list(range(size - 1, -1, -1))


def gather_flips(columns):
    return flips(columns)[1::-1] + flips(columns)[2:]


def pack_kernel(columns, cache_ref, *refs):
    *outs, by_group = refs
    groups = cache_ref.shape[2]
    own = outs[0].shape[1]
    repeat = own * columns // groups
    for side in range(2):
        for group in range(groups):
            by_group[group, side] = cache_ref[:, side, group].astype(jnp.bfloat16)
    column = lax.axis_index("cache")
    for out, flip in zip(outs, gather_flips(columns)):
        first = (column ^ flip) // repeat * own
        for slot in range(own):
            for side in range(2):
                out[side, slot] = by_group[first + slot, side]


def pack(cache, columns, own):
    share, _, groups, width = cache.shape
    slice_shape = jax.ShapeDtypeStruct((2, own, share, width), jnp.bfloat16)
    return pl.pallas_call(
        functools.partial(pack_kernel, columns),
        out_shape=[slice_shape] * columns,
        scratch_shapes=[pltpu.VMEM((groups, 2, share, width), jnp.bfloat16)],
        compiler_params=pltpu.CompilerParams(vmem_limit_bytes=16 * MIB),
        name="pack",
    )(cache)


LOG2E = math.log2(math.e)
ACROSS = (((1,), (1,)), ((), ()))
ALONG = (((1,), (0,)), ((), ()))


def load_pairs(pair_refs, keys, values):
    columns, _, own, share, width = pair_refs[0].shape
    length = columns * share
    for piece, pair_ref in enumerate(pair_refs):
        at = pl.ds(piece * length, length)
        for slot in range(own):
            keys[slot, at] = pair_ref[:, 0, slot].reshape(length, width)
            values[slot, at] = pair_ref[:, 1, slot].reshape(length, width)


def interleave(passes, *products):
    products = [product for some in products for product in some]
    steps = passes[0]
    done = 0
    for number, step in enumerate(passes[1]):
        while done < len(products) and done * steps <= number * len(products):
            products[done]()
            done += 1
    for product in products[done:]:
        product()


def score_products(keys, values, slot, queries_ref, grads_ref, tile, scores, slopes, tops):
    def product(rows, left, right_ref, out):
        def run():
            found = lax.dot_general(
                left[slot], right_ref[tile, rows], ACROSS, preferred_element_type=jnp.float32
            )
            out[:, rows] = found
            if out is scores:
                tops[:, rows] = jnp.max(found.reshape(-1, 8, found.shape[1]), axis=0)

        return run

    products = []
    for start in range(0, scores.shape[1], DOT_ROWS):
        rows = pl.ds(start, DOT_ROWS)
        products.append(product(rows, keys, queries_ref, scores))
        products.append(product(rows, values, grads_ref, slopes))
    return products


def gradient_products(key_total, value_total, slot, weights, dscores, queries_ref, grads_ref, tile):
    def product(total, left, right_ref):
        def run():
            total[slot] += lax.dot_general(
                left[...], right_ref[tile], ALONG, preferred_element_type=jnp.float32
            )

        return run

    return [
        product(key_total, dscores, queries_ref),
        product(value_total, weights, grads_ref),
    ]


def cuts_of(ref):
    return [pl.ds(start, CHUNK) for start in range(0, ref.shape[0], CHUNK)]


def exponentiate(scores, slopes, factor, peak, kept, result):
    total = None
    dotted = None
    for cut in cuts_of(scores):
        shifted = jnp.exp2(scores[cut] * factor - peak)
        product = shifted * slopes[cut]
        kept[cut] = shifted
        total = shifted if total is None else total + shifted
        dotted = product if dotted is None else dotted + product
        yield
    result.append(jnp.sum(total, axis=0, keepdims=True))
    result.append(jnp.sum(dotted, axis=0, keepdims=True))


def weigh(kept, slopes, inverse, delta, weights, dscores):
    for cut in cuts_of(weights):
        probability = kept[cut] * inverse
        weights[cut] = probability.astype(jnp.bfloat16)
        dscores[cut] = (probability * (slopes[cut] - delta)).astype(jnp.bfloat16)
        yield


def first_half_kernel(score_scale, per_group, pieces, *refs):
    pair_refs, refs = refs[:pieces][::-1], refs[pieces:]
    queries_ref, grads_ref, lse_ref, dot_ref = refs[:4]
    kept, (peak_ref, total_ref, dotted_ref, keys, values) = refs[4:8], refs[8:13]
    even, odd = refs[13:15], refs[15:17]
    tiles = queries_ref.shape[0]
    factor = score_scale * LOG2E
    load_pairs(pair_refs, keys, values)

    def place(parity, step):
        scores, tops = odd if parity else even
        return scores, kept[2 * parity].at[step], kept[2 * parity + 1].at[step], tops

    def products(tile, parity, step):
        scores, _, slopes, tops = place(parity, step)
        slot = tile // per_group
        return score_products(
            keys, values, slot, queries_ref, grads_ref, tile, scores, slopes, tops
        )

    def normalize(tile, parity, step):
        scores, shifted, slopes, tops = place(parity, step)

        def passes():
            side_lse = lse_ref[pl.ds(tile, 1)] * LOG2E
            peak = jnp.max(tops[...], axis=0, keepdims=True) * factor
            peak = jnp.maximum(peak, side_lse)
            sums = []
            yield from exponentiate(scores, slopes, factor, peak, shifted, sums)
            side = jnp.exp2(side_lse - peak)
            peak_ref[tile] = peak
            total_ref[tile] = sums[0] + side
            dotted_ref[tile] = sums[1] + side * dot_ref[pl.ds(tile, 1)]

        return len(cuts_of(scores)), passes()

    for product in products(0, 0, 0):
        product()

    def two_tiles(step):
        interleave(normalize(2 * step, 0, step), products(2 * step + 1, 1, step))
        interleave(normalize(2 * step + 1, 1, step), products(2 * step + 2, 0, step + 1))

    last = tiles // 2 - 1
    for step in range(last):
        two_tiles(step)
    interleave(normalize(tiles - 2, 0, last), products(tiles - 1, 1, last))
    interleave(normalize(tiles - 1, 1, last))


def first_half(pairs, queries, grads, lse_rows, dot_rows, score_scale):
    columns, _, own, share, width = pairs[0].shape
    positions = len(pairs) * columns * share
    tiles, row_tile, _ = queries.shape
    kept = [jax.ShapeDtypeStruct((tiles // 2, positions, row_tile), jnp.float32)] * 2
    buffers = [
        pltpu.VMEM((positions, row_tile), jnp.float32),
        pltpu.VMEM((8, row_tile), jnp.float32),
    ]
    stat = jax.ShapeDtypeStruct((tiles, 1, row_tile), jnp.float32)
    return pl.pallas_call(
        functools.partial(first_half_kernel, score_scale, tiles // own, len(pairs)),
        out_shape=kept + kept + [stat] * 3,
        scratch_shapes=[
            pltpu.VMEM((own, positions, width), jnp.bfloat16),
            pltpu.VMEM((own, positions, width), jnp.bfloat16),
        ]
        + buffers
        + buffers,
        compiler_params=pltpu.CompilerParams(vmem_limit_bytes=30 * MIB),
        cost_estimate=pl.CostEstimate(
            flops=4 * tiles * row_tile * positions * width,
            bytes_accessed=8 * tiles * row_tile * positions,
            transcendentals=tiles * row_tile * positions,
        ),
        name="first_half",
    )(*pairs[::-1], queries, grads, lse_rows, dot_rows)


def second_half_kernel(score_scale, per_group, pieces, *refs):
    pair_refs, refs = refs[:pieces], refs[pieces:]
    queries_ref, grads_ref, peak_ref, total_ref, dotted_ref = refs[:5]
    out_ref, inverse_ref, delta_ref = refs[5:8]
    keys, values, key_total, value_total = refs[8:12]
    even, odd = refs[12:17], refs[17:22]
    _, columns, _, own, share, width = out_ref.shape
    tiles = queries_ref.shape[0]
    factor = score_scale * LOG2E
    load_pairs(pair_refs, keys, values)
    key_total[...] = jnp.zeros_like(key_total)
    value_total[...] = jnp.zeros_like(value_total)

    def products(tile, buffers):
        slot = tile // per_group
        return score_products(keys, values, slot, queries_ref, grads_ref, tile, *buffers[:3])

    def normalize(tile, buffers):
        scores, slopes, tops, weights, dscores = buffers

        def passes():
            first_peak = peak_ref[tile]
            peak = jnp.max(tops[...], axis=0, keepdims=True) * factor
            peak = jnp.maximum(peak, first_peak)
            sums = []
            yield from exponentiate(scores, slopes, factor, peak, scores, sums)
            rescale = jnp.exp2(first_peak - peak)
            inverse = 1.0 / (sums[0] + total_ref[tile] * rescale)
            delta = (sums[1] + dotted_ref[tile] * rescale) * inverse
            inverse_ref[tile] = inverse * rescale
            delta_ref[tile] = delta
            yield from weigh(scores, slopes, inverse, delta, weights, dscores)

        return 2 * len(cuts_of(scores)), passes()

    def gather(tile, buffers):
        return gradient_products(
            key_total,
            value_total,
            tile // per_group,
            *buffers[3:],
            queries_ref,
            grads_ref,
            tile,
        )

    for product in products(0, even):
        product()
    interleave(normalize(0, even), products(1, odd))

    def two_tiles(step):
        tile = step * 2
        interleave(normalize(tile + 1, odd), products(tile + 2, even), gather(tile, even))
        interleave(normalize(tile + 2, even), products(tile + 3, odd), gather(tile + 1, odd))

    for step in range(tiles // 2 - 1):
        two_tiles(step)
    interleave(normalize(tiles - 1, odd), gather(tiles - 2, even))
    for product in gather(tiles - 1, odd):
        product()
    shape = out_ref.shape[:2] + (share, width)
    for slot in range(own):
        key_sum = key_total[slot] * score_scale
        out_ref[:, :, 0, slot] = key_sum.astype(jnp.bfloat16).reshape(shape)
        out_ref[:, :, 1, slot] = value_total[slot].astype(jnp.bfloat16).reshape(shape)


def second_half(pairs, queries, grads, stats, score_scale):
    columns, _, own, share, width = pairs[0].shape
    positions = len(pairs) * columns * share
    tiles, row_tile, _ = queries.shape
    stat = jax.ShapeDtypeStruct((tiles, 1, row_tile), jnp.float32)
    buffers = [
        pltpu.VMEM((positions, row_tile), jnp.float32),
        pltpu.VMEM((positions, row_tile), jnp.float32),
        pltpu.VMEM((8, row_tile), jnp.float32),
        pltpu.VMEM((positions, row_tile), jnp.bfloat16),
        pltpu.VMEM((positions, row_tile), jnp.bfloat16),
    ]
    return pl.pallas_call(
        functools.partial(second_half_kernel, score_scale, tiles // own, len(pairs)),
        out_shape=(
            jax.ShapeDtypeStruct((len(pairs),) + pairs[0].shape, jnp.bfloat16),
            stat,
            stat,
        ),
        scratch_shapes=[
            pltpu.VMEM((own, positions, width), jnp.bfloat16),
            pltpu.VMEM((own, positions, width), jnp.bfloat16),
            pltpu.VMEM((own, positions, width), jnp.float32),
            pltpu.VMEM((own, positions, width), jnp.float32),
        ]
        + buffers
        + buffers,
        compiler_params=pltpu.CompilerParams(vmem_limit_bytes=30 * MIB),
        cost_estimate=pl.CostEstimate(
            flops=8 * tiles * row_tile * positions * width,
            bytes_accessed=4 * tiles * row_tile * width,
            transcendentals=tiles * row_tile * positions,
        ),
        name="second_half",
    )(*pairs, queries, grads, *stats)


def finish_kernel(score_scale, per_group, *refs):
    kept, refs = refs[:4], refs[4:]
    queries_ref, grads_ref, inverse_ref, delta_ref, out_ref = refs[:5]
    key_total, value_total = refs[5:7]
    even, odd = refs[7:9], refs[9:11]
    _, columns, _, own, share, width = out_ref.shape
    tiles = queries_ref.shape[0]
    key_total[...] = jnp.zeros_like(key_total)
    value_total[...] = jnp.zeros_like(value_total)

    def spread(tile, parity, step, buffers):
        steps = weigh(
            kept[2 * parity].at[step],
            kept[2 * parity + 1].at[step],
            inverse_ref[tile],
            delta_ref[tile],
            *buffers,
        )
        return len(cuts_of(buffers[0])), steps

    def gather(tile, buffers):
        return gradient_products(
            key_total, value_total, tile // per_group, *buffers, queries_ref, grads_ref, tile
        )

    interleave(spread(0, 0, 0, even))

    def two_tiles(step):
        interleave(spread(2 * step + 1, 1, step, odd), gather(2 * step, even))
        interleave(spread(2 * step + 2, 0, step + 1, even), gather(2 * step + 1, odd))

    last = tiles // 2 - 1
    for step in range(last):
        two_tiles(step)
    interleave(spread(tiles - 1, 1, last, odd), gather(tiles - 2, even))
    for product in gather(tiles - 1, odd):
        product()
    shape = out_ref.shape[:2] + (share, width)
    for slot in range(own):
        out_ref[:, :, 0, slot] = (key_total[slot] * score_scale).reshape(shape)
        out_ref[:, :, 1, slot] = value_total[slot].reshape(shape)


def finish(kept, queries, grads, inverse, delta, shape, score_scale):
    _, positions, row_tile = kept[0].shape
    own, width = shape[3], shape[5]
    tiles = queries.shape[0]
    buffers = [pltpu.VMEM((positions, row_tile), jnp.bfloat16)] * 4
    return pl.pallas_call(
        functools.partial(finish_kernel, score_scale, tiles // own),
        out_shape=jax.ShapeDtypeStruct(shape, jnp.float32),
        scratch_shapes=[
            pltpu.VMEM((own, positions, width), jnp.float32),
            pltpu.VMEM((own, positions, width), jnp.float32),
        ]
        + buffers,
        compiler_params=pltpu.CompilerParams(vmem_limit_bytes=30 * MIB),
        cost_estimate=pl.CostEstimate(
            flops=4 * tiles * row_tile * positions * width,
            bytes_accessed=8 * tiles * row_tile * positions,
            transcendentals=0,
        ),
        name="finish",
    )(*kept, queries, grads, inverse, delta)


def chip_sum_kernel(mine_ref, mate_ref, *outs):
    for offset, out in enumerate(outs):
        out[...] = (mine_ref[offset] + mate_ref[offset].astype(jnp.float32)).astype(out.dtype)


def chip_sum(mine, mate):
    chips = mine.shape[0]
    shape = mine.shape[1:]
    return pl.pallas_call(
        chip_sum_kernel,
        out_shape=[
            jax.ShapeDtypeStruct(shape, jnp.bfloat16 if flip else jnp.float32)
            for flip in flips(chips)
        ],
        compiler_params=pltpu.CompilerParams(vmem_limit_bytes=16 * MIB),
        name="chip_sum",
    )(mine, mate)


def column_sum_kernel(away, mine_ref, *refs):
    others, outs = refs[:away], refs[away:]
    columns = len(outs)
    for out, flip in zip(outs, flips(columns)):
        place = gather_flips(columns).index(flip)
        total = mine_ref[place]
        for other in others:
            total = total + other[place].astype(jnp.float32)
        out[...] = total.astype(out.dtype)


def column_sum(mine, others):
    columns = mine.shape[0]
    shape = mine.shape[1:]
    return pl.pallas_call(
        functools.partial(column_sum_kernel, len(others)),
        out_shape=[
            jax.ShapeDtypeStruct(shape, jnp.bfloat16 if flip else jnp.float32)
            for flip in flips(columns)
        ],
        compiler_params=pltpu.CompilerParams(vmem_limit_bytes=16 * MIB),
        name="column_sum",
    )(mine, *others)


def adam_kernel(columns, *refs):
    parts, refs = refs[:columns], refs[columns:]
    cache_ref, first_ref, second_ref, new_cache, new_first, new_second = refs[:6]
    by_flip, gathered = refs[6:]
    groups = cache_ref.shape[2]
    own = parts[0].shape[1]
    repeat = own * columns // groups
    for part, flip in zip(parts, flips(columns)):
        by_flip[flip] = part[...].astype(jnp.float32)
    column = lax.axis_index("cache")
    for side in range(2):
        for group in range(groups):
            first_owner = group // own * repeat
            slot = group % own
            total = by_flip[column ^ first_owner, side, slot]
            for owner in range(first_owner + 1, first_owner + repeat):
                total = total + by_flip[column ^ owner, side, slot]
            gathered[:, side, group] = total
    gradient = gathered[...]
    first = beta_first * first_ref[...] + (1.0 - beta_first) * gradient
    second = beta_second * second_ref[...] + (1.0 - beta_second) * gradient * gradient
    first_hat = first / (1.0 - beta_first**STEP)
    second_hat = second / (1.0 - beta_second**STEP)
    new_cache[...] = cache_ref[...] - learn_rate * first_hat / (jnp.sqrt(second_hat) + epsilon)
    new_first[...] = first
    new_second[...] = second


def adam(parts, cache, first_moment, second_moment):
    shape = jax.ShapeDtypeStruct(cache.shape, jnp.float32)
    return pl.pallas_call(
        functools.partial(adam_kernel, len(parts)),
        out_shape=(shape, shape, shape),
        scratch_shapes=[
            pltpu.VMEM((len(parts),) + parts[0].shape, jnp.float32),
            pltpu.VMEM(cache.shape, jnp.float32),
        ],
        compiler_params=pltpu.CompilerParams(vmem_limit_bytes=16 * MIB),
        name="adam",
    )(*parts, cache, first_moment, second_moment)


def swap(value, axis, size, flip):
    return lax.ppermute(value, axis, [(place, place ^ flip) for place in range(size)])


def swap_all(values, axis, size, stride, order=flips):
    return [
        swap(value, axis, size, flip * stride) if flip else value
        for value, flip in zip(values, order(len(values)))
    ]


def per_device(
    dp_size, columns, queries, out_grad, self_lse, self_dot, cache, first_moment, second_moment
):
    _, _, groups, width = cache.shape
    tokens, heads, _ = queries.shape
    chips = dp_size // 2
    group_size = heads // groups
    score_scale = 1.0 / math.sqrt(width)
    own = max(1, groups // columns)
    repeat = own * columns // groups
    own_tokens = tokens // repeat
    column = lax.axis_index("cache")
    first_group = column // repeat * own
    first_token = column % repeat * own_tokens

    slices = pack(cache, columns, own)
    gathered = jnp.stack(swap_all(slices, "cache", columns, 1, gather_flips))
    pairs = swap_all([gathered] * chips, "dp", dp_size, 2)
    def tiles_of(array):
        parts = array.reshape((tokens, groups, group_size) + array.shape[2:])
        part = lax.dynamic_slice_in_dim(parts, first_token, own_tokens, 0)
        part = lax.dynamic_slice_in_dim(part, first_group, own, 1)
        return jnp.moveaxis(part, 1, 0).reshape((-1, ROW_TILE) + array.shape[2:])

    tiles = [tiles_of(queries), tiles_of(out_grad)]
    tiles += [tiles_of(self_lse), tiles_of(self_dot)]
    own_pair, tiles = lax.optimization_barrier((pairs[-1], tiles))
    query_tiles, grad_tiles, lse_rows, dot_rows = tiles
    mate_pairs = [swap(pair, "dp", dp_size, 1) for pair in pairs[:-1] + [own_pair]]
    *kept, peak, total, dotted = first_half(
        pairs, query_tiles, grad_tiles, lse_rows, dot_rows, score_scale
    )
    mate, inverse, delta = second_half(
        mate_pairs, query_tiles, grad_tiles, (peak, total, dotted), score_scale
    )
    from_mate = swap(mate, "dp", dp_size, 1)
    mine = finish(kept, query_tiles, grad_tiles, inverse, delta, mate.shape, score_scale)
    by_chip = chip_sum(mine, from_mate)
    *away, home = swap_all(by_chip, "dp", dp_size, 2)
    by_column = column_sum(home, away)
    parts = swap_all(by_column, "cache", columns, 1)
    return adam(parts, cache, first_moment, second_moment)


def solution(mesh):
    in_specs = (
        P("dp", None, None),
        P("dp", None, None),
        P("dp", None),
        P("dp", None),
        P(("dp", "cache"), None, None, None),
        P(("dp", "cache"), None, None, None),
        P(("dp", "cache"), None, None, None),
    )
    out_specs = (
        P(("dp", "cache"), None, None, None),
        P(("dp", "cache"), None, None, None),
        P(("dp", "cache"), None, None, None),
    )
    return jax.shard_map(
        functools.partial(per_device, mesh.shape["dp"], mesh.shape["cache"]),
        mesh=mesh,
        in_specs=in_specs,
        out_specs=out_specs,
        check_vma=False,
    )
```

```python
import functools
import math

import jax
import jax.numpy as jnp
from jax import lax
from jax.experimental import pallas as pl
from jax.experimental.pallas import tpu as pltpu
from jax.sharding import PartitionSpec as P

STEP = 200

learn_rate = 0.02
beta_first = 0.9
beta_second = 0.999
epsilon = 1e-08

ROW_TILE = 256
CHUNK = 32
DOT_ROWS = 256
MIB = 1024 * 1024


def flips(size):
    return list(range(size - 1, -1, -1))


def gather_flips(columns):
    return flips(columns)[1::-1] + flips(columns)[2:]


def pack_kernel(columns, cache_ref, *refs):
    *outs, by_group = refs
    groups = cache_ref.shape[2]
    own = outs[0].shape[1]
    repeat = own * columns // groups
    for side in range(2):
        for group in range(groups):
            by_group[group, side] = cache_ref[:, side, group].astype(jnp.bfloat16)
    column = lax.axis_index("cache")
    for out, flip in zip(outs, gather_flips(columns)):
        first = (column ^ flip) // repeat * own
        for slot in range(own):
            for side in range(2):
                out[side, slot] = by_group[first + slot, side]


def pack(cache, columns, own):
    share, _, groups, width = cache.shape
    slice_shape = jax.ShapeDtypeStruct((2, own, share, width), jnp.bfloat16)
    return pl.pallas_call(
        functools.partial(pack_kernel, columns),
        out_shape=[slice_shape] * columns,
        scratch_shapes=[pltpu.VMEM((groups, 2, share, width), jnp.bfloat16)],
        compiler_params=pltpu.CompilerParams(vmem_limit_bytes=16 * MIB),
        name="pack",
    )(cache)


LOG2E = math.log2(math.e)
ACROSS = (((1,), (1,)), ((), ()))
ALONG = (((1,), (0,)), ((), ()))


def load_pairs(pair_refs, keys, values):
    columns, _, own, share, width = pair_refs[0].shape
    length = columns * share
    for piece, pair_ref in enumerate(pair_refs):
        at = pl.ds(piece * length, length)
        for slot in range(own):
            keys[slot, at] = pair_ref[:, 0, slot].reshape(length, width)
            values[slot, at] = pair_ref[:, 1, slot].reshape(length, width)


def interleave(passes, *products):
    products = [product for some in products for product in some]
    steps = passes[0]
    done = 0
    for number, step in enumerate(passes[1]):
        while done < len(products) and done * steps <= number * len(products):
            products[done]()
            done += 1
    for product in products[done:]:
        product()


def score_products(keys, values, slot, queries_ref, grads_ref, tile, scores, slopes, tops):
    def product(rows, left, right_ref, out):
        def run():
            found = lax.dot_general(
                left[slot], right_ref[tile, rows], ACROSS, preferred_element_type=jnp.float32
            )
            out[:, rows] = found
            if out is scores:
                tops[:, rows] = jnp.max(found.reshape(-1, 8, found.shape[1]), axis=0)

        return run

    products = []
    for start in range(0, scores.shape[1], DOT_ROWS):
        rows = pl.ds(start, DOT_ROWS)
        products.append(product(rows, keys, queries_ref, scores))
        products.append(product(rows, values, grads_ref, slopes))
    return products


def gradient_products(
    key_total, value_total, per_group, weights, dscores, queries_ref, grads_ref, tile
):
    slot = tile // per_group

    def product(total, left, right_ref):
        def run():
            part = lax.dot_general(
                left[...], right_ref[tile], ALONG, preferred_element_type=jnp.float32
            )
            total[slot] = total[slot] + part if tile % per_group else part

        return run

    return [
        product(key_total, dscores, queries_ref),
        product(value_total, weights, grads_ref),
    ]


def cuts_of(ref):
    return [pl.ds(start, CHUNK) for start in range(0, ref.shape[0], CHUNK)]


def exponentiate(scores, slopes, factor, peak, kept, result):
    total = None
    dotted = None
    for cut in cuts_of(scores):
        shifted = jnp.exp2(scores[cut] * factor - peak)
        product = shifted * slopes[cut]
        kept[cut] = shifted
        total = shifted if total is None else total + shifted
        dotted = product if dotted is None else dotted + product
        yield
    result.append(jnp.sum(total, axis=0, keepdims=True))
    result.append(jnp.sum(dotted, axis=0, keepdims=True))


def weigh(kept, slopes, inverse, delta, weights, dscores):
    for cut in cuts_of(weights):
        probability = kept[cut] * inverse
        weights[cut] = probability.astype(jnp.bfloat16)
        dscores[cut] = (probability * (slopes[cut] - delta)).astype(jnp.bfloat16)
        yield


def first_half_kernel(score_scale, per_group, pieces, *refs):
    pair_refs, refs = refs[:pieces][::-1], refs[pieces:]
    queries_ref, grads_ref, lse_ref, dot_ref = refs[:4]
    kept, (peak_ref, total_ref, dotted_ref, keys, values) = refs[4:8], refs[8:13]
    even, odd = refs[13:15], refs[15:17]
    tiles = queries_ref.shape[0]
    factor = score_scale * LOG2E
    load_pairs(pair_refs, keys, values)

    def place(parity, step):
        scores, tops = odd if parity else even
        return scores, kept[2 * parity].at[step], kept[2 * parity + 1].at[step], tops

    def products(tile, parity, step):
        scores, _, slopes, tops = place(parity, step)
        slot = tile // per_group
        return score_products(
            keys, values, slot, queries_ref, grads_ref, tile, scores, slopes, tops
        )

    def normalize(tile, parity, step):
        scores, shifted, slopes, tops = place(parity, step)

        def passes():
            side_lse = lse_ref[pl.ds(tile, 1)] * LOG2E
            peak = jnp.max(tops[...], axis=0, keepdims=True) * factor
            peak = jnp.maximum(peak, side_lse)
            sums = []
            yield from exponentiate(scores, slopes, factor, peak, shifted, sums)
            side = jnp.exp2(side_lse - peak)
            peak_ref[tile] = peak
            total_ref[tile] = sums[0] + side
            dotted_ref[tile] = sums[1] + side * dot_ref[pl.ds(tile, 1)]

        return len(cuts_of(scores)), passes()

    for product in products(0, 0, 0):
        product()

    def two_tiles(step):
        interleave(normalize(2 * step, 0, step), products(2 * step + 1, 1, step))
        interleave(normalize(2 * step + 1, 1, step), products(2 * step + 2, 0, step + 1))

    last = tiles // 2 - 1
    for step in range(last):
        two_tiles(step)
    interleave(normalize(tiles - 2, 0, last), products(tiles - 1, 1, last))
    interleave(normalize(tiles - 1, 1, last))


def first_half(pairs, queries, grads, lse_rows, dot_rows, score_scale):
    columns, _, own, share, width = pairs[0].shape
    positions = len(pairs) * columns * share
    tiles, row_tile, _ = queries.shape
    kept = [jax.ShapeDtypeStruct((tiles // 2, positions, row_tile), jnp.float32)] * 2
    buffers = [
        pltpu.VMEM((positions, row_tile), jnp.float32),
        pltpu.VMEM((8, row_tile), jnp.float32),
    ]
    stat = jax.ShapeDtypeStruct((tiles, 1, row_tile), jnp.float32)
    return pl.pallas_call(
        functools.partial(first_half_kernel, score_scale, tiles // own, len(pairs)),
        out_shape=kept + kept + [stat] * 3,
        scratch_shapes=[
            pltpu.VMEM((own, positions, width), jnp.bfloat16),
            pltpu.VMEM((own, positions, width), jnp.bfloat16),
        ]
        + buffers
        + buffers,
        compiler_params=pltpu.CompilerParams(vmem_limit_bytes=30 * MIB),
        cost_estimate=pl.CostEstimate(
            flops=4 * tiles * row_tile * positions * width,
            bytes_accessed=8 * tiles * row_tile * positions,
            transcendentals=tiles * row_tile * positions,
        ),
        name="first_half",
    )(*pairs[::-1], queries, grads, lse_rows, dot_rows)


def second_half_kernel(score_scale, per_group, pieces, *refs):
    pair_refs, refs = refs[:pieces], refs[pieces:]
    queries_ref, grads_ref, peak_ref, total_ref, dotted_ref = refs[:5]
    out_ref, inverse_ref, delta_ref = refs[5:8]
    keys, values, key_total, value_total = refs[8:12]
    even, odd = refs[12:17], refs[17:22]
    _, columns, _, own, share, width = out_ref.shape
    tiles = queries_ref.shape[0]
    factor = score_scale * LOG2E
    load_pairs(pair_refs, keys, values)

    def products(tile, buffers):
        slot = tile // per_group
        return score_products(keys, values, slot, queries_ref, grads_ref, tile, *buffers[:3])

    def normalize(tile, buffers):
        scores, slopes, tops, weights, dscores = buffers

        def passes():
            first_peak = peak_ref[tile]
            peak = jnp.max(tops[...], axis=0, keepdims=True) * factor
            peak = jnp.maximum(peak, first_peak)
            sums = []
            yield from exponentiate(scores, slopes, factor, peak, scores, sums)
            rescale = jnp.exp2(first_peak - peak)
            inverse = 1.0 / (sums[0] + total_ref[tile] * rescale)
            delta = (sums[1] + dotted_ref[tile] * rescale) * inverse
            inverse_ref[tile] = inverse * rescale
            delta_ref[tile] = delta
            yield from weigh(scores, slopes, inverse, delta, weights, dscores)

        return 2 * len(cuts_of(scores)), passes()

    def gather(tile, buffers):
        return gradient_products(
            key_total,
            value_total,
            per_group,
            *buffers[3:],
            queries_ref,
            grads_ref,
            tile,
        )

    for product in products(0, even):
        product()
    interleave(normalize(0, even), products(1, odd))

    def two_tiles(step):
        tile = step * 2
        interleave(normalize(tile + 1, odd), products(tile + 2, even), gather(tile, even))
        interleave(normalize(tile + 2, even), products(tile + 3, odd), gather(tile + 1, odd))

    for step in range(tiles // 2 - 1):
        two_tiles(step)
    interleave(normalize(tiles - 1, odd), gather(tiles - 2, even))
    for product in gather(tiles - 1, odd):
        product()
    shape = out_ref.shape[:2] + (share, width)
    for slot in range(own):
        key_sum = key_total[slot] * score_scale
        out_ref[:, :, 0, slot] = key_sum.astype(jnp.bfloat16).reshape(shape)
        out_ref[:, :, 1, slot] = value_total[slot].astype(jnp.bfloat16).reshape(shape)


def second_half(pairs, queries, grads, stats, score_scale):
    columns, _, own, share, width = pairs[0].shape
    positions = len(pairs) * columns * share
    tiles, row_tile, _ = queries.shape
    stat = jax.ShapeDtypeStruct((tiles, 1, row_tile), jnp.float32)
    buffers = [
        pltpu.VMEM((positions, row_tile), jnp.float32),
        pltpu.VMEM((positions, row_tile), jnp.float32),
        pltpu.VMEM((8, row_tile), jnp.float32),
        pltpu.VMEM((positions, row_tile), jnp.bfloat16),
        pltpu.VMEM((positions, row_tile), jnp.bfloat16),
    ]
    return pl.pallas_call(
        functools.partial(second_half_kernel, score_scale, tiles // own, len(pairs)),
        out_shape=(
            jax.ShapeDtypeStruct((len(pairs),) + pairs[0].shape, jnp.bfloat16),
            stat,
            stat,
        ),
        scratch_shapes=[
            pltpu.VMEM((own, positions, width), jnp.bfloat16),
            pltpu.VMEM((own, positions, width), jnp.bfloat16),
            pltpu.VMEM((own, positions, width), jnp.float32),
            pltpu.VMEM((own, positions, width), jnp.float32),
        ]
        + buffers
        + buffers,
        compiler_params=pltpu.CompilerParams(vmem_limit_bytes=30 * MIB),
        cost_estimate=pl.CostEstimate(
            flops=8 * tiles * row_tile * positions * width,
            bytes_accessed=4 * tiles * row_tile * width,
            transcendentals=tiles * row_tile * positions,
        ),
        name="second_half",
    )(*pairs, queries, grads, *stats)


def finish_kernel(score_scale, per_group, *refs):
    kept, refs = refs[:4], refs[4:]
    queries_ref, grads_ref, inverse_ref, delta_ref, out_ref = refs[:5]
    key_total, value_total = refs[5:7]
    even, odd = refs[7:9], refs[9:11]
    _, columns, _, own, share, width = out_ref.shape
    tiles = queries_ref.shape[0]

    def spread(tile, parity, step, buffers):
        steps = weigh(
            kept[2 * parity].at[step],
            kept[2 * parity + 1].at[step],
            inverse_ref[tile],
            delta_ref[tile],
            *buffers,
        )
        return len(cuts_of(buffers[0])), steps

    def gather(tile, buffers):
        return gradient_products(
            key_total, value_total, per_group, *buffers, queries_ref, grads_ref, tile
        )

    interleave(spread(0, 0, 0, even))

    def two_tiles(step):
        interleave(spread(2 * step + 1, 1, step, odd), gather(2 * step, even))
        interleave(spread(2 * step + 2, 0, step + 1, even), gather(2 * step + 1, odd))

    last = tiles // 2 - 1
    for step in range(last):
        two_tiles(step)
    interleave(spread(tiles - 1, 1, last, odd), gather(tiles - 2, even))
    for product in gather(tiles - 1, odd):
        product()
    shape = out_ref.shape[:2] + (share, width)
    for slot in range(own):
        out_ref[:, :, 0, slot] = (key_total[slot] * score_scale).reshape(shape)
        out_ref[:, :, 1, slot] = value_total[slot].reshape(shape)


def finish(kept, queries, grads, inverse, delta, shape, score_scale):
    _, positions, row_tile = kept[0].shape
    own, width = shape[3], shape[5]
    tiles = queries.shape[0]
    buffers = [pltpu.VMEM((positions, row_tile), jnp.bfloat16)] * 4
    return pl.pallas_call(
        functools.partial(finish_kernel, score_scale, tiles // own),
        out_shape=jax.ShapeDtypeStruct(shape, jnp.float32),
        scratch_shapes=[
            pltpu.VMEM((own, positions, width), jnp.float32),
            pltpu.VMEM((own, positions, width), jnp.float32),
        ]
        + buffers,
        compiler_params=pltpu.CompilerParams(vmem_limit_bytes=30 * MIB),
        cost_estimate=pl.CostEstimate(
            flops=4 * tiles * row_tile * positions * width,
            bytes_accessed=8 * tiles * row_tile * positions,
            transcendentals=0,
        ),
        name="finish",
    )(*kept, queries, grads, inverse, delta)


def chip_sum_kernel(mine_ref, mate_ref, *outs):
    for offset, out in enumerate(outs):
        out[...] = (mine_ref[offset] + mate_ref[offset].astype(jnp.float32)).astype(out.dtype)


def chip_sum(mine, mate):
    chips = mine.shape[0]
    shape = mine.shape[1:]
    return pl.pallas_call(
        chip_sum_kernel,
        out_shape=[
            jax.ShapeDtypeStruct(shape, jnp.bfloat16 if flip else jnp.float32)
            for flip in flips(chips)
        ],
        compiler_params=pltpu.CompilerParams(vmem_limit_bytes=16 * MIB),
        name="chip_sum",
    )(mine, mate)


def column_sum_kernel(away, mine_ref, *refs):
    others, outs = refs[:away], refs[away:]
    columns = len(outs)
    for out, flip in zip(outs, flips(columns)):
        place = gather_flips(columns).index(flip)
        total = mine_ref[place]
        for other in others:
            total = total + other[place].astype(jnp.float32)
        out[...] = total.astype(out.dtype)


def column_sum(mine, others):
    columns = mine.shape[0]
    shape = mine.shape[1:]
    return pl.pallas_call(
        functools.partial(column_sum_kernel, len(others)),
        out_shape=[
            jax.ShapeDtypeStruct(shape, jnp.bfloat16 if flip else jnp.float32)
            for flip in flips(columns)
        ],
        compiler_params=pltpu.CompilerParams(vmem_limit_bytes=16 * MIB),
        name="column_sum",
    )(mine, *others)


def adam_kernel(columns, *refs):
    parts, refs = refs[:columns], refs[columns:]
    cache_ref, first_ref, second_ref, new_cache, new_first, new_second = refs[:6]
    by_flip, gathered = refs[6:]
    groups = cache_ref.shape[2]
    own = parts[0].shape[1]
    repeat = own * columns // groups
    for part, flip in zip(parts, flips(columns)):
        by_flip[flip] = part[...].astype(jnp.float32)
    column = lax.axis_index("cache")
    for side in range(2):
        for group in range(groups):
            first_owner = group // own * repeat
            slot = group % own
            total = by_flip[column ^ first_owner, side, slot]
            for owner in range(first_owner + 1, first_owner + repeat):
                total = total + by_flip[column ^ owner, side, slot]
            gathered[:, side, group] = total
    gradient = gathered[...]
    first = beta_first * first_ref[...] + (1.0 - beta_first) * gradient
    second = beta_second * second_ref[...] + (1.0 - beta_second) * gradient * gradient
    first_hat = first / (1.0 - beta_first**STEP)
    second_hat = second / (1.0 - beta_second**STEP)
    new_cache[...] = cache_ref[...] - learn_rate * first_hat / (jnp.sqrt(second_hat) + epsilon)
    new_first[...] = first
    new_second[...] = second


def adam(parts, cache, first_moment, second_moment):
    shape = jax.ShapeDtypeStruct(cache.shape, jnp.float32)
    return pl.pallas_call(
        functools.partial(adam_kernel, len(parts)),
        out_shape=(shape, shape, shape),
        scratch_shapes=[
            pltpu.VMEM((len(parts),) + parts[0].shape, jnp.float32),
            pltpu.VMEM(cache.shape, jnp.float32),
        ],
        compiler_params=pltpu.CompilerParams(vmem_limit_bytes=16 * MIB),
        name="adam",
    )(*parts, cache, first_moment, second_moment)


def swap(value, axis, size, flip):
    return lax.ppermute(value, axis, [(place, place ^ flip) for place in range(size)])


def swap_all(values, axis, size, stride, order=flips):
    return [
        swap(value, axis, size, flip * stride) if flip else value
        for value, flip in zip(values, order(len(values)))
    ]


def per_device(
    dp_size, columns, queries, out_grad, self_lse, self_dot, cache, first_moment, second_moment
):
    _, _, groups, width = cache.shape
    tokens, heads, _ = queries.shape
    chips = dp_size // 2
    group_size = heads // groups
    score_scale = 1.0 / math.sqrt(width)
    own = max(1, groups // columns)
    repeat = own * columns // groups
    own_tokens = tokens // repeat
    column = lax.axis_index("cache")
    first_group = column // repeat * own
    first_token = column % repeat * own_tokens

    slices = pack(cache, columns, own)
    gathered = jnp.stack(swap_all(slices, "cache", columns, 1, gather_flips))
    pairs = swap_all([gathered] * chips, "dp", dp_size, 2)
    def tiles_of(array):
        parts = array.reshape((tokens, groups, group_size) + array.shape[2:])
        part = lax.dynamic_slice_in_dim(parts, first_token, own_tokens, 0)
        part = lax.dynamic_slice_in_dim(part, first_group, own, 1)
        return jnp.moveaxis(part, 1, 0).reshape((-1, ROW_TILE) + array.shape[2:])

    tiles = [tiles_of(queries), tiles_of(out_grad)]
    tiles += [tiles_of(self_lse), tiles_of(self_dot)]
    own_pair, tiles = lax.optimization_barrier((pairs[-1], tiles))
    query_tiles, grad_tiles, lse_rows, dot_rows = tiles
    mate_pairs = [swap(pair, "dp", dp_size, 1) for pair in pairs[:-1] + [own_pair]]
    *kept, peak, total, dotted = first_half(
        pairs, query_tiles, grad_tiles, lse_rows, dot_rows, score_scale
    )
    mate, inverse, delta = second_half(
        mate_pairs, query_tiles, grad_tiles, (peak, total, dotted), score_scale
    )
    from_mate = swap(mate, "dp", dp_size, 1)
    mine = finish(kept, query_tiles, grad_tiles, inverse, delta, mate.shape, score_scale)
    by_chip = chip_sum(mine, from_mate)
    *away, home = swap_all(by_chip, "dp", dp_size, 2)
    by_column = column_sum(home, away)
    parts = swap_all(by_column, "cache", columns, 1)
    return adam(parts, cache, first_moment, second_moment)


def solution(mesh):
    in_specs = (
        P("dp", None, None),
        P("dp", None, None),
        P("dp", None),
        P("dp", None),
        P(("dp", "cache"), None, None, None),
        P(("dp", "cache"), None, None, None),
        P(("dp", "cache"), None, None, None),
    )
    out_specs = (
        P(("dp", "cache"), None, None, None),
        P(("dp", "cache"), None, None, None),
        P(("dp", "cache"), None, None, None),
    )
    return jax.shard_map(
        functools.partial(per_device, mesh.shape["dp"], mesh.shape["cache"]),
        mesh=mesh,
        in_specs=in_specs,
        out_specs=out_specs,
        check_vma=False,
    )
```

```python
import functools
import math

import jax
import jax.numpy as jnp
from jax import lax
from jax.experimental import pallas as pl
from jax.experimental.pallas import tpu as pltpu
from jax.sharding import PartitionSpec as P

STEP = 200

learn_rate = 0.02
beta_first = 0.9
beta_second = 0.999
epsilon = 1e-08

ROW_TILE = 256
CHUNK = 32
DOT_ROWS = 256
MIB = 1024 * 1024


def flips(size):
    return list(range(size - 1, -1, -1))


def gather_flips(columns):
    return flips(columns)[1::-1] + flips(columns)[2:]


def pack_kernel(columns, cache_ref, *refs):
    *outs, by_group = refs
    groups = cache_ref.shape[2]
    own = outs[0].shape[1]
    repeat = own * columns // groups
    for side in range(2):
        for group in range(groups):
            by_group[group, side] = cache_ref[:, side, group].astype(jnp.bfloat16)
    column = lax.axis_index("cache")
    for out, flip in zip(outs, gather_flips(columns)):
        first = (column ^ flip) // repeat * own
        for slot in range(own):
            for side in range(2):
                out[side, slot] = by_group[first + slot, side]


def pack(cache, columns, own):
    share, _, groups, width = cache.shape
    slice_shape = jax.ShapeDtypeStruct((2, own, share, width), jnp.bfloat16)
    return pl.pallas_call(
        functools.partial(pack_kernel, columns),
        out_shape=[slice_shape] * columns,
        scratch_shapes=[pltpu.VMEM((groups, 2, share, width), jnp.bfloat16)],
        compiler_params=pltpu.CompilerParams(vmem_limit_bytes=16 * MIB),
        name="pack",
    )(cache)


LOG2E = math.log2(math.e)
ACROSS = (((1,), (1,)), ((), ()))
ALONG = (((1,), (0,)), ((), ()))


def load_pairs(pair_refs, keys, values):
    columns, _, own, share, width = pair_refs[0].shape
    length = columns * share
    for piece, pair_ref in enumerate(pair_refs):
        at = pl.ds(piece * length, length)
        for slot in range(own):
            keys[slot, at] = pair_ref[:, 0, slot].reshape(length, width)
            values[slot, at] = pair_ref[:, 1, slot].reshape(length, width)


def interleave(passes, *products):
    products = [product for some in products for product in some]
    steps = passes[0]
    done = 0
    for number, step in enumerate(passes[1]):
        while done < len(products) and done * steps <= number * len(products):
            products[done]()
            done += 1
    for product in products[done:]:
        product()


def score_products(keys, values, slot, queries_ref, grads_ref, tile, scores, slopes, tops):
    def product(rows, left, right_ref, out):
        def run():
            found = lax.dot_general(
                left[slot], right_ref[tile, rows], ACROSS, preferred_element_type=jnp.float32
            )
            out[:, rows] = found
            if out is scores:
                tops[:, rows] = jnp.max(found.reshape(-1, 8, found.shape[1]), axis=0)

        return run

    products = []
    for start in range(0, scores.shape[1], DOT_ROWS):
        rows = pl.ds(start, DOT_ROWS)
        products.append(product(rows, keys, queries_ref, scores))
        products.append(product(rows, values, grads_ref, slopes))
    return products


def gradient_products(
    key_total, value_total, per_group, weights, dscores, queries_ref, grads_ref, tile
):
    slot = tile // per_group

    def product(total, left, right_ref):
        def run():
            part = lax.dot_general(
                left[...], right_ref[tile], ALONG, preferred_element_type=jnp.float32
            )
            total[slot] = total[slot] + part if tile % per_group else part

        return run

    return [
        product(key_total, dscores, queries_ref),
        product(value_total, weights, grads_ref),
    ]


def cuts_of(ref):
    return [pl.ds(start, CHUNK) for start in range(0, ref.shape[0], CHUNK)]


def exponentiate(scores, slopes, factor, peak, kept, result):
    total = None
    dotted = None
    for cut in cuts_of(scores):
        shifted = jnp.exp2(scores[cut] * factor - peak)
        product = shifted * slopes[cut]
        kept[cut] = shifted
        total = shifted if total is None else total + shifted
        dotted = product if dotted is None else dotted + product
        yield
    result.append(jnp.sum(total, axis=0, keepdims=True))
    result.append(jnp.sum(dotted, axis=0, keepdims=True))


def weigh(kept, slopes, inverse, delta, weights, dscores):
    for cut in cuts_of(weights):
        probability = kept[cut] * inverse
        weights[cut] = probability.astype(jnp.bfloat16)
        dscores[cut] = (probability * (slopes[cut] - delta)).astype(jnp.bfloat16)
        yield


def first_half_kernel(score_scale, per_group, pieces, *refs):
    pair_refs, refs = refs[:pieces][::-1], refs[pieces:]
    queries_ref, grads_ref, lse_ref, dot_ref = refs[:4]
    kept, (peak_ref, total_ref, dotted_ref, keys, values) = refs[4:8], refs[8:13]
    even, odd = refs[13:15], refs[15:17]
    tiles = queries_ref.shape[0]
    factor = score_scale * LOG2E
    load_pairs(pair_refs, keys, values)

    def place(parity, step):
        scores, tops = odd if parity else even
        return scores, kept[2 * parity].at[step], kept[2 * parity + 1].at[step], tops

    def products(tile, parity, step):
        scores, _, slopes, tops = place(parity, step)
        slot = tile // per_group
        return score_products(
            keys, values, slot, queries_ref, grads_ref, tile, scores, slopes, tops
        )

    def normalize(tile, parity, step):
        scores, shifted, slopes, tops = place(parity, step)

        def passes():
            side_lse = lse_ref[pl.ds(tile, 1)] * LOG2E
            peak = jnp.max(tops[...], axis=0, keepdims=True) * factor
            peak = jnp.maximum(peak, side_lse)
            sums = []
            yield from exponentiate(scores, slopes, factor, peak, shifted, sums)
            side = jnp.exp2(side_lse - peak)
            peak_ref[tile] = peak
            total_ref[tile] = sums[0] + side
            dotted_ref[tile] = sums[1] + side * dot_ref[pl.ds(tile, 1)]

        return len(cuts_of(scores)), passes()

    for product in products(0, 0, 0):
        product()

    def two_tiles(step):
        interleave(normalize(2 * step, 0, step), products(2 * step + 1, 1, step))
        interleave(normalize(2 * step + 1, 1, step), products(2 * step + 2, 0, step + 1))

    last = tiles // 2 - 1
    for step in range(last):
        two_tiles(step)
    interleave(normalize(tiles - 2, 0, last), products(tiles - 1, 1, last))
    interleave(normalize(tiles - 1, 1, last))


def first_half(pairs, queries, grads, lse_rows, dot_rows, score_scale):
    columns, _, own, share, width = pairs[0].shape
    positions = len(pairs) * columns * share
    tiles, row_tile, _ = queries.shape
    kept = [jax.ShapeDtypeStruct((tiles // 2, positions, row_tile), jnp.float32)] * 2
    buffers = [
        pltpu.VMEM((positions, row_tile), jnp.float32),
        pltpu.VMEM((8, row_tile), jnp.float32),
    ]
    stat = jax.ShapeDtypeStruct((tiles, 1, row_tile), jnp.float32)
    return pl.pallas_call(
        functools.partial(first_half_kernel, score_scale, tiles // own, len(pairs)),
        out_shape=kept + kept + [stat] * 3,
        scratch_shapes=[
            pltpu.VMEM((own, positions, width), jnp.bfloat16),
            pltpu.VMEM((own, positions, width), jnp.bfloat16),
        ]
        + buffers
        + buffers,
        compiler_params=pltpu.CompilerParams(vmem_limit_bytes=30 * MIB),
        cost_estimate=pl.CostEstimate(
            flops=4 * tiles * row_tile * positions * width,
            bytes_accessed=8 * tiles * row_tile * positions,
            transcendentals=tiles * row_tile * positions,
        ),
        name="first_half",
    )(*pairs[::-1], queries, grads, lse_rows, dot_rows)


def second_half_kernel(score_scale, per_group, pieces, *refs):
    pair_refs, refs = refs[:pieces], refs[pieces:]
    queries_ref, grads_ref, peak_ref, total_ref, dotted_ref = refs[:5]
    out_ref, inverse_ref, delta_ref = refs[5:8]
    keys, values, key_total, value_total = refs[8:12]
    even, odd = refs[12:17], refs[17:22]
    _, columns, _, own, share, width = out_ref.shape
    tiles = queries_ref.shape[0]
    factor = score_scale * LOG2E
    load_pairs(pair_refs, keys, values)

    def products(tile, buffers):
        slot = tile // per_group
        return score_products(keys, values, slot, queries_ref, grads_ref, tile, *buffers[:3])

    def normalize(tile, buffers):
        scores, slopes, tops, weights, dscores = buffers

        def passes():
            first_peak = peak_ref[tile]
            peak = jnp.max(tops[...], axis=0, keepdims=True) * factor
            peak = jnp.maximum(peak, first_peak)
            sums = []
            yield from exponentiate(scores, slopes, factor, peak, scores, sums)
            rescale = jnp.exp2(first_peak - peak)
            inverse = 1.0 / (sums[0] + total_ref[tile] * rescale)
            delta = (sums[1] + dotted_ref[tile] * rescale) * inverse
            inverse_ref[tile] = inverse * rescale
            delta_ref[tile] = delta
            yield from weigh(scores, slopes, inverse, delta, weights, dscores)

        return 2 * len(cuts_of(scores)), passes()

    def gather(tile, buffers):
        return gradient_products(
            key_total,
            value_total,
            per_group,
            *buffers[3:],
            queries_ref,
            grads_ref,
            tile,
        )

    for product in products(0, even):
        product()
    interleave(normalize(0, even), products(1, odd))

    def two_tiles(step):
        tile = step * 2
        interleave(normalize(tile + 1, odd), products(tile + 2, even), gather(tile, even))
        interleave(normalize(tile + 2, even), products(tile + 3, odd), gather(tile + 1, odd))

    for step in range(tiles // 2 - 1):
        two_tiles(step)
    interleave(normalize(tiles - 1, odd), gather(tiles - 2, even))
    for product in gather(tiles - 1, odd):
        product()
    shape = out_ref.shape[:2] + (share, width)
    for slot in range(own):
        key_sum = key_total[slot] * score_scale
        out_ref[:, :, 0, slot] = key_sum.astype(jnp.bfloat16).reshape(shape)
        out_ref[:, :, 1, slot] = value_total[slot].astype(jnp.bfloat16).reshape(shape)


def second_half(pairs, queries, grads, stats, score_scale):
    columns, _, own, share, width = pairs[0].shape
    positions = len(pairs) * columns * share
    tiles, row_tile, _ = queries.shape
    stat = jax.ShapeDtypeStruct((tiles, 1, row_tile), jnp.float32)
    buffers = [
        pltpu.VMEM((positions, row_tile), jnp.float32),
        pltpu.VMEM((positions, row_tile), jnp.float32),
        pltpu.VMEM((8, row_tile), jnp.float32),
        pltpu.VMEM((positions, row_tile), jnp.bfloat16),
        pltpu.VMEM((positions, row_tile), jnp.bfloat16),
    ]
    return pl.pallas_call(
        functools.partial(second_half_kernel, score_scale, tiles // own, len(pairs)),
        out_shape=(
            jax.ShapeDtypeStruct((len(pairs),) + pairs[0].shape, jnp.bfloat16),
            stat,
            stat,
        ),
        scratch_shapes=[
            pltpu.VMEM((own, positions, width), jnp.bfloat16),
            pltpu.VMEM((own, positions, width), jnp.bfloat16),
            pltpu.VMEM((own, positions, width), jnp.float32),
            pltpu.VMEM((own, positions, width), jnp.float32),
        ]
        + buffers
        + buffers,
        compiler_params=pltpu.CompilerParams(vmem_limit_bytes=30 * MIB),
        cost_estimate=pl.CostEstimate(
            flops=8 * tiles * row_tile * positions * width,
            bytes_accessed=4 * tiles * row_tile * width,
            transcendentals=tiles * row_tile * positions,
        ),
        name="second_half",
    )(*pairs, queries, grads, *stats)


def finish_kernel(score_scale, per_group, *refs):
    kept, refs = refs[:4], refs[4:]
    queries_ref, grads_ref, inverse_ref, delta_ref, out_ref = refs[:5]
    key_total, value_total = refs[5:7]
    even, odd = refs[7:9], refs[9:11]
    _, columns, _, own, share, width = out_ref.shape
    tiles = queries_ref.shape[0]

    def spread(tile, parity, step, buffers):
        steps = weigh(
            kept[2 * parity].at[step],
            kept[2 * parity + 1].at[step],
            inverse_ref[tile],
            delta_ref[tile],
            *buffers,
        )
        return len(cuts_of(buffers[0])), steps

    def gather(tile, buffers):
        return gradient_products(
            key_total, value_total, per_group, *buffers, queries_ref, grads_ref, tile
        )

    interleave(spread(0, 0, 0, even))

    def two_tiles(step):
        interleave(spread(2 * step + 1, 1, step, odd), gather(2 * step, even))
        interleave(spread(2 * step + 2, 0, step + 1, even), gather(2 * step + 1, odd))

    last = tiles // 2 - 1
    for step in range(last):
        two_tiles(step)
    interleave(spread(tiles - 1, 1, last, odd), gather(tiles - 2, even))
    for product in gather(tiles - 1, odd):
        product()
    shape = out_ref.shape[:2] + (share, width)
    for slot in range(own):
        out_ref[:, :, 0, slot] = (key_total[slot] * score_scale).reshape(shape)
        out_ref[:, :, 1, slot] = value_total[slot].reshape(shape)


def finish(kept, queries, grads, inverse, delta, shape, score_scale):
    _, positions, row_tile = kept[0].shape
    own, width = shape[3], shape[5]
    tiles = queries.shape[0]
    buffers = [pltpu.VMEM((positions, row_tile), jnp.bfloat16)] * 4
    return pl.pallas_call(
        functools.partial(finish_kernel, score_scale, tiles // own),
        out_shape=jax.ShapeDtypeStruct(shape, jnp.float32),
        scratch_shapes=[
            pltpu.VMEM((own, positions, width), jnp.float32),
            pltpu.VMEM((own, positions, width), jnp.float32),
        ]
        + buffers,
        compiler_params=pltpu.CompilerParams(vmem_limit_bytes=30 * MIB),
        cost_estimate=pl.CostEstimate(
            flops=4 * tiles * row_tile * positions * width,
            bytes_accessed=8 * tiles * row_tile * positions,
            transcendentals=0,
        ),
        name="finish",
    )(*kept, queries, grads, inverse, delta)


def chip_sum_kernel(mine_ref, mate_ref, *outs):
    for offset, out in enumerate(outs):
        out[...] = (mine_ref[offset] + mate_ref[offset].astype(jnp.float32)).astype(out.dtype)


def chip_sum(mine, mate):
    chips = mine.shape[0]
    shape = mine.shape[1:]
    return pl.pallas_call(
        chip_sum_kernel,
        out_shape=[
            jax.ShapeDtypeStruct(shape, jnp.bfloat16 if flip else jnp.float32)
            for flip in flips(chips)
        ],
        compiler_params=pltpu.CompilerParams(vmem_limit_bytes=16 * MIB),
        name="chip_sum",
    )(mine, mate)


def column_sum_kernel(away, mine_ref, *refs):
    others, outs = refs[:away], refs[away:]
    columns = len(outs)
    for out, flip in zip(outs, flips(columns)):
        place = gather_flips(columns).index(flip)
        total = mine_ref[place]
        for other in others:
            total = total + other[place].astype(jnp.float32)
        out[...] = total.astype(out.dtype)


def column_sum(mine, others):
    columns = mine.shape[0]
    shape = mine.shape[1:]
    return pl.pallas_call(
        functools.partial(column_sum_kernel, len(others)),
        out_shape=[
            jax.ShapeDtypeStruct(shape, jnp.bfloat16 if flip else jnp.float32)
            for flip in flips(columns)
        ],
        compiler_params=pltpu.CompilerParams(vmem_limit_bytes=16 * MIB),
        name="column_sum",
    )(mine, *others)


def adam_kernel(columns, *refs):
    parts, refs = refs[:columns], refs[columns:]
    cache_ref, first_ref, second_ref, new_cache, new_first, new_second = refs[:6]
    by_flip, gathered = refs[6:]
    groups = cache_ref.shape[2]
    own = parts[0].shape[1]
    repeat = own * columns // groups
    for part, flip in zip(parts, flips(columns)):
        by_flip[flip] = part[...].astype(jnp.float32)
    column = lax.axis_index("cache")
    for side in range(2):
        for group in range(groups):
            first_owner = group // own * repeat
            slot = group % own
            total = by_flip[column ^ first_owner, side, slot]
            for owner in range(first_owner + 1, first_owner + repeat):
                total = total + by_flip[column ^ owner, side, slot]
            gathered[:, side, group] = total
    gradient = gathered[...]
    first = beta_first * first_ref[...] + (1.0 - beta_first) * gradient
    second = beta_second * second_ref[...] + (1.0 - beta_second) * gradient * gradient
    first_hat = first / (1.0 - beta_first**STEP)
    second_hat = second / (1.0 - beta_second**STEP)
    new_cache[...] = cache_ref[...] - learn_rate * first_hat / (jnp.sqrt(second_hat) + epsilon)
    new_first[...] = first
    new_second[...] = second


def adam(parts, cache, first_moment, second_moment):
    shape = jax.ShapeDtypeStruct(cache.shape, jnp.float32)
    return pl.pallas_call(
        functools.partial(adam_kernel, len(parts)),
        out_shape=(shape, shape, shape),
        scratch_shapes=[
            pltpu.VMEM((len(parts),) + parts[0].shape, jnp.float32),
            pltpu.VMEM(cache.shape, jnp.float32),
        ],
        compiler_params=pltpu.CompilerParams(vmem_limit_bytes=16 * MIB),
        name="adam",
    )(*parts, cache, first_moment, second_moment)


def swap(value, axis, size, flip):
    return lax.ppermute(value, axis, [(place, place ^ flip) for place in range(size)])


def swap_all(values, axis, size, stride, order=flips):
    return [
        swap(value, axis, size, flip * stride) if flip else value
        for value, flip in zip(values, order(len(values)))
    ]


def chip_flips(chips, core):
    far, *others, own = flips(chips)
    return [far] + (others[::-1] if core else others) + [own]


def chips_swap(values, dp_size):
    chips = dp_size // 2
    orders = [chip_flips(chips, core) for core in range(2)]
    arrived = [
        lax.ppermute(
            value, "dp", [(place, place ^ (2 * orders[place % 2][j])) for place in range(dp_size)]
        )
        for j, value in enumerate(values[:-1])
    ]
    return arrived + [values[-1]]


def per_device(
    dp_size, columns, queries, out_grad, self_lse, self_dot, cache, first_moment, second_moment
):
    _, _, groups, width = cache.shape
    tokens, heads, _ = queries.shape
    chips = dp_size // 2
    group_size = heads // groups
    score_scale = 1.0 / math.sqrt(width)
    own = max(1, groups // columns)
    repeat = own * columns // groups
    own_tokens = tokens // repeat
    column = lax.axis_index("cache")
    first_group = column // repeat * own
    first_token = column % repeat * own_tokens

    slices = pack(cache, columns, own)
    gathered = jnp.stack(swap_all(slices, "cache", columns, 1, gather_flips))
    pairs = chips_swap([gathered] * chips, dp_size)
    def tiles_of(array):
        parts = array.reshape((tokens, groups, group_size) + array.shape[2:])
        part = lax.dynamic_slice_in_dim(parts, first_token, own_tokens, 0)
        part = lax.dynamic_slice_in_dim(part, first_group, own, 1)
        return jnp.moveaxis(part, 1, 0).reshape((-1, ROW_TILE) + array.shape[2:])

    tiles = [tiles_of(queries), tiles_of(out_grad)]
    tiles += [tiles_of(self_lse), tiles_of(self_dot)]
    own_pair, tiles = lax.optimization_barrier((pairs[-1], tiles))
    query_tiles, grad_tiles, lse_rows, dot_rows = tiles
    mate_pairs = [swap(pair, "dp", dp_size, 1) for pair in pairs[:-1] + [own_pair]]
    *kept, peak, total, dotted = first_half(
        pairs, query_tiles, grad_tiles, lse_rows, dot_rows, score_scale
    )
    mate, inverse, delta = second_half(
        mate_pairs, query_tiles, grad_tiles, (peak, total, dotted), score_scale
    )
    from_mate = swap(mate, "dp", dp_size, 1)
    mine = finish(kept, query_tiles, grad_tiles, inverse, delta, mate.shape, score_scale)
    by_chip = chip_sum(mine, from_mate)
    *away, home = chips_swap(by_chip, dp_size)
    by_column = column_sum(home, away)
    parts = swap_all(by_column, "cache", columns, 1)
    return adam(parts, cache, first_moment, second_moment)


def solution(mesh):
    in_specs = (
        P("dp", None, None),
        P("dp", None, None),
        P("dp", None),
        P("dp", None),
        P(("dp", "cache"), None, None, None),
        P(("dp", "cache"), None, None, None),
        P(("dp", "cache"), None, None, None),
    )
    out_specs = (
        P(("dp", "cache"), None, None, None),
        P(("dp", "cache"), None, None, None),
        P(("dp", "cache"), None, None, None),
    )
    return jax.shard_map(
        functools.partial(per_device, mesh.shape["dp"], mesh.shape["cache"]),
        mesh=mesh,
        in_specs=in_specs,
        out_specs=out_specs,
        check_vma=False,
    )
```

```python
import functools
import math

import jax
import jax.numpy as jnp
from jax import lax
from jax.experimental import pallas as pl
from jax.experimental.pallas import tpu as pltpu
from jax.sharding import PartitionSpec as P

STEP = 200

learn_rate = 0.02
beta_first = 0.9
beta_second = 0.999
epsilon = 1e-08

ROW_TILE = 256
CHUNK = 16
DOT_ROWS = 256
MIB = 1024 * 1024


def flips(size):
    return list(range(size - 1, -1, -1))


def gather_flips(columns):
    return flips(columns)[1::-1] + flips(columns)[2:]


def pack_kernel(columns, cache_ref, *refs):
    *outs, by_group = refs
    groups = cache_ref.shape[2]
    own = outs[0].shape[1]
    repeat = own * columns // groups
    for side in range(2):
        for group in range(groups):
            by_group[group, side] = cache_ref[:, side, group].astype(jnp.bfloat16)
    column = lax.axis_index("cache")
    for out, flip in zip(outs, gather_flips(columns)):
        first = (column ^ flip) // repeat * own
        for slot in range(own):
            for side in range(2):
                out[side, slot] = by_group[first + slot, side]


def pack(cache, columns, own):
    share, _, groups, width = cache.shape
    slice_shape = jax.ShapeDtypeStruct((2, own, share, width), jnp.bfloat16)
    return pl.pallas_call(
        functools.partial(pack_kernel, columns),
        out_shape=[slice_shape] * columns,
        scratch_shapes=[pltpu.VMEM((groups, 2, share, width), jnp.bfloat16)],
        compiler_params=pltpu.CompilerParams(vmem_limit_bytes=16 * MIB),
        name="pack",
    )(cache)


LOG2E = math.log2(math.e)
ACROSS = (((1,), (1,)), ((), ()))
ALONG = (((1,), (0,)), ((), ()))


def load_pairs(pair_refs, keys, values):
    columns, _, own, share, width = pair_refs[0].shape
    length = columns * share
    for piece, pair_ref in enumerate(pair_refs):
        at = pl.ds(piece * length, length)
        for slot in range(own):
            keys[slot, at] = pair_ref[:, 0, slot].reshape(length, width)
            values[slot, at] = pair_ref[:, 1, slot].reshape(length, width)


def interleave(passes, *products):
    products = [product for some in products for product in some]
    steps = passes[0]
    done = 0
    for number, step in enumerate(passes[1]):
        while done < len(products) and done * steps <= number * len(products):
            products[done]()
            done += 1
    for product in products[done:]:
        product()


def score_products(keys, values, slot, queries_ref, grads_ref, tile, scores, slopes, tops):
    def product(rows, left, right_ref, out):
        def run():
            found = lax.dot_general(
                left[slot], right_ref[tile, rows], ACROSS, preferred_element_type=jnp.float32
            )
            out[:, rows] = found
            if out is scores:
                tops[:, rows] = jnp.max(found.reshape(-1, 8, found.shape[1]), axis=0)

        return run

    products = []
    for start in range(0, scores.shape[1], DOT_ROWS):
        rows = pl.ds(start, DOT_ROWS)
        products.append(product(rows, keys, queries_ref, scores))
        products.append(product(rows, values, grads_ref, slopes))
    return products


def gradient_products(
    key_total, value_total, per_group, weights, dscores, queries_ref, grads_ref, tile
):
    slot = tile // per_group

    def product(total, left, right_ref):
        def run():
            part = lax.dot_general(
                left[...], right_ref[tile], ALONG, preferred_element_type=jnp.float32
            )
            total[slot] = total[slot] + part if tile % per_group else part

        return run

    return [
        product(key_total, dscores, queries_ref),
        product(value_total, weights, grads_ref),
    ]


def cuts_of(ref):
    return [pl.ds(start, CHUNK) for start in range(0, ref.shape[0], CHUNK)]


def exponentiate(scores, slopes, factor, peak, kept, result):
    total = None
    dotted = None
    for cut in cuts_of(scores):
        shifted = jnp.exp2(scores[cut] * factor - peak)
        product = shifted * slopes[cut]
        kept[cut] = shifted
        total = shifted if total is None else total + shifted
        dotted = product if dotted is None else dotted + product
        yield
    result.append(jnp.sum(total, axis=0, keepdims=True))
    result.append(jnp.sum(dotted, axis=0, keepdims=True))


def weigh(kept, slopes, inverse, delta, weights, dscores):
    for cut in cuts_of(weights):
        probability = kept[cut] * inverse
        weights[cut] = probability.astype(jnp.bfloat16)
        dscores[cut] = (probability * (slopes[cut] - delta)).astype(jnp.bfloat16)
        yield


def first_half_kernel(score_scale, per_group, pieces, *refs):
    pair_refs, refs = refs[:pieces][::-1], refs[pieces:]
    queries_ref, grads_ref, lse_ref, dot_ref = refs[:4]
    kept, (peak_ref, total_ref, dotted_ref, keys, values) = refs[4:8], refs[8:13]
    even, odd = refs[13:15], refs[15:17]
    tiles = queries_ref.shape[0]
    factor = score_scale * LOG2E
    load_pairs(pair_refs, keys, values)

    def place(parity, step):
        scores, tops = odd if parity else even
        return scores, kept[2 * parity].at[step], kept[2 * parity + 1].at[step], tops

    def products(tile, parity, step):
        scores, _, slopes, tops = place(parity, step)
        slot = tile // per_group
        return score_products(
            keys, values, slot, queries_ref, grads_ref, tile, scores, slopes, tops
        )

    def normalize(tile, parity, step):
        scores, shifted, slopes, tops = place(parity, step)

        def passes():
            side_lse = lse_ref[pl.ds(tile, 1)] * LOG2E
            peak = jnp.max(tops[...], axis=0, keepdims=True) * factor
            peak = jnp.maximum(peak, side_lse)
            sums = []
            yield from exponentiate(scores, slopes, factor, peak, shifted, sums)
            side = jnp.exp2(side_lse - peak)
            peak_ref[tile] = peak
            total_ref[tile] = sums[0] + side
            dotted_ref[tile] = sums[1] + side * dot_ref[pl.ds(tile, 1)]

        return len(cuts_of(scores)), passes()

    for product in products(0, 0, 0):
        product()

    def two_tiles(step):
        interleave(normalize(2 * step, 0, step), products(2 * step + 1, 1, step))
        interleave(normalize(2 * step + 1, 1, step), products(2 * step + 2, 0, step + 1))

    last = tiles // 2 - 1
    for step in range(last):
        two_tiles(step)
    interleave(normalize(tiles - 2, 0, last), products(tiles - 1, 1, last))
    interleave(normalize(tiles - 1, 1, last))


def first_half(pairs, queries, grads, lse_rows, dot_rows, score_scale):
    columns, _, own, share, width = pairs[0].shape
    positions = len(pairs) * columns * share
    tiles, row_tile, _ = queries.shape
    kept = [jax.ShapeDtypeStruct((tiles // 2, positions, row_tile), jnp.float32)] * 2
    buffers = [
        pltpu.VMEM((positions, row_tile), jnp.float32),
        pltpu.VMEM((8, row_tile), jnp.float32),
    ]
    stat = jax.ShapeDtypeStruct((tiles, 1, row_tile), jnp.float32)
    return pl.pallas_call(
        functools.partial(first_half_kernel, score_scale, tiles // own, len(pairs)),
        out_shape=kept + kept + [stat] * 3,
        scratch_shapes=[
            pltpu.VMEM((own, positions, width), jnp.bfloat16),
            pltpu.VMEM((own, positions, width), jnp.bfloat16),
        ]
        + buffers
        + buffers,
        compiler_params=pltpu.CompilerParams(vmem_limit_bytes=30 * MIB),
        cost_estimate=pl.CostEstimate(
            flops=4 * tiles * row_tile * positions * width,
            bytes_accessed=8 * tiles * row_tile * positions,
            transcendentals=tiles * row_tile * positions,
        ),
        name="first_half",
    )(*pairs[::-1], queries, grads, lse_rows, dot_rows)


def second_half_kernel(score_scale, per_group, pieces, *refs):
    pair_refs, refs = refs[:pieces], refs[pieces:]
    queries_ref, grads_ref, peak_ref, total_ref, dotted_ref = refs[:5]
    out_ref, inverse_ref, delta_ref = refs[5:8]
    keys, values, key_total, value_total = refs[8:12]
    even, odd = refs[12:17], refs[17:22]
    _, columns, _, own, share, width = out_ref.shape
    tiles = queries_ref.shape[0]
    factor = score_scale * LOG2E
    load_pairs(pair_refs, keys, values)

    def products(tile, buffers):
        slot = tile // per_group
        return score_products(keys, values, slot, queries_ref, grads_ref, tile, *buffers[:3])

    def normalize(tile, buffers):
        scores, slopes, tops, weights, dscores = buffers

        def passes():
            first_peak = peak_ref[tile]
            peak = jnp.max(tops[...], axis=0, keepdims=True) * factor
            peak = jnp.maximum(peak, first_peak)
            sums = []
            yield from exponentiate(scores, slopes, factor, peak, scores, sums)
            rescale = jnp.exp2(first_peak - peak)
            inverse = 1.0 / (sums[0] + total_ref[tile] * rescale)
            delta = (sums[1] + dotted_ref[tile] * rescale) * inverse
            inverse_ref[tile] = inverse * rescale
            delta_ref[tile] = delta
            yield from weigh(scores, slopes, inverse, delta, weights, dscores)

        return 2 * len(cuts_of(scores)), passes()

    def gather(tile, buffers):
        return gradient_products(
            key_total,
            value_total,
            per_group,
            *buffers[3:],
            queries_ref,
            grads_ref,
            tile,
        )

    for product in products(0, even):
        product()
    interleave(normalize(0, even), products(1, odd))

    def two_tiles(step):
        tile = step * 2
        interleave(normalize(tile + 1, odd), products(tile + 2, even), gather(tile, even))
        interleave(normalize(tile + 2, even), products(tile + 3, odd), gather(tile + 1, odd))

    for step in range(tiles // 2 - 1):
        two_tiles(step)
    interleave(normalize(tiles - 1, odd), gather(tiles - 2, even))
    for product in gather(tiles - 1, odd):
        product()
    shape = out_ref.shape[:2] + (share, width)
    for slot in range(own):
        key_sum = key_total[slot] * score_scale
        out_ref[:, :, 0, slot] = key_sum.astype(jnp.bfloat16).reshape(shape)
        out_ref[:, :, 1, slot] = value_total[slot].astype(jnp.bfloat16).reshape(shape)


def second_half(pairs, queries, grads, stats, score_scale):
    columns, _, own, share, width = pairs[0].shape
    positions = len(pairs) * columns * share
    tiles, row_tile, _ = queries.shape
    stat = jax.ShapeDtypeStruct((tiles, 1, row_tile), jnp.float32)
    buffers = [
        pltpu.VMEM((positions, row_tile), jnp.float32),
        pltpu.VMEM((positions, row_tile), jnp.float32),
        pltpu.VMEM((8, row_tile), jnp.float32),
        pltpu.VMEM((positions, row_tile), jnp.bfloat16),
        pltpu.VMEM((positions, row_tile), jnp.bfloat16),
    ]
    return pl.pallas_call(
        functools.partial(second_half_kernel, score_scale, tiles // own, len(pairs)),
        out_shape=(
            jax.ShapeDtypeStruct((len(pairs),) + pairs[0].shape, jnp.bfloat16),
            stat,
            stat,
        ),
        scratch_shapes=[
            pltpu.VMEM((own, positions, width), jnp.bfloat16),
            pltpu.VMEM((own, positions, width), jnp.bfloat16),
            pltpu.VMEM((own, positions, width), jnp.float32),
            pltpu.VMEM((own, positions, width), jnp.float32),
        ]
        + buffers
        + buffers,
        compiler_params=pltpu.CompilerParams(vmem_limit_bytes=30 * MIB),
        cost_estimate=pl.CostEstimate(
            flops=8 * tiles * row_tile * positions * width,
            bytes_accessed=4 * tiles * row_tile * width,
            transcendentals=tiles * row_tile * positions,
        ),
        name="second_half",
    )(*pairs, queries, grads, *stats)


def finish_kernel(score_scale, per_group, *refs):
    kept, refs = refs[:4], refs[4:]
    queries_ref, grads_ref, inverse_ref, delta_ref, out_ref = refs[:5]
    key_total, value_total = refs[5:7]
    even, odd = refs[7:9], refs[9:11]
    _, columns, _, own, share, width = out_ref.shape
    tiles = queries_ref.shape[0]

    def spread(tile, parity, step, buffers):
        steps = weigh(
            kept[2 * parity].at[step],
            kept[2 * parity + 1].at[step],
            inverse_ref[tile],
            delta_ref[tile],
            *buffers,
        )
        return len(cuts_of(buffers[0])), steps

    def gather(tile, buffers):
        return gradient_products(
            key_total, value_total, per_group, *buffers, queries_ref, grads_ref, tile
        )

    interleave(spread(0, 0, 0, even))

    def two_tiles(step):
        interleave(spread(2 * step + 1, 1, step, odd), gather(2 * step, even))
        interleave(spread(2 * step + 2, 0, step + 1, even), gather(2 * step + 1, odd))

    last = tiles // 2 - 1
    for step in range(last):
        two_tiles(step)
    interleave(spread(tiles - 1, 1, last, odd), gather(tiles - 2, even))
    for product in gather(tiles - 1, odd):
        product()
    shape = out_ref.shape[:2] + (share, width)
    for slot in range(own):
        out_ref[:, :, 0, slot] = (key_total[slot] * score_scale).reshape(shape)
        out_ref[:, :, 1, slot] = value_total[slot].reshape(shape)


def finish(kept, queries, grads, inverse, delta, shape, score_scale):
    _, positions, row_tile = kept[0].shape
    own, width = shape[3], shape[5]
    tiles = queries.shape[0]
    buffers = [pltpu.VMEM((positions, row_tile), jnp.bfloat16)] * 4
    return pl.pallas_call(
        functools.partial(finish_kernel, score_scale, tiles // own),
        out_shape=jax.ShapeDtypeStruct(shape, jnp.float32),
        scratch_shapes=[
            pltpu.VMEM((own, positions, width), jnp.float32),
            pltpu.VMEM((own, positions, width), jnp.float32),
        ]
        + buffers,
        compiler_params=pltpu.CompilerParams(vmem_limit_bytes=30 * MIB),
        cost_estimate=pl.CostEstimate(
            flops=4 * tiles * row_tile * positions * width,
            bytes_accessed=8 * tiles * row_tile * positions,
            transcendentals=0,
        ),
        name="finish",
    )(*kept, queries, grads, inverse, delta)


def chip_sum_kernel(mine_ref, mate_ref, *outs):
    for offset, out in enumerate(outs):
        out[...] = (mine_ref[offset] + mate_ref[offset].astype(jnp.float32)).astype(out.dtype)


def chip_sum(mine, mate):
    chips = mine.shape[0]
    shape = mine.shape[1:]
    return pl.pallas_call(
        chip_sum_kernel,
        out_shape=[
            jax.ShapeDtypeStruct(shape, jnp.bfloat16 if flip else jnp.float32)
            for flip in flips(chips)
        ],
        compiler_params=pltpu.CompilerParams(vmem_limit_bytes=16 * MIB),
        name="chip_sum",
    )(mine, mate)


def column_sum_kernel(away, mine_ref, *refs):
    others, outs = refs[:away], refs[away:]
    columns = len(outs)
    for out, flip in zip(outs, flips(columns)):
        place = gather_flips(columns).index(flip)
        total = mine_ref[place]
        for other in others:
            total = total + other[place].astype(jnp.float32)
        out[...] = total.astype(out.dtype)


def column_sum(mine, others):
    columns = mine.shape[0]
    shape = mine.shape[1:]
    return pl.pallas_call(
        functools.partial(column_sum_kernel, len(others)),
        out_shape=[
            jax.ShapeDtypeStruct(shape, jnp.bfloat16 if flip else jnp.float32)
            for flip in flips(columns)
        ],
        compiler_params=pltpu.CompilerParams(vmem_limit_bytes=16 * MIB),
        name="column_sum",
    )(mine, *others)


def adam_kernel(columns, *refs):
    parts, refs = refs[:columns], refs[columns:]
    cache_ref, first_ref, second_ref, new_cache, new_first, new_second = refs[:6]
    by_flip, gathered = refs[6:]
    groups = cache_ref.shape[2]
    own = parts[0].shape[1]
    repeat = own * columns // groups
    for part, flip in zip(parts, flips(columns)):
        by_flip[flip] = part[...].astype(jnp.float32)
    column = lax.axis_index("cache")
    for side in range(2):
        for group in range(groups):
            first_owner = group // own * repeat
            slot = group % own
            total = by_flip[column ^ first_owner, side, slot]
            for owner in range(first_owner + 1, first_owner + repeat):
                total = total + by_flip[column ^ owner, side, slot]
            gathered[:, side, group] = total
    gradient = gathered[...]
    first = beta_first * first_ref[...] + (1.0 - beta_first) * gradient
    second = beta_second * second_ref[...] + (1.0 - beta_second) * gradient * gradient
    first_hat = first / (1.0 - beta_first**STEP)
    second_hat = second / (1.0 - beta_second**STEP)
    new_cache[...] = cache_ref[...] - learn_rate * first_hat / (jnp.sqrt(second_hat) + epsilon)
    new_first[...] = first
    new_second[...] = second


def adam(parts, cache, first_moment, second_moment):
    shape = jax.ShapeDtypeStruct(cache.shape, jnp.float32)
    return pl.pallas_call(
        functools.partial(adam_kernel, len(parts)),
        out_shape=(shape, shape, shape),
        scratch_shapes=[
            pltpu.VMEM((len(parts),) + parts[0].shape, jnp.float32),
            pltpu.VMEM(cache.shape, jnp.float32),
        ],
        compiler_params=pltpu.CompilerParams(vmem_limit_bytes=16 * MIB),
        name="adam",
    )(*parts, cache, first_moment, second_moment)


def swap(value, axis, size, flip):
    return lax.ppermute(value, axis, [(place, place ^ flip) for place in range(size)])


def swap_all(values, axis, size, stride, order=flips):
    return [
        swap(value, axis, size, flip * stride) if flip else value
        for value, flip in zip(values, order(len(values)))
    ]


def per_device(
    dp_size, columns, queries, out_grad, self_lse, self_dot, cache, first_moment, second_moment
):
    _, _, groups, width = cache.shape
    tokens, heads, _ = queries.shape
    chips = dp_size // 2
    group_size = heads // groups
    score_scale = 1.0 / math.sqrt(width)
    own = max(1, groups // columns)
    repeat = own * columns // groups
    own_tokens = tokens // repeat
    column = lax.axis_index("cache")
    first_group = column // repeat * own
    first_token = column % repeat * own_tokens

    slices = pack(cache, columns, own)
    gathered = jnp.stack(swap_all(slices, "cache", columns, 1, gather_flips))
    pairs = swap_all([gathered] * chips, "dp", dp_size, 2)
    def tiles_of(array):
        parts = array.reshape((tokens, groups, group_size) + array.shape[2:])
        part = lax.dynamic_slice_in_dim(parts, first_token, own_tokens, 0)
        part = lax.dynamic_slice_in_dim(part, first_group, own, 1)
        return jnp.moveaxis(part, 1, 0).reshape((-1, ROW_TILE) + array.shape[2:])

    tiles = [tiles_of(queries), tiles_of(out_grad)]
    tiles += [tiles_of(self_lse), tiles_of(self_dot)]
    own_pair, tiles = lax.optimization_barrier((pairs[-1], tiles))
    query_tiles, grad_tiles, lse_rows, dot_rows = tiles
    mate_pairs = [swap(pair, "dp", dp_size, 1) for pair in pairs[:-1] + [own_pair]]
    *kept, peak, total, dotted = first_half(
        pairs, query_tiles, grad_tiles, lse_rows, dot_rows, score_scale
    )
    mate, inverse, delta = second_half(
        mate_pairs, query_tiles, grad_tiles, (peak, total, dotted), score_scale
    )
    from_mate = swap(mate, "dp", dp_size, 1)
    mine = finish(kept, query_tiles, grad_tiles, inverse, delta, mate.shape, score_scale)
    by_chip = chip_sum(mine, from_mate)
    *away, home = swap_all(by_chip, "dp", dp_size, 2)
    by_column = column_sum(home, away)
    parts = swap_all(by_column, "cache", columns, 1)
    return adam(parts, cache, first_moment, second_moment)


def solution(mesh):
    in_specs = (
        P("dp", None, None),
        P("dp", None, None),
        P("dp", None),
        P("dp", None),
        P(("dp", "cache"), None, None, None),
        P(("dp", "cache"), None, None, None),
        P(("dp", "cache"), None, None, None),
    )
    out_specs = (
        P(("dp", "cache"), None, None, None),
        P(("dp", "cache"), None, None, None),
        P(("dp", "cache"), None, None, None),
    )
    return jax.shard_map(
        functools.partial(per_device, mesh.shape["dp"], mesh.shape["cache"]),
        mesh=mesh,
        in_specs=in_specs,
        out_specs=out_specs,
        check_vma=False,
    )
```
